32 devices in a mesh: dev: 32 (over z, y, x, core).
Axes of the slice: x: 2, y: 2, z: 4, core: 2. Of those that a mesh axis runs over, the one named last changes fastest.
Arguments:
- layer_input: bfloat16 [2, 3072, 2048], P(None, 'dev'), may hold values from -6 to 6
- output_cotangent: bfloat16 [2, 3072, 2048], P(None, 'dev'), may hold values from -6 to 6
- segment_ids: int32 [2, 3072], P(None, 'dev'), may hold values from 0 to 2, never falling along the last dimension, each value on 1 to 2048 neighbouring positions
- padding_mask: int32 [2, 3072], P(None, 'dev'), may hold values 0 or 1
- bucket_table: int32 [2047], replicated, may hold values from 0 to 31
- attention_norm_gain: bfloat16 [2048], P('dev'), may hold values from 0.099609375 to 1.8984375
- stacked_query_key_value: bfloat16 [2048, 6144], P('dev'), may hold values from -0.0625 to 0.0625
- attention_out: bfloat16 [2048, 2048], P('dev'), may hold values from -1.5 to 1.5
- position_bias: bfloat16 [1024], P('dev'), may hold values from -4 to 4
- feed_gain: bfloat16 [2048], P('dev'), may hold values from 0.099609375 to 1.8984375
- feed_in: bfloat16 [2048, 10240], P('dev'), may hold values from -0.125 to 0.125
- feed_out: bfloat16 [5120, 2048], P('dev'), may hold values from -0.078125 to 0.078125
Outputs:
- layer_output: bfloat16 [2, 3072, 2048], P(None, 'dev')
- input_grad: bfloat16 [2, 3072, 2048], P(None, 'dev')
- grad_attention_gain: float32 [2048], P('dev')
- grad_query_key_value: float32 [2048, 6144], P('dev')
- grad_attention_out: float32 [2048, 2048], P('dev')
- grad_position_bias: float32 [1024], P('dev')
- grad_feed_gain: float32 [2048], P('dev')
- grad_feed_in: float32 [2048, 10240], P('dev')
- grad_feed_out: float32 [5120, 2048], P('dev')
The draws below stay inside these ranges and needn't reach their ends.
Inputs may be any that keep to these rules, and one draw needn't show every extreme that they name: `segment_ids`: segment numbers never fall along a micro-batch; every segment holds 1 to 2048 tokens.
All inputs are finite; a program needn't handle non-finite values. No bound on the sum of `padding_mask` on one device may be relied on, other than what follows from the above.
Results may differ from the reference program's by a relative error of at most 0.015.
The reference program's roundings to bfloat16 on the way count: a program that leaves them out, or rounds other values in their place, can miss the bound.
Values may be sent and summed in bfloat16 or wider, within the bound.
No kernel may reach another device: no remote copies, remote signals or barrier semaphores. Data moves between devices by JAX's collectives and lax.ppermute only.
A program may use at most 368 MiB of HBM per device.

```python
import math
from functools import partial
import jax
import jax.numpy as jnp
import numpy as np
from jax import lax

D = 2048
HEADS = 32
HEAD_DIM = 64
FF = 5120
BUCKETS = 32
WINDOW = 1024
MB = 2
TOKENS = 3072
DOCS = 3
DOC_MOST = 2048


def with_ends(result, key, smallest, largest):
    index_at = [jax.random.randint(jax.random.fold_in(key, axis), (), 0, length) for axis, length in enumerate(result.shape)]
    widest = result.shape.index(max(result.shape))
    beside = index_at[:widest] + [(index_at[widest] + 1) % result.shape[widest]] + index_at[widest + 1:]
    return result.at[tuple(index_at)].set(smallest).at[tuple(beside)].set(largest)


def levels(key, shape, shards, least, top_value):
    def one(axis_at, blocks):
        draws = jax.random.uniform(jax.random.fold_in(jax.random.fold_in(key, 6), axis_at), (blocks,), jnp.float32, least / len(shards), top_value / len(shards))
        return jnp.repeat(jnp.exp(draws), shape[axis_at] // blocks).reshape((-1,) + (1,) * (len(shape) - axis_at - 1))

    level = one(*shards[0])
    for cut in shards[1:]:
        level = level * one(*cut)
    return level


def length_profile(number_of, total, limit, skew):
    loads = [(1 << 20) // math.isqrt(standing ** skew) + 1 for standing in range(2, number_of + 1)]
    spare, holding = total - limit - (number_of - 1), [1] * (number_of - 1)
    while spare > 0:
        movable = [i for i in range(number_of - 1) if holding[i] < limit]
        pool, budget = sum([loads[i] for i in movable]), spare
        for i in movable:
            more = min(limit - holding[i], max(1, budget * loads[i] // pool), spare)
            holding[i] = holding[i] + more
            spare = spare - more
    return np.array([limit] + holding)


def uneven_parts(own_key, number_of, total, reach, lean):
    if number_of == 2:
        one = jax.random.randint(own_key, (), max(1, total - reach), min(reach, total - 1) + 1)
        return jnp.stack([one, total - one])
    sizes = jnp.asarray(length_profile(number_of, total, reach, lean), jnp.int32)
    twos = (number_of - 1) // 2
    giver, taker = sizes[1:1 + 2 * twos:2], sizes[2:2 + 2 * twos:2]
    room = jnp.minimum(giver - 1, reach - taker)
    passed = jax.random.randint(jax.random.fold_in(own_key, 1), (twos,), 0, 1 << 20) % (room + 1)
    sizes = sizes.at[1:1 + 2 * twos:2].set(giver - passed).at[2:2 + 2 * twos:2].set(taker + passed)
    return sizes[jax.random.permutation(jax.random.fold_in(own_key, 2), number_of)]


def bell_draw(stream_key, dims, deviation, reach, shards=(), kind=jnp.bfloat16):
    array = jax.random.normal(stream_key, dims, jnp.float32) * deviation
    if len(shards) > 0:
        array = levels(stream_key, dims, shards, -0.22, 0.18) * array
    return jnp.clip(array, min=-reach, max=reach).astype(kind)


def setup_inputs(seed: int = 0) -> dict:
    arg_keys = jax.random.split(jax.random.key(seed), 13)
    layer_input = bell_draw(arg_keys[0], (MB, TOKENS, D), 1.0, 6.0, ((1, 32),))
    output_cotangent = bell_draw(arg_keys[1], (MB, TOKENS, D), 1.0, 6.0, ((1, 32),))
    segment_ids = jax.vmap(lambda own: jnp.searchsorted(jnp.cumsum(uneven_parts(own, DOCS, TOKENS, DOC_MOST, 1)), jnp.arange(TOKENS), side="right"))(jax.random.split(arg_keys[2], MB)).reshape((MB, TOKENS)).astype(jnp.int32)
    padding_mask = with_ends((jax.random.randint(arg_keys[3], (MB, TOKENS), 0, 8) < 7).astype(jnp.int32), jax.random.fold_in(arg_keys[3], 1), 0, 1)
    bucket_table = with_ends(jax.random.randint(arg_keys[4], (2 * WINDOW - 1,), 0, BUCKETS), jax.random.fold_in(arg_keys[4], 1), 0, BUCKETS - 1).astype(jnp.int32)
    attention_norm_gain = jnp.clip(1.0 + 0.18 * jax.random.normal(arg_keys[5], (D,), jnp.float32), 0.099609375, 1.8984375).astype(jnp.bfloat16)
    stacked_query_key_value = bell_draw(arg_keys[6], (D, 3 * D), (4 * D) ** -0.5, 0.0625, ((0, 32),))
    attention_out = bell_draw(arg_keys[7], (D, D), (max(D // 128, 1)) ** -0.5, 1.5, ((0, 32),))
    position_bias = bell_draw(arg_keys[8], (BUCKETS * HEADS,), 1.0, 4.0, ((0, 32),))
    feed_gain = jnp.clip(1.0 + 0.18 * jax.random.normal(arg_keys[9], (D,), jnp.float32), 0.099609375, 1.8984375).astype(jnp.bfloat16)
    feed_in = bell_draw(arg_keys[10], (D, 2 * FF), D ** -0.5, 0.125, ((0, 32),))
    feed_out = bell_draw(arg_keys[11], (FF, D), FF ** -0.5, 0.078125, ((0, 32),))
    return dict(layer_input=layer_input, output_cotangent=output_cotangent, segment_ids=segment_ids, padding_mask=padding_mask, bucket_table=bucket_table, attention_norm_gain=attention_norm_gain, stacked_query_key_value=stacked_query_key_value, attention_out=attention_out, position_bias=position_bias, feed_gain=feed_gain, feed_in=feed_in, feed_out=feed_out)


EPS = 1e-06
HIGH = lax.Precision.HIGHEST

@jax.custom_vjp
def low(v):
    return lax.optimization_barrier(v.astype(jnp.bfloat16)).astype(jnp.float32)

@jax.custom_vjp
def low_back(v):
    return v

def low_keep(v):
    return (low(v), None)

def low_pass(kept, grad):
    return (grad,)

def back_keep(v):
    return (v, None)

def back_low(kept, grad):
    return (low(grad),)
low.defvjp(low_keep, low_pass)
low_back.defvjp(back_keep, back_low)

def gelu_tanh(value):
    return 0.5 * value * (1.0 + jnp.tanh(0.7978845608028654 * (value + 0.044715 * value * value * value)))

def rms_norm(hidden, gain):
    scale = lax.rsqrt(lax.optimization_barrier(jnp.mean(hidden * hidden, axis=-1, keepdims=True)) + EPS)
    return hidden * scale * gain

def matmul(left, right):
    return jnp.dot(left, right, precision=HIGH, preferred_element_type=jnp.float32)

def attend(queries, keys, values, segments, padding, bias_flat, buckets):
    length = queries.shape[0]
    block = math.gcd(length, 512)
    span = block + 2 * WINDOW
    keys_pad = jnp.pad(keys, ((WINDOW, WINDOW), (0, 0)))
    values_pad = jnp.pad(values, ((WINDOW, WINDOW), (0, 0)))
    seg_pad = jnp.pad(segments, (WINDOW, WINDOW), constant_values=-1)
    mask_pad = jnp.pad(padding, (WINDOW, WINDOW))
    table = bias_flat.reshape(BUCKETS, HEADS)

    def one_block(index):
        start = (index * block).astype(jnp.int32)
        query_blk = lax.dynamic_slice_in_dim(queries, start, block, 0).reshape(block, HEADS, HEAD_DIM)
        key_blk = lax.dynamic_slice_in_dim(keys_pad, start, span, 0).reshape(span, HEADS, HEAD_DIM)
        value_window_block = lax.dynamic_slice_in_dim(values_pad, start, span, 0).reshape(span, HEADS, HEAD_DIM)
        seg_query = lax.dynamic_slice_in_dim(segments, start, block, 0)
        seg_key = lax.dynamic_slice_in_dim(seg_pad, start, span, 0)
        mask_key = lax.dynamic_slice_in_dim(mask_pad, start, span, 0)
        query_pos = start + jnp.arange(block, dtype=jnp.int32)
        key_pos = start - WINDOW + jnp.arange(span, dtype=jnp.int32)
        distance = key_pos[None, :] - query_pos[:, None]
        allowed = (seg_query[:, None] == seg_key[None, :]) & (jnp.abs(distance) < WINDOW) & ((mask_key[None, :] == 1) | (distance == 0))
        offset = jnp.clip(distance + WINDOW - 1, 0, 2 * WINDOW - 2)
        bucket = jnp.take(buckets, offset)
        bias = jnp.take(table, bucket, axis=0).transpose(2, 0, 1)
        logit_scores = jnp.einsum('qhd,khd->hqk', query_blk, key_blk, precision=HIGH) + bias
        logit_scores = low_back(logit_scores)
        logit_scores = jnp.where(allowed[None], logit_scores, -1000000000.0)
        probs = jax.nn.softmax(logit_scores, axis=-1)
        mixed = jnp.einsum('hqk,khd->qhd', low(probs), value_window_block, precision=HIGH)
        return mixed.reshape(block, HEADS * HEAD_DIM)
    blocks = lax.map(jax.checkpoint(one_block), jnp.arange(length // block, dtype=jnp.int32))
    return blocks.reshape(length, HEADS * HEAD_DIM)

def forward(layer_x, gain_attn, project_w, out_w, bias_flat, gain_feed, expand_w, down_w, segment_ids, padding_mask, bucket_table):
    batches, length, width = layer_x.shape
    normed_one = low(rms_norm(layer_x, gain_attn)).reshape(batches * length, width)
    projected = low_back(low(matmul(normed_one, project_w))).reshape(batches, length, 3 * width)
    mixed_list = []
    for batch in range(batches):
        mixed_list.append(attend(projected[batch, :, :width], projected[batch, :, width:2 * width], projected[batch, :, 2 * width:], segment_ids[batch], padding_mask[batch], bias_flat, bucket_table))
    mixed = low_back(low(jnp.stack(mixed_list, axis=0))).reshape(batches * length, width)
    hidden_one = layer_x + low_back(matmul(mixed, out_w)).reshape(layer_x.shape)
    normed_two = low(rms_norm(hidden_one, gain_feed)).reshape(batches * length, width)
    gate_up = low_back(matmul(normed_two, expand_w))
    inner = low(gelu_tanh(gate_up[:, :FF]) * gate_up[:, FF:])
    return hidden_one + low_back(matmul(inner, down_w)).reshape(layer_x.shape)

def reference(layer_input, output_cotangent, segment_ids, padding_mask, bucket_table, attention_norm_gain, stacked_query_key_value, attention_out, position_bias, feed_gain, feed_in, feed_out):
    floats = [arr.astype(jnp.float32) for arr in (layer_input, attention_norm_gain, stacked_query_key_value, attention_out, position_bias, feed_gain, feed_in, feed_out)]
    run = partial(forward, segment_ids=segment_ids, padding_mask=padding_mask, bucket_table=bucket_table)
    final_output, pullback = jax.vjp(run, *floats)
    cotangent = output_cotangent.astype(jnp.float32) * padding_mask.astype(jnp.float32)[..., None]
    grads = pullback(cotangent)
    return (final_output.astype(jnp.bfloat16), grads[0].astype(jnp.bfloat16), grads[1], grads[2], grads[3], grads[4], grads[5], grads[6], grads[7])
```

```python
import jax
import jax.numpy as jnp
from jax import lax
from jax.experimental import pallas as pl
from jax.experimental.pallas import tpu as pltpu
from jax.sharding import Mesh, PartitionSpec as P

EPS = 1e-06
AXES = ("b", "h", "p", "q", "r", "c")
CUBE = ("p", "q", "r")
SWAP = [(0, 1), (1, 0)]
LOW = jnp.bfloat16
F32 = jnp.float32
HEAD_DIM = 64
BUCKETS = 32
WINDOW = 1024
BLK = 256
FAR = float(2**30)
NT = (((1,), (1,)), ((), ()))
NN = (((1,), (0,)), ((), ()))
DIAGS = 2 * (WINDOW // BLK) + 1
MID = WINDOW // BLK


def dot(a, b, dims=NN):
    return lax.dot_general(a, b, dims, preferred_element_type=jnp.float32)


def fill_rows(table, own, other, rows, targets):
    pieces = own.shape[0] // rows
    for side, src in enumerate((own, other)):
        for i in range(pieces):
            at = pl.multiple_of(table[side * pieces + i], rows)
            col = 0
            for dst in targets:
                wide = dst.shape[-1]
                dst[pl.ds(at, rows), :] = src[i * rows : (i + 1) * rows, col : col + wide]
                col += wide


def drain_rows(table, src, own, other, rows, col):
    pieces = own.shape[0] // rows
    wide = src.shape[-1]
    for side, dst in enumerate((own, other)):
        for i in range(pieces):
            at = pl.multiple_of(table[side * pieces + i], rows)
            dst[i * rows : (i + 1) * rows, col : col + wide] = src[pl.ds(at, rows), :]


def make_tiles(diag_ref, tiles):
    for n in range(2):
        for d in range(DIAGS):
            line = diag_ref[n * DIAGS + d : n * DIAGS + d + 1, :]
            wide = jnp.broadcast_to(line, (BLK, 2 * BLK))
            skew = pltpu.roll(wide, 0, 1, stride=1, stride_axis=0)
            tiles[n * (DIAGS + 1) + d] = skew[:, BLK:]


def make_own_tile(pad_ref, tiles, at):
    rows = lax.broadcasted_iota(jnp.int32, (BLK, BLK), 0)
    cols = lax.broadcasted_iota(jnp.int32, (BLK, BLK), 1)
    gone = jnp.where(rows == cols, 0.0, pad_ref[pl.ds(at, BLK), :])
    for n in range(2):
        tiles[n * (DIAGS + 1) + DIAGS] = tiles[n * (DIAGS + 1) + MID] + gone


def build_pairs(q, k, qa_ref, ka_ref, qx, kx):
    def fill_q(i, _):
        rows = pl.ds(pl.multiple_of(i * BLK, BLK), BLK)
        for n in range(2):
            part = q[rows, n * HEAD_DIM : (n + 1) * HEAD_DIM]
            qx[2 * n, rows, :] = jnp.concatenate([part, qa_ref[rows, :HEAD_DIM]], axis=1)
            qx[2 * n + 1, rows, :] = jnp.concatenate([part, qa_ref[rows, HEAD_DIM:]], axis=1)
        return 0

    def fill_k(i, _):
        rows = pl.ds(pl.multiple_of(i * BLK, BLK), BLK)
        for n in range(2):
            part = k[rows, n * HEAD_DIM : (n + 1) * HEAD_DIM]
            kx[n, rows, :] = jnp.concatenate([part, ka_ref[rows, :]], axis=1)
        return 0

    lax.fori_loop(0, q.shape[0] // BLK, fill_q, 0)
    lax.fori_loop(0, k.shape[0] // BLK, fill_k, 0)


def forward_kernel(local, halo, *refs):
    if local:
        (pos, pos_out, rng, own, other, qa, ka, pad, diag, out_own, out_other, mixed_t, lse,
         q, k, v, qx, kx, vt, tiles, joined) = refs
        fill_rows(pos, own, other, own.shape[0] // 48, (q, k, v))
    else:
        (rng, q, k, v, qa, ka, pad, diag, joined, mixed_t, lse, qx, kx, vt, tiles) = refs
    make_tiles(diag, tiles)
    build_pairs(q, k, qa, ka, qx, kx)

    def turn(i, _):
        rows = pl.ds(pl.multiple_of(i * BLK, BLK), BLK)
        vt[:, rows] = v[rows, :].T
        return 0

    lax.fori_loop(0, v.shape[0] // BLK, turn, 0)

    def query_block(i, _):
        at = pl.multiple_of(i * BLK, BLK)
        here = i + halo // BLK
        make_own_tile(pad, tiles, pl.multiple_of(here * BLK, BLK))

        def key_block(j, carry):
            span = pl.ds(pl.multiple_of(j * BLK, BLK), BLK)
            same = (j == here).astype(jnp.int32)
            slot = jnp.where(j == here, DIAGS, j - here + MID)
            out = []
            for n in range(2):
                top, total, acc = carry[n]
                s = dot(kx[n, span, :], qx[2 * n + 1 - same, pl.ds(at, BLK), :], NT)
                s = s + tiles[n * (DIAGS + 1) + slot]
                high = jnp.maximum(top, jnp.max(s, axis=0, keepdims=True))
                p = jnp.exp(s - high)
                shrink = jnp.exp(top - high)
                total = total * shrink + jnp.sum(p, axis=0, keepdims=True)
                acc = acc * shrink + dot(
                    vt[n * HEAD_DIM : (n + 1) * HEAD_DIM, span], p.astype(jnp.bfloat16)
                )
                out.append((high, total, acc))
            return tuple(out)

        start = (
            jnp.full((1, BLK), -1e30, jnp.float32),
            jnp.zeros((1, BLK), jnp.float32),
            jnp.zeros((HEAD_DIM, BLK), jnp.float32),
        )
        done = lax.fori_loop(rng[0, i], rng[1, i], key_block, (start, start))
        for n in range(2):
            top, total, acc = done[n]
            mixed_t[n * HEAD_DIM : (n + 1) * HEAD_DIM, pl.ds(at, BLK)] = acc / total
            lse[n : n + 1, pl.ds(at, BLK)] = top + jnp.log(total)
        joined[pl.ds(at, BLK), :] = mixed_t[:, pl.ds(at, BLK)].T.astype(jnp.bfloat16)
        return 0

    lax.fori_loop(0, q.shape[0] // BLK, query_block, 0)
    if local:
        drain_rows(pos_out, joined, out_own, out_other, out_own.shape[0] // 16, 0)


def backward_kernel(local, halo, *refs):
    if local:
        (pos, pos_out, rng, own, other, qa, ka, pad, diag, g_own, g_other, mixed_t, lse,
         dqkv_own, dqkv_other, d_diag,
         q, k, v, g, dq, dk_low, dv_low, qx, kx, vx, gx, kt, tiles, dk, dv, dtiles) = refs
        fill_rows(pos, own, other, own.shape[0] // 48, (q, k, v))
        fill_rows(pos_out, g_own, g_other, g_own.shape[0] // 16, (g,))
    else:
        (rng, q, k, v, qa, ka, pad, diag, g, mixed_t, lse,
         dq, dk_out, dv_out, d_diag, qx, kx, vx, gx, kt, tiles, dk, dv, dtiles) = refs
    make_tiles(diag, tiles)
    build_pairs(q, k, qa, ka, qx, kx)
    blank = jnp.zeros((BLK, HEAD_DIM), jnp.bfloat16)

    def turn(i, _):
        rows = pl.ds(pl.multiple_of(i * BLK, BLK), BLK)
        kt[:, rows] = k[rows, :].T
        for n in range(2):
            part = v[rows, n * HEAD_DIM : (n + 1) * HEAD_DIM]
            vx[n, rows, :] = jnp.concatenate([part, blank], axis=1)
            dk[n, rows, :] = jnp.zeros((BLK, 2 * HEAD_DIM), jnp.float32)
            dv[n, rows, :] = jnp.zeros((BLK, 2 * HEAD_DIM), jnp.float32)
        return 0

    def spread(i, _):
        rows = pl.ds(pl.multiple_of(i * BLK, BLK), BLK)
        for n in range(2):
            part = g[rows, n * HEAD_DIM : (n + 1) * HEAD_DIM]
            gx[n, rows, :] = jnp.concatenate([part, blank], axis=1)
        return 0

    lax.fori_loop(0, k.shape[0] // BLK, turn, 0)
    lax.fori_loop(0, q.shape[0] // BLK, spread, 0)
    for slot in range(2 * DIAGS):
        dtiles[slot] = jnp.zeros((BLK, BLK), jnp.float32)

    def query_block(i, _):
        at = pl.multiple_of(i * BLK, BLK)
        rows = pl.ds(at, BLK)
        here = i + halo // BLK
        make_own_tile(pad, tiles, pl.multiple_of(here * BLK, BLK))
        turned = g[rows, :].astype(jnp.float32).T * mixed_t[:, rows]
        delta = [
            jnp.sum(turned[n * HEAD_DIM : (n + 1) * HEAD_DIM], axis=0, keepdims=True)
            for n in range(2)
        ]
        level = [lse[n : n + 1, rows] for n in range(2)]

        def key_block(j, carry):
            span = pl.ds(pl.multiple_of(j * BLK, BLK), BLK)
            same = (j == here).astype(jnp.int32)
            away = j - here + MID
            slot = jnp.where(j == here, DIAGS, away)
            out = []
            for n in range(2):
                variant = 2 * n + 1 - same
                s = dot(kx[n, span, :], qx[variant, rows, :], NT)
                p = jnp.exp(s + tiles[n * (DIAGS + 1) + slot] - level[n])
                dp = dot(vx[n, span, :], gx[n, rows, :], NT)
                ds = (p * (dp - delta[n])).astype(jnp.bfloat16)
                dtiles[n * DIAGS + away] += ds.astype(jnp.float32)
                dv[n, span, :] += dot(p.astype(jnp.bfloat16), gx[n, rows, :])
                dk[n, span, :] += dot(ds, qx[variant, rows, :])
                out.append(
                    carry[n] + dot(kt[n * HEAD_DIM : (n + 1) * HEAD_DIM, span], ds)
                )
            return tuple(out)

        zero = jnp.zeros((HEAD_DIM, BLK), jnp.float32)
        done = lax.fori_loop(rng[0, i], rng[1, i], key_block, (zero, zero))
        joined = jnp.concatenate(done, axis=0).T
        dq[rows, :] = joined.astype(dq.dtype)
        return 0

    lax.fori_loop(0, q.shape[0] // BLK, query_block, 0)

    flip = (
        lax.broadcasted_iota(jnp.int32, (BLK, BLK), 0)
        + lax.broadcasted_iota(jnp.int32, (BLK, BLK), 1)
        == BLK - 1
    ).astype(jnp.float32)
    nothing = jnp.zeros((BLK, BLK), jnp.float32)
    for slot in range(2 * DIAGS):
        turned = lax.dot_general(
            flip, dtiles[slot], NN, precision=lax.Precision.HIGHEST,
            preferred_element_type=jnp.float32,
        )
        wide = jnp.concatenate([nothing, turned], axis=1)
        skew = pltpu.roll(wide, BLK + 1, 1, stride=1, stride_axis=0)
        d_diag[slot : slot + 1, :] = jnp.sum(skew, axis=0, keepdims=True)

    def finish(i, _):
        rows = pl.ds(pl.multiple_of(i * BLK, BLK), BLK)
        both_k = jnp.concatenate([dk[n, rows, :HEAD_DIM] for n in range(2)], axis=1)
        both_v = jnp.concatenate([dv[n, rows, :HEAD_DIM] for n in range(2)], axis=1)
        if local:
            dk_low[rows, :] = both_k.astype(jnp.bfloat16)
            dv_low[rows, :] = both_v.astype(jnp.bfloat16)
        else:
            dk_out[rows, :] = both_k
            dv_out[rows, :] = both_v
        return 0

    lax.fori_loop(0, k.shape[0] // BLK, finish, 0)
    if local:
        rows = own.shape[0] // 48
        for col, src in enumerate((dq, dk_low, dv_low)):
            drain_rows(pos, src, dqkv_own, dqkv_other, rows, col * 2 * HEAD_DIM)


def specs(smem, vmem):
    return [pl.BlockSpec(memory_space=pltpu.SMEM)] * smem + [pl.BlockSpec(memory_space=pltpu.VMEM)] * vmem


def common_scratch(length, reach):
    return [
        pltpu.VMEM((4, length, 128), jnp.bfloat16),
        pltpu.VMEM((2, reach, 128), jnp.bfloat16),
    ]


def costs(length, times):
    pairs = 2 * length * 1400
    return pl.CostEstimate(flops=pairs * 256 * times, bytes_accessed=8 << 20, transcendentals=pairs)


def attend_forward(local, halo, tables, tokens, extras):
    length = extras[0].shape[0]
    reach = extras[1].shape[0]
    both = 2 * HEAD_DIM
    shape = jax.ShapeDtypeStruct
    saved = [shape((both, length), jnp.float32), shape((2, length), jnp.float32)]
    tiles = pltpu.VMEM((2 * (DIAGS + 1), BLK, BLK), jnp.float32)
    low = jnp.bfloat16
    if local:
        outs = [shape((length // 2, both), low)] * 2 + saved
        scratch = [pltpu.VMEM((length, both), low)] + [pltpu.VMEM((reach, both), low)] * 2
    else:
        outs = [shape((length, both), low)] + saved
        scratch = []
    scratch += common_scratch(length, reach) + [pltpu.VMEM((both, reach), low), tiles]
    if local:
        scratch += [pltpu.VMEM((length, both), low)]
    return pl.pallas_call(
        lambda *refs: forward_kernel(local, halo, *refs),
        out_shape=outs,
        in_specs=specs(len(tables), len(tokens) + len(extras)),
        out_specs=specs(0, len(outs)),
        scratch_shapes=scratch,
        compiler_params=pltpu.CompilerParams(vmem_limit_bytes=56 << 20),
        cost_estimate=costs(length, 2),
    )(*tables, *tokens, *extras)


def attend_backward(local, halo, tables, tokens, extras, grads, saved):
    length = extras[0].shape[0]
    reach = extras[1].shape[0]
    both = 2 * HEAD_DIM
    shape = jax.ShapeDtypeStruct
    low = jnp.bfloat16
    d_diag = shape((2 * DIAGS, 2 * BLK), jnp.float32)
    if local:
        outs = [shape((length // 2, 3 * both), low)] * 2 + [d_diag]
        scratch = [pltpu.VMEM((length, both), low), pltpu.VMEM((reach, both), low), pltpu.VMEM((reach, both), low),
                   pltpu.VMEM((length, both), low), pltpu.VMEM((length, both), low), pltpu.VMEM((reach, both), low),
                   pltpu.VMEM((reach, both), low)]
    else:
        outs = [shape((length, both), jnp.float32)] + [shape((reach, both), jnp.float32)] * 2 + [d_diag]
        scratch = []
    scratch += common_scratch(length, reach) + [
        pltpu.VMEM((2, reach, both), low),
        pltpu.VMEM((2, length, both), low),
        pltpu.VMEM((both, reach), low),
        pltpu.VMEM((2 * (DIAGS + 1), BLK, BLK), jnp.float32),
        pltpu.VMEM((2, reach, both), jnp.float32),
        pltpu.VMEM((2, reach, both), jnp.float32),
        pltpu.VMEM((2 * DIAGS, BLK, BLK), jnp.float32),
    ]
    return pl.pallas_call(
        lambda *refs: backward_kernel(local, halo, *refs),
        out_shape=outs,
        in_specs=specs(len(tables), len(tokens) + len(extras) + len(grads) + len(saved)),
        out_specs=specs(0, len(outs)),
        scratch_shapes=scratch,
        compiler_params=pltpu.CompilerParams(vmem_limit_bytes=60 << 20),
        cost_estimate=costs(length, 5),
    )(*tables, *tokens, *extras, *grads, *saved)


def skewed_bias(bias):
    edge = jnp.full((2, 2 * BLK), -FAR, jnp.float32)
    wide = jnp.concatenate([edge, bias, edge], axis=1)
    lines = []
    for n in range(2):
        for d in range(DIAGS):
            first = BLK * (d - MID + 1) - (2 * BLK - 1) + WINDOW - 1 + 2 * BLK
            lines.append(wide[n, first : first + 2 * BLK][::-1])
    return jnp.stack(lines)


def unskew(d_diag):
    total = jnp.zeros((2, 2 * WINDOW - 1 + 4 * BLK), jnp.float32)
    for n in range(2):
        for d in range(DIAGS):
            first = BLK * (d - MID + 1) - (2 * BLK - 1) + WINDOW - 1 + 2 * BLK
            total = total.at[n, first : first + 2 * BLK].add(d_diag[n * DIAGS + d][::-1])
    return total[:, 2 * BLK : 2 * BLK + 2 * WINDOW - 1]


def pair_extras(segments, padding, halo, count):
    reach = segments.shape[0]
    length = reach - 2 * halo
    names = jnp.arange(16, dtype=jnp.int32)
    key_hot = segments[:, None] == names
    query_hot = key_hot[halo : halo + length]
    barred = jnp.where(query_hot, 0.0, -FAR).astype(jnp.bfloat16)
    one = jnp.ones((length, 1), jnp.bfloat16)
    rest = jnp.zeros((length, HEAD_DIM - 17), jnp.bfloat16)
    qa = jnp.concatenate([barred, 0 * one, rest, barred, one, rest], axis=1)
    gone = jnp.where(padding == 1, 0.0, -FAR)[:, None]
    ka = jnp.concatenate(
        [key_hot.astype(jnp.bfloat16), gone.astype(jnp.bfloat16), jnp.zeros((reach, HEAD_DIM - 17), jnp.bfloat16)],
        axis=1,
    )

    blocks = length // BLK
    first = halo + BLK * jnp.arange(blocks, dtype=jnp.int32)
    last = first + BLK - 1
    low = jnp.sum(segments[None, :] < segments[first][:, None], axis=1)
    high = jnp.sum(segments[None, :] <= segments[last][:, None], axis=1)
    low = jnp.maximum(low, jnp.maximum(first - WINDOW + 1, 0))
    high = jnp.minimum(high, jnp.minimum(last + WINDOW, reach))
    rng = jnp.stack([low // BLK, (high + BLK - 1) // BLK]).astype(jnp.int32)
    return rng, (qa, ka, gone)


def swap(value, axis):
    return lax.ppermute(value, axis, SWAP)


def pick(value, index, axis=0):
    return lax.dynamic_index_in_dim(value, index, axis, keepdims=False)


def both(mine, theirs, bit, axis, joined=False):
    put = jnp.concatenate if joined else jnp.stack
    return jnp.where(bit == 0, put([mine, theirs], axis), put([theirs, mine], axis))


def matmul(left, right, dims=NN):
    return lax.dot_general(left, right, dims, preferred_element_type=F32)


TN = (((0,), (0,)), ((), ()))


def spread(rows):
    third = rows.shape[0] // 3
    parts = [rows[k * third : (k + 1) * third][None] for k in range(3)]
    for step in range(3):
        got = [swap(parts[k], CUBE[(k + step) % 3]) for k in range(3)]
        parts = [jnp.concatenate([a, b], axis=0) for a, b in zip(parts, got)]
    return jnp.concatenate([part.reshape(-1, rows.shape[1]) for part in parts], axis=0)


def collect(rows):
    width = rows.shape[1]
    parts = list(rows.astype(LOW).reshape(3, 8, -1, width))
    for step in (2, 1, 0):
        half = parts[0].shape[0] // 2
        got = [swap(parts[k][half:], CUBE[(k + step) % 3]) for k in range(3)]
        parts = [(a[:half].astype(F32) + b.astype(F32)).astype(LOW) for a, b in zip(parts, got)]
    return jnp.concatenate([part[0] for part in parts], axis=0).astype(F32)


def exchange(chunks):
    return lax.all_to_all(chunks, CUBE, 0, 0)


def tell_all(line):
    count = lax.axis_size(AXES)
    return lax.all_to_all(jnp.broadcast_to(line, (count,) + line.shape), AXES, 0, 0)


def sum_line(line):
    count = lax.axis_size(AXES)
    return jnp.sum(lax.all_to_all(line.reshape(count, -1), AXES, 0, 0), axis=0)


def over_halves(shard, at):
    if lax.axis_size("b") == 1:
        return both(shard, swap(shard, "h"), at["h"], 0)
    return lax.all_gather(shard, ("b", "h"), axis=0)


def sum_halves(parts, at):
    if lax.axis_size("b") == 1:
        got = swap(pick(parts, 1 - at["h"]).astype(LOW), "h")
        return pick(parts, at["h"]).astype(F32) + got.astype(F32)
    return lax.psum_scatter(parts.astype(F32), ("b", "h"), scatter_dimension=0, tiled=False)


def fetch_columns(chunks, at):
    halves = over_halves(exchange(chunks), at)
    full = both(halves, swap(halves, "c"), at["c"], 2)
    return full.reshape(-1, full.shape[-1])


def return_columns(grad, at, turn=None):
    count = lax.axis_size("b") * 2
    grad = grad.astype(LOW).reshape(count, 8, 2, -1, grad.shape[-1])
    got = swap(pick(grad, 1 - at["c"], 2), "c")
    if turn is not None:
        got = turn(got)
    mine = pick(grad, at["c"], 2).astype(F32) + got.astype(F32)
    return exchange(sum_halves(mine.astype(LOW), at).astype(LOW))


def fetch_out(shard, at):
    if lax.axis_size("b") > 1:
        whole = lax.all_gather(shard, AXES, axis=0, tiled=True)
        width = whole.shape[1]
        return whole.reshape(2, 8, 2, HEAD_DIM, width).transpose(1, 2, 0, 3, 4).reshape(-1, width)
    rows, width = shard.shape
    shard = both(shard, swap(shard, "h"), at["h"], 0)
    cuts = [(0, 640), (640, 1408), (1408, 2048)]
    wholes = []
    for k, (low, high) in enumerate(cuts):
        part = shard[:, :, low:high].reshape(1, 1, 1, 2, rows, high - low)
        for step in range(3):
            axis = (k + step) % 3
            part = both(part, swap(part, CUBE[axis]), at[CUBE[axis]], axis, joined=True)
        part = both(part, swap(part, "c"), at["c"], 3)
        wholes.append(part.reshape(-1, high - low))
    return jnp.concatenate(wholes, axis=1)


def return_out(grad, at):
    width = grad.shape[1]
    if lax.axis_size("b") > 1:
        whole = grad.reshape(8, 2, 2, HEAD_DIM, width).transpose(2, 0, 1, 3, 4).reshape(-1, width)
        return lax.psum_scatter(whole, AXES, scatter_dimension=0, tiled=True)
    grad = grad.astype(LOW).reshape(2, 2, 2, 2, 2, HEAD_DIM, width)
    got = swap(pick(grad, 1 - at["c"], 3), "c")
    grad = (pick(grad, at["c"], 3).astype(F32) + got.astype(F32)).astype(LOW)
    done = []
    for k, (low, high) in enumerate([(0, 640), (640, 1408), (1408, 2048)]):
        part = grad[..., low:high]
        for step in range(3):
            axis = (k + step) % 3
            name = CUBE[axis]
            got = swap(lax.dynamic_index_in_dim(part, 1 - at[name], axis), name)
            mine = lax.dynamic_index_in_dim(part, at[name], axis)
            part = (mine.astype(F32) + got.astype(F32)).astype(LOW)
        part = part.reshape(2, HEAD_DIM, high - low)
        got = swap(pick(part, 1 - at["h"]), "h")
        done.append(pick(part, at["h"]).astype(F32) + got.astype(F32))
    return jnp.concatenate(done, axis=1)


def gelu_tanh(value):
    return (
        0.5
        * value
        * (1.0 + jnp.tanh(0.7978845608028654 * (value + 0.044715 * value * value * value)))
    )


def normalize(hidden):
    scale = lax.rsqrt(jnp.mean(hidden * hidden, axis=-1, keepdims=True) + EPS)
    return (hidden * scale, scale)


def norm_back(grad_unit, unit, scale):
    return scale * (grad_unit - unit * jnp.mean(grad_unit * unit, axis=-1, keepdims=True))


def piece_tables(rows, at):
    third = rows // 3
    spread_at, chunk_at = [], []
    for core in (at["c"], 1 - at["c"]):
        for other in range(2):
            half = at["h"] ^ other
            for k in range(3):
                for i in range(8):
                    mask = 0
                    for step in range(3):
                        if i >> step & 1:
                            mask |= 4 >> (k + step) % 3
                    spread_at.append((16 * half + 2 * (at["cube"] ^ mask) + core) * rows + k * third)
        for place in range(8):
            for other in range(2):
                chunk_at.append((16 * (at["h"] ^ other) + 2 * place + core) * rows)
    return jnp.stack(spread_at).astype(jnp.int32), jnp.stack(chunk_at).astype(jnp.int32)


def in_order(pieces, table):
    count = table.shape[0]
    cut = pieces.reshape(count, -1, pieces.shape[-1])
    return jnp.take(cut, jnp.argsort(table), axis=0).reshape(pieces.shape)


def as_pieces(rows, table):
    count = table.shape[0]
    cut = rows.reshape(count, -1, rows.shape[-1])
    return jnp.take(cut, table // cut.shape[1], axis=0).reshape(rows.shape)


def with_sides(rows, halo):
    count = lax.axis_size("b")
    before = lax.ppermute(rows[-halo:], "b", [(i, i + 1) for i in range(count - 1)])
    after = lax.ppermute(rows[:halo], "b", [(i + 1, i) for i in range(count - 1)])
    return jnp.concatenate([before, rows, after], axis=0)


def add_sides(rows, halo):
    count = lax.axis_size("b")
    after = lax.ppermute(rows[:halo], "b", [(i + 1, i) for i in range(count - 1)])
    before = lax.ppermute(rows[-halo:], "b", [(i, i + 1) for i in range(count - 1)])
    mine = rows[halo:-halo]
    return mine.at[-halo:].add(after).at[:halo].add(before)


def bucket_lines(bucket_table):
    edge = jnp.full((2 * BLK,), -1, jnp.int32)
    wide = jnp.concatenate([edge, bucket_table, edge])[::-1]
    size = wide.shape[0]
    lines = []
    for d in range(DIAGS):
        last = BLK * (d - MID + 1) + WINDOW - 1 + 2 * BLK
        lines.append(wide[size - 1 - last : size - 1 - last + 2 * BLK])
    return jnp.stack(lines)


def local(
    layer_input,
    output_cotangent,
    segment_ids,
    padding_mask,
    bucket_table,
    attention_norm_gain,
    stacked_query_key_value,
    attention_out,
    position_bias,
    feed_gain,
    feed_in,
    feed_out,
):
    at = {name: lax.axis_index(name) for name in AXES}
    at["cube"] = 4 * at["p"] + 2 * at["q"] + at["r"]
    blocks = lax.axis_size("b")
    halves = 2 * blocks
    _, rows, width = layer_input.shape
    shard_rows = stacked_query_key_value.shape[0]
    hidden_shard = feed_out.shape[0]
    hidden_here = hidden_shard * halves * 2
    halo = 0 if blocks == 1 else WINDOW
    length = 32 * rows
    near = at["h"]
    far = 1 - near

    x_near = pick(layer_input, near)
    x_far = swap(pick(layer_input, far), "h")

    code = (segment_ids * 2 + padding_mask).astype(LOW).reshape(-1)
    gains = attention_norm_gain.shape[0]
    line = jnp.concatenate([attention_norm_gain, feed_gain, position_bias, code])
    lines = tell_all(line)
    gain_attn = lines[:, :gains].reshape(-1).astype(F32)
    gain_feed = lines[:, gains : 2 * gains].reshape(-1).astype(F32)
    bias_end = 2 * gains + position_bias.shape[0]
    bias_full = lines[:, 2 * gains : bias_end].reshape(BUCKETS, -1).astype(F32)
    codes = pick(lines[:, bias_end:].astype(jnp.int32).reshape(-1, 2, rows), near, 1).reshape(-1)
    if halo:
        rim = jnp.full((halo,), -2, jnp.int32)
        codes = jnp.concatenate([rim, codes, rim])
        codes = lax.dynamic_slice_in_dim(codes, at["b"] * length, length + 2 * halo)
    segments = jnp.where(codes < 0, -1, codes // 2)
    padding = jnp.where(codes < 0, 0, codes % 2)

    parts = stacked_query_key_value.reshape(shard_rows, 3, 2, 8, 2, HEAD_DIM)
    parts = parts.transpose(3, 0, 4, 1, 2, 5).reshape(8, shard_rows, -1)
    project = fetch_columns(parts, at)
    third = project.shape[1] // 2
    project = jnp.where(
        at["c"] == 0, project, jnp.concatenate([project[:, third:], project[:, :third]], axis=1)
    )
    out_full = fetch_out(attention_out, at)
    parts = feed_in.reshape(shard_rows, 2, halves, 8, 2, hidden_shard)
    parts = parts.transpose(3, 0, 1, 2, 4, 5).reshape(8, shard_rows, -1)
    expand = fetch_columns(parts, at)
    down = over_halves(feed_out, at)
    down = both(down, swap(down, "c"), at["c"], 1).reshape(hidden_here, width)

    gathered = [spread(x_near), spread(x_far)]
    gathered = jnp.concatenate(gathered, axis=0).astype(F32)
    normed_one = (normalize(gathered)[0] * gain_attn).astype(LOW)
    projected = matmul(normed_one, project).astype(LOW)
    own, other = projected[:, :third], swap(projected[:, third:], "c")

    spread_at, chunk_at = piece_tables(rows, at)
    lane = 2 * at["cube"] + at["c"]
    bias_here = pick(bias_full.reshape(BUCKETS, 2, -1), lane, 2)
    chosen = bucket_table[None] == jnp.arange(BUCKETS, dtype=jnp.int32)[:, None]
    bias_line = jnp.sum(jnp.where(chosen[:, None], bias_here[:, :, None], 0.0), axis=0)
    diag = skewed_bias(bias_line)
    rng, extras = pair_extras(segments, padding, halo, None)
    extras = (*extras, diag)
    span = 2 * HEAD_DIM
    if halo == 0:
        tables = (spread_at, chunk_at, rng)
        tokens = (own, other)
        mixed_own, mixed_other, mixed_t, level = attend_forward(True, 0, tables, tokens, extras)
    else:
        tables = (rng,)
        ordered = in_order(jnp.concatenate([own, other], axis=0), spread_at)
        sides = with_sides(ordered[:, span:], halo)
        tokens = (ordered[:, :span], sides[:, :span], sides[:, span:])
        mixed_all, mixed_t, level = attend_forward(False, halo, tables, tokens, extras)
        mixed_all = as_pieces(mixed_all, chunk_at)
        mixed_own, mixed_other = jnp.split(mixed_all, 2, axis=0)
    mixed = both(mixed_own, swap(mixed_other, "c"), at["c"], 1, joined=True)
    mixed = exchange(mixed.reshape(8, 2 * rows, 2 * span))
    mixed = mixed.transpose(1, 0, 2).reshape(2 * rows, -1)
    tokens_here = jnp.concatenate([x_near, x_far], axis=0).astype(F32)
    hidden_one = tokens_here + matmul(mixed, out_full)

    unit_two, scale_two = normalize(hidden_one)
    normed_two = (unit_two * gain_feed).astype(LOW)
    fed = jnp.concatenate([spread(normed_two[:rows]), spread(normed_two[rows:])], axis=0)
    gate_up = matmul(fed, expand)
    gate = gate_up[:, :hidden_here]
    upward = gate_up[:, hidden_here:]
    activated, gelu_pull = jax.vjp(gelu_tanh, gate)
    inner = (activated * upward).astype(LOW)
    final = matmul(inner, down).astype(LOW)
    final_far = hidden_one[rows:] + collect(final[8 * rows :])
    final_far = swap(final_far.astype(LOW), "h")
    final_near = (hidden_one[:rows] + collect(final[: 8 * rows])).astype(LOW)
    layer_output = both(final_near, final_far, near, 0)

    masked = output_cotangent * padding_mask[..., None].astype(LOW)
    res_near = pick(masked, near)
    res_far = swap(pick(masked, far), "h")
    res_all = jnp.concatenate([spread(res_near), spread(res_far)], axis=0)
    grad_res = jnp.concatenate([res_near, res_far], axis=0).astype(F32)
    grad_inner = matmul(res_all, down, NT)
    grad_gate = gelu_pull(grad_inner * upward)[0]
    grad_gate_up = jnp.concatenate([grad_gate, grad_inner * activated], axis=1).astype(LOW)
    grad_fed = matmul(grad_gate_up, expand, NT).astype(LOW)
    grad_normed_two = jnp.concatenate(
        [collect(grad_fed[: 8 * rows]), collect(grad_fed[8 * rows :])], axis=0
    )
    grad_down = matmul(inner, res_all, TN)
    grad_expand = matmul(fed, grad_gate_up, TN)
    grad_feed_gain = sum_line(jnp.sum(grad_normed_two * unit_two, axis=0))
    grad_hidden = grad_res + norm_back(grad_normed_two * gain_feed, unit_two, scale_two)

    grad_hidden_low = grad_hidden.astype(LOW)
    grad_mixed = matmul(grad_hidden_low, out_full, NT).astype(LOW)
    grad_mixed = exchange(grad_mixed.reshape(2 * rows, 8, -1).transpose(1, 0, 2))
    grad_mixed = grad_mixed.reshape(16 * rows, 2, span)
    g_own = pick(grad_mixed, at["c"], 1)
    g_other = swap(pick(grad_mixed, 1 - at["c"], 1), "c")
    grad_out = matmul(mixed, grad_hidden_low, TN)
    if halo == 0:
        d_own, d_other, d_diag = attend_backward(
            True, 0, tables, tokens, extras, (g_own, g_other), (mixed_t, level)
        )
    else:
        g_all = in_order(jnp.concatenate([g_own, g_other], axis=0), chunk_at)
        dq, dk, dv, d_diag = attend_backward(
            False, halo, tables, tokens, extras, (g_all,), (mixed_t, level)
        )
        d_all = jnp.concatenate([dq, add_sides(dk, halo), add_sides(dv, halo)], axis=1)
        d_own, d_other = jnp.split(as_pieces(d_all.astype(LOW), spread_at), 2, axis=0)
    grad_projected = jnp.concatenate([d_own, swap(d_other, "c")], axis=1)
    grad_normed_one = matmul(grad_projected, project, NT).astype(LOW)
    g_far = collect(grad_normed_one[8 * rows :])
    g_near = collect(grad_normed_one[: 8 * rows])
    unit_one, scale_one = normalize(tokens_here)
    grad_gain_rows = 0.0
    results = []
    for part, low in ((g_far, rows), (g_near, 0)):
        cut = slice(low, low + rows)
        grad_gain_rows = grad_gain_rows + jnp.sum(part * unit_one[cut], axis=0)
        whole = grad_hidden[cut] + norm_back(part * gain_attn, unit_one[cut], scale_one[cut])
        results.append(whole.astype(LOW))
    input_grad = both(results[1], swap(results[0], "h"), near, 0)
    grad_attention_gain = sum_line(grad_gain_rows)

    hot = bucket_lines(bucket_table)[None] == jnp.arange(BUCKETS, dtype=jnp.int32)[:, None, None]
    sums = d_diag.reshape(2, DIAGS, 2 * BLK)
    sums = jnp.sum(jnp.where(hot[None], sums[:, None], 0.0), axis=(2, 3)).T
    lanes = (jnp.arange(16, dtype=jnp.int32) == lane).astype(F32)
    grad_position_bias = sum_line((sums[:, :, None] * lanes).reshape(-1))

    grad_project = matmul(normed_one, grad_projected, TN)

    def turn(got):
        return jnp.concatenate([got[..., third:], got[..., :third]], axis=-1)

    grad_project = return_columns(grad_project, at, turn)
    grad_project = jnp.where(at["c"] == 0, grad_project, turn(grad_project))
    grad_project = grad_project.reshape(8, shard_rows, 2, 3, 2, HEAD_DIM)
    grad_project = grad_project.transpose(1, 3, 4, 0, 2, 5).reshape(shard_rows, -1).astype(F32)
    grad_expand = return_columns(grad_expand, at)
    grad_expand = grad_expand.reshape(8, shard_rows, 2, halves, 2, hidden_shard)
    grad_expand = grad_expand.transpose(1, 2, 3, 0, 4, 5).reshape(shard_rows, -1).astype(F32)
    grad_down = grad_down.astype(LOW).reshape(halves, 2, hidden_shard, width)
    got = swap(pick(grad_down, 1 - at["c"], 1), "c")
    grad_down = pick(grad_down, at["c"], 1).astype(F32) + got.astype(F32)
    grad_down = sum_halves(grad_down.astype(LOW), at).astype(F32)
    grad_out = return_out(grad_out, at)
    return (
        layer_output,
        input_grad,
        grad_attention_gain,
        grad_project,
        grad_out,
        grad_position_bias,
        grad_feed_gain,
        grad_expand,
        grad_down,
    )


def solution(mesh):
    wide = Mesh(mesh.devices.reshape(-1, 2, 2, 2, 2, 2), AXES)
    lead, tokens, rows = P(AXES), P(None, AXES), P(AXES, None)
    return jax.shard_map(
        local,
        mesh=wide,
        in_specs=(tokens, tokens, tokens, tokens, P(), lead, rows, rows, lead, lead, rows, rows),
        out_specs=(tokens, tokens, lead, rows, rows, lead, lead, rows, rows),
        check_vma=False,
    )
```

```python
import jax
import jax.numpy as jnp
import numpy as np
from jax import lax
from jax.experimental import pallas as pl
from jax.experimental.pallas import tpu as pltpu
from jax.sharding import Mesh, PartitionSpec as P

EPS = 1e-06
AXES = ("b", "h", "p", "q", "r", "c")
CUBE = ("p", "q", "r")
SWAP = [(0, 1), (1, 0)]
LOW = jnp.bfloat16
F32 = jnp.float32
HEAD_DIM = 64
BUCKETS = 32
WINDOW = 1024
BLK = 256
FAR = float(2**30)
NT = (((1,), (1,)), ((), ()))
NN = (((1,), (0,)), ((), ()))
DIAGS = 2 * (WINDOW // BLK) + 1
MID = WINDOW // BLK
PAD_LANE = 16
LINE = (DIAGS + 1) * BLK
FORWARD_COST = 1
BACKWARD_COST = 1


def dot(a, b, dims=NN):
    return lax.dot_general(a, b, dims, preferred_element_type=jnp.float32)


def fill_rows(table, own, other, rows, targets):
    pieces = own.shape[0] // rows
    for side, src in enumerate((own, other)):
        for i in range(pieces):
            at = pl.multiple_of(table[side * pieces + i], rows)
            col = 0
            for dst in targets:
                wide = dst.shape[-1]
                dst[pl.ds(at, rows), :] = src[i * rows : (i + 1) * rows, col : col + wide]
                col += wide


def drain_rows(table, src, own, other, rows, col):
    pieces = own.shape[0] // rows
    wide = src.shape[-1]
    for side, dst in enumerate((own, other)):
        for i in range(pieces):
            at = pl.multiple_of(table[side * pieces + i], rows)
            dst[i * rows : (i + 1) * rows, col : col + wide] = src[pl.ds(at, rows), :]


def make_tiles(line, tiles):
    strip = jnp.broadcast_to(line[...], (8, LINE))
    strip = pltpu.roll(strip, 0, 1, stride=1, stride_axis=0)
    for g in range(BLK // 8):
        moved = strip if g == 0 else pltpu.roll(strip, 8 * g, 1)
        for d in range(DIAGS):
            first = BLK * (DIAGS - d)
            tiles[d, 8 * g : 8 * g + 8, :] = moved[:, first : first + BLK]
    tiles[DIAGS + 1] = jnp.full((BLK, BLK), -FAR, jnp.float32)


def sum_tiles(tiles, line):
    total = jnp.zeros((8, LINE), jnp.float32)
    edge = jnp.zeros((8, BLK), jnp.float32)
    for g in range(BLK // 8):
        parts = [tiles[d, 8 * g : 8 * g + 8, :] for d in reversed(range(DIAGS))]
        strip = jnp.concatenate([edge] + parts, axis=1)
        total = total + (strip if g == 0 else pltpu.roll(strip, LINE - 8 * g, 1))
    out = total[0:1]
    for r in range(1, 8):
        out = out + pltpu.roll(total[r : r + 1], LINE - r, 1)
    line[...] = out


def make_own_tile(key_more, tiles, at):
    rows = lax.broadcasted_iota(jnp.int32, (BLK, BLK), 0)
    cols = lax.broadcasted_iota(jnp.int32, (BLK, BLK), 1)
    gone = key_more[pl.ds(at, BLK), PAD_LANE : PAD_LANE + 1].astype(jnp.float32)
    tiles[DIAGS] = tiles[MID] + jnp.where(rows == cols, 0.0, gone)


def half_of(n):
    lanes = lax.broadcasted_iota(jnp.int32, (BLK, 2 * HEAD_DIM), 1)
    return (lanes < HEAD_DIM) if n == 0 else (lanes >= HEAD_DIM)


def build_pairs(n, q, k, query_more, key_more, qx, kx):
    here = half_of(n)
    lanes = lax.broadcasted_iota(jnp.int32, (BLK, 2 * HEAD_DIM), 1)
    mark = jnp.where(lanes % HEAD_DIM == PAD_LANE, 1.0, 0.0).astype(jnp.bfloat16)

    def fill_q(i, _):
        rows = pl.ds(pl.multiple_of(i * BLK, BLK), BLK)
        more = query_more[rows, :]
        qx[0, rows, :] = jnp.where(here, q[rows, :], more)
        qx[1, rows, :] = jnp.where(here, q[rows, :], more + mark)
        return 0

    def fill_k(i, _):
        rows = pl.ds(pl.multiple_of(i * BLK, BLK), BLK)
        kx[rows, :] = jnp.where(here, k[rows, :], key_more[rows, :])
        return 0

    lax.fori_loop(0, q.shape[0] // BLK, fill_q, 0)
    lax.fori_loop(0, k.shape[0] // BLK, fill_k, 0)


def pair_of(j, first, end, here):
    out = []
    for m in range(2):
        block = first + 2 * j + m
        there = block < end
        block = jnp.minimum(block, end - 1)
        same = (there & (block == here)).astype(jnp.int32)
        away = block - here + MID
        tile = jnp.where(there, jnp.where(block == here, DIAGS, away), DIAGS + 1)
        out.append((pl.ds(pl.multiple_of(block * BLK, BLK), BLK), same, away, tile))
    return out


def forward_kernel(local, halo, n, *refs):
    if local:
        pos, pos_out, rng, own, other, query_more, key_more, diag, *refs = refs
        before, refs = refs[:n], refs[n:]
        outs, refs = (refs[:2], refs[2:]) if n else ((), refs)
        mixed_t, lse, q, k, v, qx, kx, vt, tiles, *joined = refs
        fill_rows(pos, own, other, own.shape[0] // 48, (q, k, v))
    else:
        rng, q, k, v, query_more, key_more, diag, *refs = refs
        before, refs = refs[:n], refs[n:]
        joined, refs = refs[:n], refs[n:]
        mixed_t, lse, qx, kx, vt, tiles = refs
    make_tiles(diag, tiles)
    build_pairs(n, q, k, query_more, key_more, qx, kx)
    cols = slice(n * HEAD_DIM, (n + 1) * HEAD_DIM)

    def turn(i, _):
        rows = pl.ds(pl.multiple_of(i * BLK, BLK), BLK)
        vt[:, rows] = v[rows, :].T[cols]
        return 0

    lax.fori_loop(0, v.shape[0] // BLK, turn, 0)

    def query_block(i, _):
        at = pl.multiple_of(i * BLK, BLK)
        rows = pl.ds(at, BLK)
        here = i + halo // BLK
        first, end = rng[0, i], rng[1, i]
        make_own_tile(key_more, tiles, pl.multiple_of(here * BLK, BLK))

        def key_blocks(j, carry):
            top, total, acc = carry
            both = pair_of(j, first, end, here)
            s = [
                dot(kx[span, :], qx[1 - same, rows, :], NT) + tiles[tile]
                for span, same, _, tile in both
            ]
            high = jnp.max(jnp.maximum(s[0], s[1]), axis=0, keepdims=True)
            high = jnp.maximum(top, high)
            p = [jnp.exp(part - high) for part in s]
            shrink = jnp.exp(top - high)
            total = total * shrink + jnp.sum(p[0] + p[1], axis=0, keepdims=True)
            acc = acc * shrink
            for part, (span, _, _, _) in zip(p, both):
                acc = acc + dot(vt[:, span], part.astype(jnp.bfloat16))
            return high, total, acc

        start = (
            jnp.full((1, BLK), -1e30, jnp.float32),
            jnp.zeros((1, BLK), jnp.float32),
            jnp.zeros((HEAD_DIM, BLK), jnp.float32),
        )
        top, total, acc = lax.fori_loop(0, (end - first + 1) // 2, key_blocks, start)
        mixed_t[:, rows] = acc / total
        lse[:, rows] = top + jnp.log(total)
        if n:
            whole = jnp.concatenate([before[0][:, rows], mixed_t[:, rows]], axis=0)
            joined[0][rows, :] = whole.T.astype(jnp.bfloat16)
        return 0

    lax.fori_loop(0, q.shape[0] // BLK, query_block, 0)
    if local and n:
        drain_rows(pos_out, joined[0], *outs, outs[0].shape[0] // 16, 0)


def backward_kernel(local, halo, n, *refs):
    if local:
        pos, pos_out, rng, own, other, query_more, key_more, diag, g_own, g_other, mixed_t, lse, *refs = refs
        before, refs = refs[: 3 * n], refs[3 * n :]
        outs, refs = refs[: 3 - n], refs[3 - n :]
        d_diag, q, k, v, g, qx, kx, vx, gx, kt, tiles, dk, dv, dtiles, *whole = refs
        fill_rows(pos, own, other, own.shape[0] // 48, (q, k, v))
        fill_rows(pos_out, g_own, g_other, g_own.shape[0] // 16, (g,))
        dq_out, dk_out, dv_out = whole if n else outs
    else:
        rng, q, k, v, query_more, key_more, diag, g, mixed_t, lse, *refs = refs
        before, refs = refs[: 3 * n], refs[3 * n :]
        dq_out, dk_out, dv_out, d_diag, qx, kx, vx, gx, kt, tiles, dk, dv, dtiles = refs
    make_tiles(diag, tiles)
    build_pairs(n, q, k, query_more, key_more, qx, kx)
    blank = jnp.zeros((BLK, 2 * HEAD_DIM), jnp.bfloat16)
    mine = half_of(n)
    cols = slice(n * HEAD_DIM, (n + 1) * HEAD_DIM)

    def store(out, slot, rows, part):
        part = part.astype(out.dtype)
        out[rows, :] = jnp.where(mine, part, before[slot][rows, :]) if n else part

    def turn(i, _):
        rows = pl.ds(pl.multiple_of(i * BLK, BLK), BLK)
        kt[:, rows] = k[rows, :].T[cols]
        vx[rows, :] = jnp.where(mine, v[rows, :], blank)
        dk[rows, :] = jnp.zeros((BLK, 2 * HEAD_DIM), jnp.float32)
        dv[rows, :] = jnp.zeros((BLK, 2 * HEAD_DIM), jnp.float32)
        return 0

    def spread_g(i, _):
        rows = pl.ds(pl.multiple_of(i * BLK, BLK), BLK)
        gx[rows, :] = jnp.where(mine, g[rows, :], blank)
        return 0

    lax.fori_loop(0, k.shape[0] // BLK, turn, 0)
    lax.fori_loop(0, q.shape[0] // BLK, spread_g, 0)
    for slot in range(DIAGS):
        dtiles[slot] = jnp.zeros((BLK, BLK), jnp.float32)

    def query_block(i, _):
        at = pl.multiple_of(i * BLK, BLK)
        rows = pl.ds(at, BLK)
        here = i + halo // BLK
        first, end = rng[0, i], rng[1, i]
        make_own_tile(key_more, tiles, pl.multiple_of(here * BLK, BLK))
        turned = g[rows, :].astype(jnp.float32).T[cols] * mixed_t[:, rows]
        delta = jnp.sum(turned, axis=0, keepdims=True)
        level = lse[:, rows]

        def key_blocks(j, acc):
            both = pair_of(j, first, end, here)
            s = [
                dot(kx[span, :], qx[1 - same, rows, :], NT) + tiles[tile]
                for span, same, _, tile in both
            ]
            dp = [dot(vx[span, :], gx[rows, :], NT) for span, _, _, _ in both]
            for m, (span, same, away, _) in enumerate(both):
                p = jnp.exp(s[m] - level)
                ds = (p * (dp[m] - delta)).astype(jnp.bfloat16)
                dtiles[away] += ds.astype(jnp.float32)
                dv[span, :] += dot(p.astype(jnp.bfloat16), gx[rows, :])
                dk[span, :] += dot(ds, qx[0, rows, :])
                acc = acc + dot(kt[:, span], ds)
            return acc

        zero = jnp.zeros((HEAD_DIM, BLK), jnp.float32)
        acc = lax.fori_loop(0, (end - first + 1) // 2, key_blocks, zero)
        empty = jnp.zeros((HEAD_DIM, BLK), jnp.float32)
        store(dq_out, 0, rows, jnp.concatenate([empty, acc] if n else [acc, empty], axis=0).T)
        return 0

    lax.fori_loop(0, q.shape[0] // BLK, query_block, 0)

    sum_tiles(dtiles, d_diag)

    def finish(i, _):
        rows = pl.ds(pl.multiple_of(i * BLK, BLK), BLK)
        store(dk_out, 1, rows, dk[rows, :])
        store(dv_out, 2, rows, dv[rows, :])
        return 0

    lax.fori_loop(0, k.shape[0] // BLK, finish, 0)
    if local and n:
        rows = own.shape[0] // 48
        for col, src in enumerate(whole):
            drain_rows(pos, src, *outs, rows, col * 2 * HEAD_DIM)


def specs(smem, vmem):
    return [pl.BlockSpec(memory_space=pltpu.SMEM)] * smem + [pl.BlockSpec(memory_space=pltpu.VMEM)] * vmem


def costs(length, times):
    return pl.CostEstimate(flops=length * times, bytes_accessed=1 << 16, transcendentals=0)


def attend_forward(local, halo, n, tables, tokens, extras, before):
    length, reach = extras[0].shape[0], extras[1].shape[0]
    both = 2 * HEAD_DIM
    shape = jax.ShapeDtypeStruct
    low = jnp.bfloat16
    outs, scratch, last = [], [], []
    if n:
        outs = [shape((length // 2, both), low)] * 2 if local else [shape((length, both), low)]
    outs = outs + [shape((HEAD_DIM, length), jnp.float32), shape((1, length), jnp.float32)]
    if local:
        scratch = [pltpu.VMEM((length, both), low)] + [pltpu.VMEM((reach, both), low)] * 2
        last = [pltpu.VMEM((length, both), low)] * n
    scratch = scratch + [
        pltpu.VMEM((2, length, both), low),
        pltpu.VMEM((reach, both), low),
        pltpu.VMEM((HEAD_DIM, reach), low),
        pltpu.VMEM((DIAGS + 2, BLK, BLK), jnp.float32),
    ]
    return pl.pallas_call(
        lambda *refs: forward_kernel(local, halo, n, *refs),
        out_shape=outs,
        in_specs=specs(len(tables), len(tokens) + len(extras) + len(before)),
        out_specs=specs(0, len(outs)),
        scratch_shapes=scratch + last,
        compiler_params=pltpu.CompilerParams(vmem_limit_bytes=56 << 20),
        cost_estimate=costs(length, FORWARD_COST),
    )(*tables, *tokens, *extras, *before)


def attend_backward(local, halo, n, tables, tokens, extras, grads, saved, before):
    length, reach = extras[0].shape[0], extras[1].shape[0]
    both = 2 * HEAD_DIM
    shape = jax.ShapeDtypeStruct
    low = jnp.bfloat16
    kind = low if local else jnp.float32
    d_diag = shape((1, LINE), jnp.float32)
    scratch, last = [], []
    if local and n:
        outs = [shape((length // 2, 3 * both), low)] * 2 + [d_diag]
    else:
        outs = [shape((length, both), kind)] + [shape((reach, both), kind)] * 2 + [d_diag]
    if local:
        scratch = [pltpu.VMEM((size, both), low) for size in (length, reach, reach, length)]
        last = [pltpu.VMEM((size, both), low) for size in (length, reach, reach)] * n
    scratch = scratch + [
        pltpu.VMEM((2, length, both), low),
        pltpu.VMEM((reach, both), low),
        pltpu.VMEM((reach, both), low),
        pltpu.VMEM((length, both), low),
        pltpu.VMEM((HEAD_DIM, reach), low),
        pltpu.VMEM((DIAGS + 2, BLK, BLK), jnp.float32),
        pltpu.VMEM((reach, both), jnp.float32),
        pltpu.VMEM((reach, both), jnp.float32),
        pltpu.VMEM((DIAGS, BLK, BLK), jnp.float32),
    ]
    operands = (*tokens, *extras, *grads, *saved, *before)
    return pl.pallas_call(
        lambda *refs: backward_kernel(local, halo, n, *refs),
        out_shape=outs,
        in_specs=specs(len(tables), len(operands)),
        out_specs=specs(0, len(outs)),
        scratch_shapes=scratch + last,
        compiler_params=pltpu.CompilerParams(vmem_limit_bytes=60 << 20),
        cost_estimate=costs(length, BACKWARD_COST),
    )(*tables, *operands)


def bucket_line(bucket_table):
    edge = jnp.full((2 * BLK,), -1, jnp.int32)
    wide = jnp.concatenate([edge, bucket_table, edge])[::-1]
    return wide[BLK - 1 : BLK - 1 + LINE]


def query_ranges(segments, halo):
    reach = segments.shape[0]
    first = halo + BLK * jnp.arange((reach - 2 * halo) // BLK, dtype=jnp.int32)
    last = first + BLK - 1
    cut = segments.reshape(-1, BLK)[halo // BLK : (reach - halo) // BLK]
    low = jnp.sum(segments[None, :] < cut[:, :1], axis=1)
    high = jnp.sum(segments[None, :] <= cut[:, -1:], axis=1)
    low = jnp.maximum(low, jnp.maximum(first - WINDOW + 1, 0))
    high = jnp.minimum(high, jnp.minimum(last + WINDOW, reach))
    return jnp.stack([low // BLK, (high + BLK - 1) // BLK]).astype(jnp.int32)


def barring_lanes(codes, halo):
    lanes = jnp.arange(2 * HEAD_DIM, dtype=jnp.int32) % HEAD_DIM
    segments = (codes >> 1)[:, None]
    key_more = jnp.where(lanes == segments, 1.0, 0.0)
    key_more = jnp.where((lanes == PAD_LANE) & ((codes & 1) == 0)[:, None], -FAR, key_more)
    mine = segments[halo : codes.shape[0] - halo]
    query_more = jnp.where((lanes < PAD_LANE) & (lanes != mine), -FAR, 0.0)
    return query_more.astype(jnp.bfloat16), key_more.astype(jnp.bfloat16)


def swap(value, axis):
    return lax.ppermute(value, axis, SWAP)


def pick(value, index, axis=0):
    return lax.dynamic_index_in_dim(value, index, axis, keepdims=False)


def both(mine, theirs, bit, axis, joined=False):
    put = jnp.concatenate if joined else jnp.stack
    return jnp.where(bit == 0, put([mine, theirs], axis), put([theirs, mine], axis))


def matmul(left, right, dims=NN):
    return lax.dot_general(left, right, dims, preferred_element_type=F32)


TN = (((0,), (0,)), ((), ()))


def fence(*values):
    return lax.optimization_barrier(values)


def cut_kernel(order, wide, src, out):
    for m in range(8):
        for j, o in enumerate(order):
            first = (o * 8 + m) * wide
            out[m, :, j * wide : (j + 1) * wide] = src[:, first : first + wide]


def cut_columns(matrix, order, wide):
    rows = matrix.shape[0]
    return pl.pallas_call(
        lambda src, out: cut_kernel(order, wide, src, out),
        out_shape=jax.ShapeDtypeStruct((8, rows, len(order) * wide), matrix.dtype),
        in_specs=specs(0, 1),
        out_specs=specs(0, 1)[0],
        compiler_params=pltpu.CompilerParams(vmem_limit_bytes=32 << 20),
        cost_estimate=pl.CostEstimate(flops=0, bytes_accessed=4 * matrix.size, transcendentals=0),
    )(matrix)


def join_kernel(order, wide, src, out):
    for m in range(8):
        for j, o in enumerate(order):
            first = (o * 8 + m) * wide
            part = src[m, :, j * wide : (j + 1) * wide]
            out[:, first : first + wide] = part.astype(jnp.float32)


def join_columns(chunks, order, wide):
    rows = chunks.shape[1]
    return pl.pallas_call(
        lambda src, out: join_kernel(order, wide, src, out),
        out_shape=jax.ShapeDtypeStruct((rows, len(order) * 8 * wide), F32),
        in_specs=specs(0, 1),
        out_specs=specs(0, 1)[0],
        compiler_params=pltpu.CompilerParams(vmem_limit_bytes=32 << 20),
        cost_estimate=pl.CostEstimate(flops=0, bytes_accessed=6 * chunks.size, transcendentals=0),
    )(chunks)


def distance(k, i):
    mask = 0
    for step in range(3):
        if i >> step & 1:
            mask |= 4 >> (k + step) % 3
    return mask


def join_kernel_rows(counts, *refs):
    total = sum(counts)
    sources, outs, sems = refs[:total], refs[total : total + len(counts)], refs[-1]
    copies = []
    for out, count in zip(outs, counts):
        at = 0
        for src in sources[len(copies) : len(copies) + count]:
            rows = src.shape[0]
            copies.append(pltpu.make_async_copy(src, out.at[pl.ds(at, rows)], sems.at[len(copies)]))
            at += rows
    for copy in copies:
        copy.start()
    for copy in copies:
        copy.wait()


def join_rows(*lists):
    counts = [len(pieces) for pieces in lists]
    pieces = [piece for listed in lists for piece in listed]
    shapes = [
        jax.ShapeDtypeStruct((sum(p.shape[0] for p in listed),) + listed[0].shape[1:], listed[0].dtype)
        for listed in lists
    ]
    outs = pl.pallas_call(
        lambda *refs: join_kernel_rows(counts, *refs),
        out_shape=shapes,
        in_specs=[pl.BlockSpec(memory_space=pl.ANY)] * len(pieces),
        out_specs=specs(0, len(lists)),
        scratch_shapes=[pltpu.SemaphoreType.DMA((len(pieces),))],
        compiler_params=pltpu.CompilerParams(vmem_limit_bytes=32 << 20),
        cost_estimate=pl.CostEstimate(
            flops=0, bytes_accessed=4 * sum(p.size for p in pieces), transcendentals=0
        ),
    )(*pieces)
    return list(outs)


def gather_send(parts, step):
    return [swap(parts[k], CUBE[(k + step) % 3]) for k in range(3)]


def gather_join(parts, wires):
    return join_rows(*([a, b] for a, b in zip(parts, wires)))


def gather_step(parts, step):
    return gather_join(parts, gather_send(parts, step))


def reduce_send(parts):
    half = parts[0].shape[0] // 2
    step = half.bit_length() - 1
    return [swap(parts[k][half:], CUBE[(k + step) % 3]) for k in range(3)]


def reduce_add(parts, wires):
    half = parts[0].shape[0] // 2
    return [(a[:half].astype(F32) + b.astype(F32)).astype(LOW) for a, b in zip(parts, wires)]


def reduce_step(parts, step):
    return reduce_add(parts, reduce_send(parts))


def thirds(rows):
    third = rows.shape[0] // 3
    return [rows[k * third : (k + 1) * third][None] for k in range(3)]


def gathered_rows(parts):
    return join_rows([part.reshape(-1, part.shape[-1]) for part in parts])[0]


def to_parts(rows):
    return list(rows.reshape(3, 8, -1, rows.shape[-1]))


def own_rows(parts):
    return jnp.concatenate([part[0] for part in parts], axis=0).astype(F32)


def exchange(chunks):
    return lax.all_to_all(chunks, CUBE, 0, 0)


def move_kernel(gather, rows, table, src, out):
    for n in range(src.shape[0] // rows):
        fixed = pl.ds(n * rows, rows)
        moved = pl.ds(pl.multiple_of(table[n], rows), rows)
        if gather:
            out[fixed, :] = src[moved, :]
        else:
            out[moved, :] = src[fixed, :]


def move_rows(table, src, gather):
    rows = src.shape[0] // table.shape[0]
    return pl.pallas_call(
        lambda *refs: move_kernel(gather, rows, *refs),
        out_shape=jax.ShapeDtypeStruct(src.shape, src.dtype),
        in_specs=specs(1, 1),
        out_specs=specs(0, 1)[0],
        compiler_params=pltpu.CompilerParams(vmem_limit_bytes=32 << 20),
        cost_estimate=pl.CostEstimate(flops=0, bytes_accessed=4 * src.size, transcendentals=0),
    )(table, src)


def tell_all(line):
    count = lax.axis_size(AXES)
    return lax.all_to_all(jnp.broadcast_to(line, (count,) + line.shape), AXES, 0, 0)


def sum_line(line):
    count = lax.axis_size(AXES)
    return jnp.sum(lax.all_to_all(line.reshape(count, -1), AXES, 0, 0), axis=0)


def wire_halves(shard):
    if lax.axis_size("b") == 1:
        return swap(shard, "h")
    return lax.all_gather(shard, ("b", "h"), axis=0)


def wire_halves_twice(shard):
    if lax.axis_size("b") == 1:
        return swap(shard[:4], "h"), swap(shard[4:], "h")
    return (wire_halves(shard),)


def light_distance(part, i):
    return (i & 1) * 4 | (i >> 1 & 1) * (2, 1)[part] | (i >> 2 & 1) * (1, 2)[part]


def light_send(parts):
    half = parts[0].shape[0] // 2
    axes = {4: ("r", "q"), 2: ("q", "r"), 1: ("p", "p")}[half]
    return [swap(part[half:], axis) for part, axis in zip(parts, axes)]


def by_rows_kernel(src, out):
    count = src.shape[0] // 48
    for part in range(2):
        for i in range(8):
            mask = light_distance(part, i)
            for j in range(3):
                row = 3 * part + j
                k = row // 2
                place = [distance(k, e) for e in range(8)].index(mask)
                first = ((k * 8 + place) * 2 + row % 2) * count
                at = ((part * 8 + i) * 3 + j) * count
                out[at : at + count, :] = src[first : first + count, :]


def by_rows_of_light(rows):
    return pl.pallas_call(
        by_rows_kernel,
        out_shape=jax.ShapeDtypeStruct(rows.shape, rows.dtype),
        in_specs=specs(0, 1),
        out_specs=specs(0, 1)[0],
        compiler_params=pltpu.CompilerParams(vmem_limit_bytes=32 << 20),
        cost_estimate=pl.CostEstimate(flops=0, bytes_accessed=1 << 16, transcendentals=0),
    )(rows)


def by_light_kernel(table, src, out):
    rows, wide = src.shape[0] // 8, src.shape[1] // 2
    for part in range(2):
        for i in range(8):
            at = pl.ds(pl.multiple_of((table[0] ^ light_distance(part, i)) * rows, rows), rows)
            to = (part * 8 + i) * wide
            out[:, to : to + wide] = src[at, part * wide : (part + 1) * wide]


def by_light_distance(chunks, at):
    tall, wide = chunks.shape
    return pl.pallas_call(
        by_light_kernel,
        out_shape=jax.ShapeDtypeStruct((tall // 8, wide * 8), chunks.dtype),
        in_specs=specs(1, 1),
        out_specs=specs(0, 1)[0],
        compiler_params=pltpu.CompilerParams(vmem_limit_bytes=32 << 20),
        cost_estimate=pl.CostEstimate(flops=0, bytes_accessed=1 << 16, transcendentals=0),
    )(at["cube"][None].astype(jnp.int32), chunks)


def gather_halves(shard):
    return lax.all_gather(shard, ("b", "h"), axis=0)


def scatter_halves(parts):
    return lax.psum_scatter(parts, ("b", "h"), scatter_dimension=0, tiled=False)


def weave_halves(halves, core, at):
    if lax.axis_size("b") > 1:
        return both(halves, core, at["c"], 2)
    count = halves.shape[1]
    halves, core = (v.reshape((-1,) + v.shape[2:]) for v in (halves, core))
    return weave([(halves, None, 0), (core, None, 1)], at, count, True)


def join_halves(shard, wire, at):
    return both(shard, wire, at["h"], 0) if lax.axis_size("b") == 1 else wire


def send_halves(parts, at):
    if lax.axis_size("b") == 1:
        return swap(pick(parts, 1 - at["h"]), "h")
    return lax.psum_scatter(parts.astype(F32), ("b", "h"), scatter_dimension=0, tiled=False)


def add_halves(parts, wire, at):
    if lax.axis_size("b") == 1:
        return pick(parts, at["h"]).astype(F32) + wire.astype(F32)
    return wire


def add_cores(grad, wire, at, axis):
    return (pick(grad, at["c"], axis).astype(F32) + wire.astype(F32)).astype(LOW)


def send_cores(grad, at, axis):
    return swap(pick(grad, 1 - at["c"], axis), "c")


def fetch_out_wide(shard):
    whole = lax.all_gather(shard, AXES, axis=0, tiled=True)
    whole = whole.reshape(2, 8, 2, HEAD_DIM, -1).transpose(1, 0, 2, 3, 4)
    return whole.reshape(-1, whole.shape[-1])


def grad_out_wide(grad):
    grad = grad.reshape(8, 2, 2, HEAD_DIM, -1).transpose(1, 0, 2, 3, 4)
    return lax.psum_scatter(grad.reshape(-1, grad.shape[-1]), AXES, scatter_dimension=0, tiled=True)


def gelu_tanh(value):
    return (
        0.5
        * value
        * (1.0 + jnp.tanh(0.7978845608028654 * (value + 0.044715 * value * value * value)))
    )


def normalize(hidden):
    scale = lax.rsqrt(jnp.mean(hidden * hidden, axis=-1, keepdims=True) + EPS)
    return (hidden * scale, scale)


def norm_back(grad_unit, unit, scale):
    return scale * (grad_unit - unit * jnp.mean(grad_unit * unit, axis=-1, keepdims=True))


def piece_tables(rows, at):
    both_rows = 2 * rows
    third = both_rows // 3
    side, k, i, half = np.meshgrid(range(2), range(3), range(8), range(2), indexing="ij")
    mask = np.vectorize(distance)(k, i)
    row = k * third + half * (third // 2)
    other, row = row // rows, row % rows
    side, other, row, mask = (jnp.asarray(v.reshape(-1), jnp.int32) for v in (side, other, row, mask))
    spread_at = (16 * (at["h"] ^ other) + 2 * (at["cube"] ^ mask) + (at["c"] ^ side)) * rows + row
    side, place, other = np.meshgrid(range(2), range(8), range(2), indexing="ij")
    side, place, other = (jnp.asarray(v.reshape(-1), jnp.int32) for v in (side, place, other))
    chunk_at = (16 * (at["h"] ^ other) + 2 * place + (at["c"] ^ side)) * rows
    k, i = np.meshgrid(range(3), range(8), indexing="ij")
    mask = jnp.asarray(np.vectorize(distance)(k, i).reshape(-1), jnp.int32)
    cube_at = (at["cube"] ^ mask) * both_rows + jnp.asarray(k.reshape(-1) * third, jnp.int32)
    return spread_at, chunk_at, cube_at


def weave_kernel(kinds, by_half, turn, *refs):
    place, sources, out, sems = refs[0], refs[1:-2], refs[-2], refs[-1]
    copies = []
    for src, (half_off, core_off) in zip(sources, kinds):
        core = place[1] ^ core_off
        count = out.shape[1]
        for part in range(src.shape[0] // count):
            half = part
            if by_half and half_off is not None:
                half = place[0] ^ part
            rows_part = src.at[part * count : (part + 1) * count]
            for j in range(2 if turn else 1):
                dst, src_part = out.at[half, :, core], rows_part
                if turn:
                    first = pl.multiple_of((j ^ place[1]) * turn, turn)
                    dst = out.at[half, :, core, :, pl.ds(first, turn)]
                    src_part = rows_part.at[:, :, j * turn : (j + 1) * turn]
                copies.append(pltpu.make_async_copy(src_part, dst, sems.at[len(copies)]))
    for copy in copies:
        copy.start()
    for copy in copies:
        copy.wait()


def weave(pieces, at, count, by_half, turn=0):
    rows, wide = pieces[0][0].shape[1:]
    place = jnp.stack([at["h"], at["c"]]).astype(jnp.int32)
    kinds = [piece[1:] for piece in pieces]
    arrays = [piece[0] for piece in pieces]
    return pl.pallas_call(
        lambda *refs: weave_kernel(kinds, by_half, turn, *refs),
        out_shape=jax.ShapeDtypeStruct((2 if by_half else 1, count, 2, rows, wide), arrays[0].dtype),
        in_specs=specs(1, 0) + [pl.BlockSpec(memory_space=pl.ANY)] * len(arrays),
        out_specs=specs(0, 1)[0],
        scratch_shapes=[pltpu.SemaphoreType.DMA((4 * len(arrays),))],
        compiler_params=pltpu.CompilerParams(vmem_limit_bytes=32 << 20),
        cost_estimate=pl.CostEstimate(flops=0, bytes_accessed=1 << 16, transcendentals=0),
    )(place, *arrays)


def small_line(segment_ids, padding_mask, attention_norm_gain, feed_gain, position_bias):
    codes = (segment_ids * 2 + padding_mask).astype(LOW)
    fields = [codes[0], codes[1], attention_norm_gain, feed_gain, position_bias]
    return jnp.concatenate([jnp.pad(field, (0, 128 - field.shape[0])) for field in fields])


def prepare_kernel(rows, place, lines, buckets, gains, query_more, key_more, diag, rng):
    count = lines.shape[0]
    fields = [lines[:, 128 * i : 128 * (i + 1)].astype(jnp.float32) for i in range(5)]
    codes = jnp.where(place[0] == 0, fields[0], fields[1])
    turned = codes.T
    lanes = lax.broadcasted_iota(jnp.int32, (rows, 2 * HEAD_DIM), 1) % HEAD_DIM
    for dev in range(count):
        code = turned[:rows, dev : dev + 1].astype(jnp.int32)
        segment = code >> 1
        key = jnp.where(lanes == segment, 1.0, 0.0)
        key = jnp.where((lanes == PAD_LANE) & ((code & 1) == 0), -FAR, key)
        query = jnp.where((lanes < PAD_LANE) & (lanes != segment), -FAR, 0.0)
        key_more[dev * rows : (dev + 1) * rows, :] = key.astype(key_more.dtype)
        query_more[dev * rows : (dev + 1) * rows, :] = query.astype(query_more.dtype)
        wide = gains.shape[1] // count
        for i in range(2):
            gains[i : i + 1, dev * wide : (dev + 1) * wide] = fields[2 + i][dev : dev + 1, :wide]
    heads = lax.broadcasted_iota(jnp.int32, fields[4].shape, 1)
    line = buckets[...]
    hot = lax.broadcasted_iota(jnp.int32, (BUCKETS, line.shape[1]), 0) == line
    for n in range(2):
        bias = jnp.sum(jnp.where(heads == 2 * place[1] + n, fields[4], 0.0), axis=1, keepdims=True)
        chosen = jnp.sum(jnp.where(hot, bias, 0.0), axis=0, keepdims=True)
        diag[n : n + 1, :] = jnp.where(line < 0, -FAR, chosen)
    real = lax.broadcasted_iota(jnp.int32, codes.shape, 1) < rows
    segments = codes.astype(jnp.int32) >> 1
    total = count * rows
    starts = [jnp.sum(jnp.where(real & (segments < s), 1.0, 0.0)).astype(jnp.int32) for s in range(1, PAD_LANE)]
    for i in range(total // BLK):
        first, last = i * BLK, i * BLK + BLK - 1
        low, high = jnp.int32(max(first - WINDOW + 1, 0)), jnp.int32(min(last + WINDOW, total))
        for start in starts:
            low = jnp.where(start <= first, jnp.maximum(low, start), low)
            high = jnp.where(start > last, jnp.minimum(high, start), high)
        rng[0, i] = low // BLK
        rng[1, i] = (high + BLK - 1) // BLK


def prepare(lines, buckets, near, lane, rows):
    count = lines.shape[0]
    place = jnp.stack([near, lane]).astype(jnp.int32)
    shape = jax.ShapeDtypeStruct
    total = count * rows
    gains, query_more, key_more, diag, rng = pl.pallas_call(
        lambda *refs: prepare_kernel(rows, *refs),
        out_shape=[
            shape((2, count * HEAD_DIM), F32),
            shape((total, 2 * HEAD_DIM), LOW),
            shape((total, 2 * HEAD_DIM), LOW),
            shape((2, LINE), F32),
            shape((2, total // BLK), jnp.int32),
        ],
        in_specs=specs(1, 2),
        out_specs=specs(0, 4) + specs(1, 0),
        compiler_params=pltpu.CompilerParams(vmem_limit_bytes=32 << 20),
        cost_estimate=pl.CostEstimate(flops=0, bytes_accessed=1 << 16, transcendentals=0),
    )(place, lines, buckets[None])
    return gains, (query_more, key_more), diag, rng


def prepare_wide(lines, buckets, near, lane, rows, halo, at):
    count = lines.shape[0]
    shard = 32 * HEAD_DIM // count
    gain_attn = lines[:, 256 : 256 + shard].reshape(-1).astype(F32)
    gain_feed = lines[:, 384 : 384 + shard].reshape(-1).astype(F32)
    bias_full = lines[:, 512 : 512 + BUCKETS * 32 // count].reshape(BUCKETS, -1).astype(F32)
    codes = pick(jnp.stack([lines[:, :rows], lines[:, 128 : 128 + rows]]).astype(jnp.int32), near)
    rim = jnp.full((halo,), -2, jnp.int32)
    codes = jnp.concatenate([rim, codes.reshape(-1), rim])
    length = 32 * rows
    codes = lax.dynamic_slice_in_dim(codes, at["b"] * length, length + 2 * halo)
    bias_here = pick(bias_full.reshape(BUCKETS, -1, 2), lane, 1)
    hot = buckets[None] == jnp.arange(BUCKETS, dtype=jnp.int32)[:, None]
    diag = jnp.sum(jnp.where(hot[:, None], bias_here[:, :, None], 0.0), axis=0)
    diag = jnp.where(buckets < 0, -FAR, diag)
    return gain_attn, gain_feed, barring_lanes(codes, halo), diag, query_ranges(codes >> 1, halo)


def in_order(pieces, table):
    count = table.shape[0]
    cut = pieces.reshape(count, -1, pieces.shape[-1])
    return jnp.take(cut, jnp.argsort(table), axis=0).reshape(pieces.shape)


def as_pieces(rows, table):
    count = table.shape[0]
    cut = rows.reshape(count, -1, rows.shape[-1])
    return jnp.take(cut, table // cut.shape[1], axis=0).reshape(rows.shape)


def with_sides(rows, halo):
    count = lax.axis_size("b")
    before = lax.ppermute(rows[-halo:], "b", [(i, i + 1) for i in range(count - 1)])
    after_it = lax.ppermute(rows[:halo], "b", [(i + 1, i) for i in range(count - 1)])
    return jnp.concatenate([before, rows, after_it], axis=0)


def add_sides(rows, halo):
    count = lax.axis_size("b")
    after_it = lax.ppermute(rows[:halo], "b", [(i + 1, i) for i in range(count - 1)])
    before = lax.ppermute(rows[-halo:], "b", [(i, i + 1) for i in range(count - 1)])
    mine = rows[halo:-halo]
    return mine.at[-halo:].add(after_it).at[:halo].add(before)


def local(
    layer_input,
    output_cotangent,
    segment_ids,
    padding_mask,
    bucket_table,
    attention_norm_gain,
    stacked_query_key_value,
    attention_out,
    position_bias,
    feed_gain,
    feed_in,
    feed_out,
):
    at = {name: lax.axis_index(name) for name in AXES}
    at["cube"] = 4 * at["p"] + 2 * at["q"] + at["r"]
    blocks = lax.axis_size("b")
    halves = 2 * blocks
    one_block = blocks == 1
    _, rows, width = layer_input.shape
    shard_rows = stacked_query_key_value.shape[0]
    hidden_shard = feed_out.shape[0]
    hidden_here = hidden_shard * halves * 2
    halo = 0 if one_block else WINDOW
    length = 32 * rows
    near = at["h"]
    far = 1 - near
    span = 2 * HEAD_DIM
    side = 3 * span
    lane = 8 * at["c"] + at["cube"]
    expand_order = tuple(range(2 * halves))
    project_order = (0, 2, 4, 1, 3, 5)

    lines = tell_all(small_line(segment_ids, padding_mask, attention_norm_gain, feed_gain, position_bias))
    x_near = pick(layer_input, near)
    x_far = swap(pick(layer_input, far), "h")
    cut = cut_columns(stacked_query_key_value, project_order, span)
    cut_in = cut_columns(feed_in, expand_order, 2 * hidden_shard)
    masked = output_cotangent * padding_mask[..., None].astype(LOW)
    x_far, lines, cut, cut_in, masked, attention_out, feed_out = fence(
        x_far, lines, cut, cut_in, masked, attention_out, feed_out
    )

    cut = exchange(cut)
    x_here = jnp.concatenate([x_near, x_far], axis=0)
    x_parts = gather_step(thirds(x_here), 0)
    buckets = bucket_line(bucket_table)
    spread_at, chunk_at, cube_at = piece_tables(rows, at)
    out_wire = swap(attention_out, "h") if one_block else ()
    x_parts, cut, buckets, spread_at, chunk_at, cube_at, masked, out_wire = fence(
        x_parts, cut, buckets, spread_at, chunk_at, cube_at, masked, out_wire
    )
    project_wire = wire_halves(cut)
    x_parts = gather_step(x_parts, 1)
    x_parts, project_wire, masked, feed_out = fence(x_parts, project_wire, masked, feed_out)
    x_parts = gather_step(x_parts, 2)
    res_far = swap(pick(masked, far), "h")
    if one_block:
        gains_both, barring, diag, rng = prepare(lines, buckets, near, lane, rows)
        gain_attn, gain_feed = gains_both[0], gains_both[1]
        project_pair = join_rows([cut, project_wire])[0]
    else:
        gain_attn, gain_feed, barring, diag, rng = prepare_wide(lines, buckets, near, lane, rows, halo, at)
        project_pair = project_wire.reshape(-1, shard_rows, 2 * side)
    if one_block:
        out_halves = both(attention_out, out_wire, at["h"], 0)
        out_halves = jnp.broadcast_to(out_halves, (8,) + out_halves.shape)
    else:
        out_halves = ()
    x_parts, gain_attn, gain_feed, barring, diag, rng, cut_in, project_pair, out_halves, res_far = fence(
        x_parts, gain_attn, gain_feed, barring, diag, rng, cut_in, project_pair, out_halves, res_far
    )

    project_core = swap(project_pair, "c")
    cut_in = exchange(cut_in)
    gathered = gathered_rows(x_parts)
    gathered, project_core = fence(gathered, project_core)
    gathered_unit, gathered_scale = normalize(gathered.astype(F32))
    normed_one = (gathered_unit * gain_attn).astype(LOW)
    if one_block:
        pieces = [(project_pair, 0, 0), (project_core, 0, 1)]
        project = weave(pieces, at, 8, True, side).reshape(width, -1)
    else:
        shape = (-1, 8, shard_rows, 2 * side)
        project = both(project_pair.reshape(shape), project_core.reshape(shape), at["c"], 2).reshape(width, -1)
        project = jnp.where(
            at["c"] == 0, project, jnp.concatenate([project[:, side:], project[:, :side]], axis=1)
        )
    projected = matmul(normed_one, project).astype(LOW)
    projected, cut_in, masked, out_halves = fence(projected, cut_in, masked, out_halves)
    out_chunks = exchange(out_halves) if one_block else ()
    own, other = projected[:, :side], swap(projected[:, side:], "c")
    res = jnp.concatenate([pick(masked, near), res_far], axis=0)
    res_parts = thirds(res)
    res_wires = gather_send(res_parts, 0)
    own, other = fence(own, other)

    expand_halves = gather_halves(cut_in)
    if one_block:
        tables = (spread_at, chunk_at, rng)
        tokens = (own, other)
    else:
        tables = (rng,)
        ordered = in_order(jnp.concatenate([own, other], axis=0), spread_at)
        sides = with_sides(ordered[:, span:], halo)
        tokens = (ordered[:, :span], sides[:, :span], sides[:, span:])
    extras = [(*barring, diag[n : n + 1]) for n in range(2)]
    first = attend_forward(one_block, halo, 0, tables, tokens, extras[0], ())
    *mixed, mixed_t, level = attend_forward(one_block, halo, 1, tables, tokens, extras[1], first[:1])
    saved = (first, (mixed_t, level))
    if not one_block:
        mixed = jnp.split(as_pieces(mixed[0], chunk_at), 2, axis=0)
    mixed, mixed_other, out_chunks, feed_out, res_wires, expand_halves = fence(
        *mixed, out_chunks, feed_out, res_wires, expand_halves
    )
    down_halves = gather_halves(feed_out)
    mixed_wire = swap(mixed_other, "c")
    out_wire = swap(out_chunks, "c") if one_block else ()
    res_parts = gather_join(res_parts, res_wires)
    mixed, mixed_wire, res_parts, out_wire = fence(mixed, mixed_wire, res_parts, out_wire)
    mixed = both(mixed, mixed_wire, at["c"], 1, joined=True)
    mixed = exchange(mixed.reshape(8, 2 * rows, 2 * span))
    expand_core = swap(expand_halves, "c")
    if one_block:
        pieces = [(out_chunks.reshape(16, HEAD_DIM, width), 0, 0), (out_wire.reshape(16, HEAD_DIM, width), 0, 1)]
        out_full = weave(pieces, at, 16, False).reshape(-1, width)
    else:
        out_full = fetch_out_wide(attention_out)
    mixed, out_full, expand_core = fence(mixed, out_full, expand_core)
    mixed_chunks = mixed.reshape(16 * rows, 2 * span)
    res_wires = gather_send(res_parts, 1)
    mixed = mixed.transpose(1, 0, 2).reshape(2 * rows, -1)
    tokens_here = x_here.astype(F32)
    hidden_one = tokens_here + matmul(mixed, out_full)

    unit_two, scale_two = normalize(hidden_one)
    normed_two = (unit_two * gain_feed).astype(LOW)
    normed_two, mixed = fence(normed_two, mixed)
    parts = gather_step(thirds(normed_two), 0)
    expand = weave_halves(expand_halves, expand_core, at).reshape(width, -1)
    parts, expand, res_wires, down_halves = fence(parts, expand, res_wires, down_halves)
    res_parts = gather_join(res_parts, res_wires)
    down_core = swap(down_halves, "c")
    parts = gather_step(parts, 1)
    (parts,) = fence(parts)
    parts = gather_step(parts, 2)
    res_wires = gather_send(res_parts, 2)
    down = weave_halves(down_halves[:, None], down_core[:, None], at).reshape(hidden_here, width)
    parts, down = fence(parts, down)
    fed = gathered_rows(parts)
    gate_up = matmul(fed, expand)
    gate = gate_up[:, :hidden_here]
    upward = gate_up[:, hidden_here:]
    activated, gelu_pull = jax.vjp(gelu_tanh, gate)
    inner = (activated * upward).astype(LOW)

    inner, res_wires = fence(inner, res_wires)
    res_all = gathered_rows(gather_join(res_parts, res_wires))
    grad_res = res.astype(F32)
    grad_inner = matmul(res_all, down, NT)
    grad_gate = gelu_pull(grad_inner * upward)[0]
    grad_gate_up = jnp.concatenate([grad_gate, grad_inner * activated], axis=1).astype(LOW)
    grad_fed = matmul(grad_gate_up, expand, NT).astype(LOW)
    grad_fed, inner, res_all, fed = fence(grad_fed, inner, res_all, fed)
    parts = reduce_step(to_parts(grad_fed), 2)
    grad_down = matmul(inner, res_all, TN).astype(LOW).reshape(halves, 2, hidden_shard, width)
    parts, inner, grad_down = fence(parts, inner, grad_down)
    parts = reduce_step(parts, 1)
    down_wire = send_cores(grad_down, at, 1)
    final = matmul(by_rows_of_light(inner), down).astype(LOW)
    parts, final, down_wire = fence(parts, final, down_wire)
    parts = reduce_step(parts, 0)
    grad_down = add_cores(grad_down, down_wire, at, 1)
    parts, grad_down = fence(parts, grad_down)
    grad_normed_two = own_rows(parts)
    grad_hidden = grad_res + norm_back(grad_normed_two * gain_feed, unit_two, scale_two)

    grad_hidden_low = grad_hidden.astype(LOW)
    grad_mixed = matmul(grad_hidden_low, out_full, NT).astype(LOW)
    grad_mixed = grad_mixed.reshape(2 * rows, 8, 2 * span).transpose(1, 0, 2)
    grad_mixed, fed, grad_down = fence(grad_mixed, fed, grad_down)
    grad_down = scatter_halves(grad_down)
    grad_mixed = exchange(grad_mixed)
    grad_expand = matmul(fed, grad_gate_up, TN).astype(LOW).reshape(halves, 8, 2, shard_rows, -1)
    if one_block:
        mixed = by_light_distance(mixed_chunks, at)
    grad_mixed, final, mixed, grad_expand = fence(grad_mixed, final, mixed, grad_expand)
    final_parts = list(final.reshape(2, 8, rows, width))
    grad_mixed = grad_mixed.reshape(16 * rows, 2 * span)
    g_halves = grad_mixed[:, :span], grad_mixed[:, span:]
    g_own = jnp.where(at["c"] == 0, *g_halves)
    g_other = swap(jnp.where(at["c"] == 0, *g_halves[::-1]), "c")
    expand_wire = send_cores(grad_expand, at, 2)
    grad_out = matmul(mixed, grad_hidden_low, TN)
    if one_block:
        grad_out = grad_out.astype(LOW).reshape(2, 8, 2, HEAD_DIM, width)
        out_wire = send_cores(grad_out, at, 2)
    else:
        out_wire = ()
    g_own, g_other, expand_wire, out_wire = fence(g_own, g_other, expand_wire, out_wire)
    grad_expand = add_cores(grad_expand, expand_wire, at, 2)
    if one_block:
        grads = (g_own, g_other)
    else:
        grads = (in_order(jnp.concatenate([g_own, g_other], axis=0), chunk_at),)
    final_wires = light_send(final_parts)
    grad_expand = scatter_halves(grad_expand)
    *half_grads, d_diag_first = attend_backward(one_block, halo, 0, tables, tokens, extras[0], grads, saved[0], ())
    half_grads, final_wires, out_wire, grad_out = fence(half_grads, final_wires, out_wire, grad_out)
    final_parts = reduce_add(final_parts, final_wires)
    final_wires = light_send(final_parts)
    if one_block:
        out_parts = list(add_cores(grad_out, out_wire, at, 2))
        out_wires = light_send(out_parts)
    else:
        out_parts = out_wires = ()
    *d_all, d_diag = attend_backward(
        one_block, halo, 1, tables, tokens, extras[1], grads, saved[1], tuple(half_grads)
    )
    if one_block:
        d_own, d_other = d_all
    else:
        dq, dk, dv = d_all
        d_all = jnp.concatenate([dq, add_sides(dk, halo), add_sides(dv, halo)], axis=1)
        d_own, d_other = jnp.split(as_pieces(d_all.astype(LOW), spread_at), 2, axis=0)
    d_own, d_other, final_wires, out_wires, grad_expand = fence(d_own, d_other, final_wires, out_wires, grad_expand)
    d_other = swap(d_other, "c")
    final_parts = reduce_add(final_parts, final_wires)
    final_wires = light_send(final_parts)
    if one_block:
        out_parts = reduce_add(out_parts, out_wires)
        out_wires = light_send(out_parts)
    (d_other,) = fence(d_other)
    grad_projected = jnp.concatenate([d_own, d_other], axis=1)
    grad_normed_one = matmul(grad_projected, project, NT).astype(LOW)
    grad_normed_one, grad_projected, final_wires, out_wires, final_parts, out_parts = fence(
        grad_normed_one, grad_projected, final_wires, out_wires, final_parts, out_parts
    )

    def turn(got):
        return jnp.concatenate([got[..., side:], got[..., :side]], axis=-1)

    parts = reduce_step(to_parts(grad_normed_one), 2)
    grad_expand = exchange(grad_expand)
    grad_project = matmul(normed_one, grad_projected, TN).astype(LOW).reshape(halves, 8, 2, shard_rows, -1)
    project_wire = send_cores(grad_project, at, 2)
    grad_project = add_cores(grad_project, turn(project_wire), at, 2)
    moved = grad_normed_one.astype(F32) * gathered_scale * gathered.astype(F32)
    grad_gain_rows = jnp.sum(moved, axis=0)
    grad_feed_gain = jnp.sum(grad_normed_two * unit_two, axis=0)
    sums = jnp.concatenate([d_diag_first, d_diag], axis=0)
    hot = buckets == jnp.arange(BUCKETS, dtype=jnp.int32)[:, None]
    sums = jnp.sum(jnp.where(hot[:, None], sums, 0.0), axis=2)
    lanes = (jnp.arange(16, dtype=jnp.int32) == lane).astype(F32)
    grad_position_bias = (sums[:, None, :] * lanes[:, None]).reshape(-1)
    count = lax.axis_size(AXES)
    gains = attention_norm_gain.shape[0]
    small = [grad_feed_gain, grad_gain_rows, grad_position_bias]
    small = jnp.concatenate([line.reshape(count, -1) for line in small], axis=1)
    final_near, final_far = [part[0].astype(F32) for part in reduce_add(final_parts, final_wires)]
    final_near = (hidden_one[:rows] + final_near).astype(LOW)
    final_far = (hidden_one[rows:] + final_far).astype(LOW)
    if one_block:
        out_parts = reduce_add(out_parts, out_wires)
    parts, small, final_far, grad_project, out_parts = fence(parts, small, final_far, grad_project, out_parts)
    grad_project = scatter_halves(grad_project)
    small = sum_line(small)
    parts = reduce_step(parts, 1)
    final_far = swap(final_far, "h")
    if one_block:
        out_wires = light_send(out_parts)
    parts, small, out_wires = fence(parts, small, out_wires)
    parts = reduce_step(parts, 0)
    if one_block:
        grad_out = scatter_halves(jnp.concatenate(reduce_add(out_parts, out_wires), axis=0))
    parts, grad_project = fence(parts, grad_project)
    grad_part = own_rows(parts)
    unit_one, scale_one = normalize(tokens_here)
    token_grad = grad_hidden + norm_back(grad_part * gain_attn, unit_one, scale_one)
    token_grad = token_grad.astype(LOW)
    input_grad = both(token_grad[:rows], swap(token_grad[rows:], "h"), near, 0)
    grad_project = exchange(grad_project)
    layer_output = both(final_near, final_far, near, 0)
    grad_expand = join_columns(grad_expand, expand_order, 2 * hidden_shard)
    grad_feed_gain = small[:gains]
    grad_attention_gain = small[gains : 2 * gains]
    grad_position_bias = small[2 * gains :]
    grad_out = grad_out.astype(F32) if one_block else grad_out_wide(grad_out)
    grad_down = grad_down.astype(F32)
    grad_project = jnp.where(at["c"] == 0, grad_project, turn(grad_project))
    grad_project = join_columns(grad_project, project_order, span)
    return (
        layer_output,
        input_grad,
        grad_attention_gain,
        grad_project,
        grad_out,
        grad_position_bias,
        grad_feed_gain,
        grad_expand,
        grad_down,
    )


def solution(mesh):
    wide = Mesh(mesh.devices.reshape(-1, 2, 2, 2, 2, 2), AXES)
    lead, tokens, rows = P(AXES), P(None, AXES), P(AXES, None)
    return jax.shard_map(
        local,
        mesh=wide,
        in_specs=(tokens, tokens, tokens, tokens, P(), lead, rows, rows, lead, lead, rows, rows),
        out_specs=(tokens, tokens, lead, rows, rows, lead, lead, rows, rows),
        check_vma=False,
    )
```

```python
import jax
import jax.numpy as jnp
import numpy as np
from jax import lax
from jax.experimental import pallas as pl
from jax.experimental.pallas import tpu as pltpu
from jax.sharding import Mesh, PartitionSpec as P

EPS = 1e-06
AXES = ("b", "h", "p", "q", "r", "c")
CUBE = ("p", "q", "r")
SWAP = [(0, 1), (1, 0)]
LOW = jnp.bfloat16
F32 = jnp.float32
HEAD_DIM = 64
BUCKETS = 32
WINDOW = 1024
BLK = 256
FAR = float(2**30)
NT = (((1,), (1,)), ((), ()))
NN = (((1,), (0,)), ((), ()))
DIAGS = 2 * (WINDOW // BLK) + 1
MID = WINDOW // BLK
PAD_LANE = 16
LINE = (DIAGS + 1) * BLK
FORWARD_COST = 1
BACKWARD_COST = 1


def dot(a, b, dims=NN):
    return lax.dot_general(a, b, dims, preferred_element_type=jnp.float32)


def fill_rows(table, own, other, rows, targets):
    pieces = own.shape[0] // rows
    for side, src in enumerate((own, other)):
        for i in range(pieces):
            at = pl.multiple_of(table[side * pieces + i], rows)
            col = 0
            for dst in targets:
                wide = dst.shape[-1]
                dst[pl.ds(at, rows), :] = src[i * rows : (i + 1) * rows, col : col + wide]
                col += wide


def drain_rows(table, src, own, other, rows, col):
    pieces = own.shape[0] // rows
    wide = src.shape[-1]
    for side, dst in enumerate((own, other)):
        for i in range(pieces):
            at = pl.multiple_of(table[side * pieces + i], rows)
            dst[i * rows : (i + 1) * rows, col : col + wide] = src[pl.ds(at, rows), :]


def make_tiles(line, tiles):
    strip = jnp.broadcast_to(line[...], (8, LINE))
    strip = pltpu.roll(strip, 0, 1, stride=1, stride_axis=0)
    for g in range(BLK // 8):
        moved = strip if g == 0 else pltpu.roll(strip, 8 * g, 1)
        for d in range(DIAGS):
            first = BLK * (DIAGS - d)
            tiles[d, 8 * g : 8 * g + 8, :] = moved[:, first : first + BLK]
    tiles[DIAGS + 1] = jnp.full((BLK, BLK), -FAR, jnp.float32)


def sum_tiles(tiles, line):
    total = jnp.zeros((8, LINE), jnp.float32)
    edge = jnp.zeros((8, BLK), jnp.float32)
    for g in range(BLK // 8):
        parts = [tiles[d, 8 * g : 8 * g + 8, :] for d in reversed(range(DIAGS))]
        strip = jnp.concatenate([edge] + parts, axis=1)
        total = total + (strip if g == 0 else pltpu.roll(strip, LINE - 8 * g, 1))
    out = total[0:1]
    for r in range(1, 8):
        out = out + pltpu.roll(total[r : r + 1], LINE - r, 1)
    line[...] = out


def make_own_tile(key_more, tiles, at):
    rows = lax.broadcasted_iota(jnp.int32, (BLK, BLK), 0)
    cols = lax.broadcasted_iota(jnp.int32, (BLK, BLK), 1)
    gone = key_more[pl.ds(at, BLK), PAD_LANE : PAD_LANE + 1].astype(jnp.float32)
    tiles[DIAGS] = tiles[MID] + jnp.where(rows == cols, 0.0, gone)


def half_of(n):
    lanes = lax.broadcasted_iota(jnp.int32, (BLK, 2 * HEAD_DIM), 1)
    return (lanes < HEAD_DIM) if n == 0 else (lanes >= HEAD_DIM)


def build_pairs(n, q, k, query_more, key_more, qx, kx):
    here = half_of(n)
    lanes = lax.broadcasted_iota(jnp.int32, (BLK, 2 * HEAD_DIM), 1)
    mark = jnp.where(lanes % HEAD_DIM == PAD_LANE, 1.0, 0.0).astype(jnp.bfloat16)

    def fill_q(i, _):
        rows = pl.ds(pl.multiple_of(i * BLK, BLK), BLK)
        more = query_more[rows, :]
        qx[0, rows, :] = jnp.where(here, q[rows, :], more)
        qx[1, rows, :] = jnp.where(here, q[rows, :], more + mark)
        return 0

    def fill_k(i, _):
        rows = pl.ds(pl.multiple_of(i * BLK, BLK), BLK)
        kx[rows, :] = jnp.where(here, k[rows, :], key_more[rows, :])
        return 0

    lax.fori_loop(0, q.shape[0] // BLK, fill_q, 0)
    lax.fori_loop(0, k.shape[0] // BLK, fill_k, 0)


def pair_of(j, first, end, here):
    out = []
    for m in range(2):
        block = first + 2 * j + m
        there = block < end
        block = jnp.minimum(block, end - 1)
        same = (there & (block == here)).astype(jnp.int32)
        away = block - here + MID
        tile = jnp.where(there, jnp.where(block == here, DIAGS, away), DIAGS + 1)
        out.append((pl.ds(pl.multiple_of(block * BLK, BLK), BLK), same, away, tile))
    return out


def forward_kernel(local, halo, n, *refs):
    if local:
        pos, pos_out, rng, own, other, query_more, key_more, diag, *refs = refs
        before, refs = refs[:n], refs[n:]
        outs, refs = (refs[:2], refs[2:]) if n else ((), refs)
        mixed_t, lse, q, k, v, qx, kx, vt, tiles, *joined = refs
        fill_rows(pos, own, other, own.shape[0] // 48, (q, k, v))
    else:
        rng, q, k, v, query_more, key_more, diag, *refs = refs
        before, refs = refs[:n], refs[n:]
        joined, refs = refs[:n], refs[n:]
        mixed_t, lse, qx, kx, vt, tiles = refs
    make_tiles(diag, tiles)
    build_pairs(n, q, k, query_more, key_more, qx, kx)
    cols = slice(n * HEAD_DIM, (n + 1) * HEAD_DIM)

    def turn(i, _):
        rows = pl.ds(pl.multiple_of(i * BLK, BLK), BLK)
        vt[:, rows] = v[rows, :].T[cols]
        return 0

    lax.fori_loop(0, v.shape[0] // BLK, turn, 0)

    def query_block(i, _):
        at = pl.multiple_of(i * BLK, BLK)
        rows = pl.ds(at, BLK)
        here = i + halo // BLK
        first, end = rng[0, i], rng[1, i]
        make_own_tile(key_more, tiles, pl.multiple_of(here * BLK, BLK))

        def key_blocks(j, carry):
            top, total, acc = carry
            both = pair_of(j, first, end, here)
            s = [
                dot(kx[span, :], qx[1 - same, rows, :], NT) + tiles[tile]
                for span, same, _, tile in both
            ]
            high = jnp.max(jnp.maximum(s[0], s[1]), axis=0, keepdims=True)
            high = jnp.maximum(top, high)
            p = [jnp.exp(part - high) for part in s]
            shrink = jnp.exp(top - high)
            total = total * shrink + jnp.sum(p[0] + p[1], axis=0, keepdims=True)
            acc = acc * shrink
            for part, (span, _, _, _) in zip(p, both):
                acc = acc + dot(vt[:, span], part.astype(jnp.bfloat16))
            return high, total, acc

        start = (
            jnp.full((1, BLK), -1e30, jnp.float32),
            jnp.zeros((1, BLK), jnp.float32),
            jnp.zeros((HEAD_DIM, BLK), jnp.float32),
        )
        top, total, acc = lax.fori_loop(0, (end - first + 1) // 2, key_blocks, start)
        mixed_t[:, rows] = acc / total
        lse[:, rows] = top + jnp.log(total)
        if n:
            whole = jnp.concatenate([before[0][:, rows], mixed_t[:, rows]], axis=0)
            joined[0][rows, :] = whole.T.astype(jnp.bfloat16)
        return 0

    lax.fori_loop(0, q.shape[0] // BLK, query_block, 0)
    if local and n:
        drain_rows(pos_out, joined[0], *outs, outs[0].shape[0] // 16, 0)


def backward_kernel(local, halo, n, *refs):
    if local:
        pos, pos_out, rng, own, other, query_more, key_more, diag, g_own, g_other, mixed_t, lse, *refs = refs
        before, refs = refs[: 3 * n], refs[3 * n :]
        outs, refs = refs[: 3 - n], refs[3 - n :]
        d_diag, q, k, v, g, qx, kx, vx, gx, kt, tiles, dk, dv, dtiles, *whole = refs
        fill_rows(pos, own, other, own.shape[0] // 48, (q, k, v))
        fill_rows(pos_out, g_own, g_other, g_own.shape[0] // 16, (g,))
        dq_out, dk_out, dv_out = whole if n else outs
    else:
        rng, q, k, v, query_more, key_more, diag, g, mixed_t, lse, *refs = refs
        before, refs = refs[: 3 * n], refs[3 * n :]
        dq_out, dk_out, dv_out, d_diag, qx, kx, vx, gx, kt, tiles, dk, dv, dtiles = refs
    make_tiles(diag, tiles)
    build_pairs(n, q, k, query_more, key_more, qx, kx)
    blank = jnp.zeros((BLK, 2 * HEAD_DIM), jnp.bfloat16)
    mine = half_of(n)
    cols = slice(n * HEAD_DIM, (n + 1) * HEAD_DIM)

    def store(out, slot, rows, part):
        part = part.astype(out.dtype)
        out[rows, :] = jnp.where(mine, part, before[slot][rows, :]) if n else part

    def turn(i, _):
        rows = pl.ds(pl.multiple_of(i * BLK, BLK), BLK)
        kt[:, rows] = k[rows, :].T[cols]
        vx[rows, :] = jnp.where(mine, v[rows, :], blank)
        dk[rows, :] = jnp.zeros((BLK, 2 * HEAD_DIM), jnp.float32)
        dv[rows, :] = jnp.zeros((BLK, 2 * HEAD_DIM), jnp.float32)
        return 0

    def spread_g(i, _):
        rows = pl.ds(pl.multiple_of(i * BLK, BLK), BLK)
        gx[rows, :] = jnp.where(mine, g[rows, :], blank)
        return 0

    lax.fori_loop(0, k.shape[0] // BLK, turn, 0)
    lax.fori_loop(0, q.shape[0] // BLK, spread_g, 0)
    for slot in range(DIAGS):
        dtiles[slot] = jnp.zeros((BLK, BLK), jnp.float32)

    def query_block(i, _):
        at = pl.multiple_of(i * BLK, BLK)
        rows = pl.ds(at, BLK)
        here = i + halo // BLK
        first, end = rng[0, i], rng[1, i]
        make_own_tile(key_more, tiles, pl.multiple_of(here * BLK, BLK))
        turned = g[rows, :].astype(jnp.float32).T[cols] * mixed_t[:, rows]
        delta = jnp.sum(turned, axis=0, keepdims=True)
        level = lse[:, rows]

        def key_blocks(j, acc):
            both = pair_of(j, first, end, here)
            s = [
                dot(kx[span, :], qx[1 - same, rows, :], NT) + tiles[tile]
                for span, same, _, tile in both
            ]
            dp = [dot(vx[span, :], gx[rows, :], NT) for span, _, _, _ in both]
            for m, (span, same, away, _) in enumerate(both):
                p = jnp.exp(s[m] - level)
                ds = (p * (dp[m] - delta)).astype(jnp.bfloat16)
                dtiles[away] += ds.astype(jnp.float32)
                dv[span, :] += dot(p.astype(jnp.bfloat16), gx[rows, :])
                dk[span, :] += dot(ds, qx[0, rows, :])
                acc = acc + dot(kt[:, span], ds)
            return acc

        zero = jnp.zeros((HEAD_DIM, BLK), jnp.float32)
        acc = lax.fori_loop(0, (end - first + 1) // 2, key_blocks, zero)
        empty = jnp.zeros((HEAD_DIM, BLK), jnp.float32)
        store(dq_out, 0, rows, jnp.concatenate([empty, acc] if n else [acc, empty], axis=0).T)
        return 0

    lax.fori_loop(0, q.shape[0] // BLK, query_block, 0)

    sum_tiles(dtiles, d_diag)

    def finish(i, _):
        rows = pl.ds(pl.multiple_of(i * BLK, BLK), BLK)
        store(dk_out, 1, rows, dk[rows, :])
        store(dv_out, 2, rows, dv[rows, :])
        return 0

    lax.fori_loop(0, k.shape[0] // BLK, finish, 0)
    if local and n:
        rows = own.shape[0] // 48
        for col, src in enumerate(whole):
            drain_rows(pos, src, *outs, rows, col * 2 * HEAD_DIM)


def specs(smem, vmem):
    return [pl.BlockSpec(memory_space=pltpu.SMEM)] * smem + [pl.BlockSpec(memory_space=pltpu.VMEM)] * vmem


def costs(length, times):
    return pl.CostEstimate(flops=length * times, bytes_accessed=1 << 16, transcendentals=0)


def attend_forward(local, halo, n, tables, tokens, extras, before):
    length, reach = extras[0].shape[0], extras[1].shape[0]
    both = 2 * HEAD_DIM
    shape = jax.ShapeDtypeStruct
    low = jnp.bfloat16
    outs, scratch, last = [], [], []
    if n:
        outs = [shape((length // 2, both), low)] * 2 if local else [shape((length, both), low)]
    outs = outs + [shape((HEAD_DIM, length), jnp.float32), shape((1, length), jnp.float32)]
    if local:
        scratch = [pltpu.VMEM((length, both), low)] + [pltpu.VMEM((reach, both), low)] * 2
        last = [pltpu.VMEM((length, both), low)] * n
    scratch = scratch + [
        pltpu.VMEM((2, length, both), low),
        pltpu.VMEM((reach, both), low),
        pltpu.VMEM((HEAD_DIM, reach), low),
        pltpu.VMEM((DIAGS + 2, BLK, BLK), jnp.float32),
    ]
    return pl.pallas_call(
        lambda *refs: forward_kernel(local, halo, n, *refs),
        out_shape=outs,
        in_specs=specs(len(tables), len(tokens) + len(extras) + len(before)),
        out_specs=specs(0, len(outs)),
        scratch_shapes=scratch + last,
        compiler_params=pltpu.CompilerParams(vmem_limit_bytes=56 << 20),
        cost_estimate=costs(length, FORWARD_COST),
    )(*tables, *tokens, *extras, *before)


def attend_backward(local, halo, n, tables, tokens, extras, grads, saved, before):
    length, reach = extras[0].shape[0], extras[1].shape[0]
    both = 2 * HEAD_DIM
    shape = jax.ShapeDtypeStruct
    low = jnp.bfloat16
    kind = low if local else jnp.float32
    d_diag = shape((1, LINE), jnp.float32)
    scratch, last = [], []
    if local and n:
        outs = [shape((length // 2, 3 * both), low)] * 2 + [d_diag]
    else:
        outs = [shape((length, both), kind)] + [shape((reach, both), kind)] * 2 + [d_diag]
    if local:
        scratch = [pltpu.VMEM((size, both), low) for size in (length, reach, reach, length)]
        last = [pltpu.VMEM((size, both), low) for size in (length, reach, reach)] * n
    scratch = scratch + [
        pltpu.VMEM((2, length, both), low),
        pltpu.VMEM((reach, both), low),
        pltpu.VMEM((reach, both), low),
        pltpu.VMEM((length, both), low),
        pltpu.VMEM((HEAD_DIM, reach), low),
        pltpu.VMEM((DIAGS + 2, BLK, BLK), jnp.float32),
        pltpu.VMEM((reach, both), jnp.float32),
        pltpu.VMEM((reach, both), jnp.float32),
        pltpu.VMEM((DIAGS, BLK, BLK), jnp.float32),
    ]
    operands = (*tokens, *extras, *grads, *saved, *before)
    return pl.pallas_call(
        lambda *refs: backward_kernel(local, halo, n, *refs),
        out_shape=outs,
        in_specs=specs(len(tables), len(operands)),
        out_specs=specs(0, len(outs)),
        scratch_shapes=scratch + last,
        compiler_params=pltpu.CompilerParams(vmem_limit_bytes=60 << 20),
        cost_estimate=costs(length, BACKWARD_COST),
    )(*tables, *operands)


def bucket_line(bucket_table):
    edge = jnp.full((2 * BLK,), -1, jnp.int32)
    wide = jnp.concatenate([edge, bucket_table, edge])[::-1]
    return wide[BLK - 1 : BLK - 1 + LINE]


def query_ranges(segments, halo):
    reach = segments.shape[0]
    first = halo + BLK * jnp.arange((reach - 2 * halo) // BLK, dtype=jnp.int32)
    last = first + BLK - 1
    cut = segments.reshape(-1, BLK)[halo // BLK : (reach - halo) // BLK]
    low = jnp.sum(segments[None, :] < cut[:, :1], axis=1)
    high = jnp.sum(segments[None, :] <= cut[:, -1:], axis=1)
    low = jnp.maximum(low, jnp.maximum(first - WINDOW + 1, 0))
    high = jnp.minimum(high, jnp.minimum(last + WINDOW, reach))
    return jnp.stack([low // BLK, (high + BLK - 1) // BLK]).astype(jnp.int32)


def barring_lanes(codes, halo):
    lanes = jnp.arange(2 * HEAD_DIM, dtype=jnp.int32) % HEAD_DIM
    segments = (codes >> 1)[:, None]
    key_more = jnp.where(lanes == segments, 1.0, 0.0)
    key_more = jnp.where((lanes == PAD_LANE) & ((codes & 1) == 0)[:, None], -FAR, key_more)
    mine = segments[halo : codes.shape[0] - halo]
    query_more = jnp.where((lanes < PAD_LANE) & (lanes != mine), -FAR, 0.0)
    return query_more.astype(jnp.bfloat16), key_more.astype(jnp.bfloat16)


def swap(value, axis):
    return lax.ppermute(value, axis, SWAP)


def pick(value, index, axis=0):
    return lax.dynamic_index_in_dim(value, index, axis, keepdims=False)


def both(mine, theirs, bit, axis, joined=False):
    put = jnp.concatenate if joined else jnp.stack
    return jnp.where(bit == 0, put([mine, theirs], axis), put([theirs, mine], axis))


def matmul(left, right, dims=NN):
    return lax.dot_general(left, right, dims, preferred_element_type=F32)


TN = (((0,), (0,)), ((), ()))


def fence(*values):
    return lax.optimization_barrier(values)


def cut_kernel(order, wide, src, out):
    for m in range(8):
        for j, o in enumerate(order):
            first = (o * 8 + m) * wide
            out[m, :, j * wide : (j + 1) * wide] = src[:, first : first + wide]


def cut_columns(matrix, order, wide):
    rows = matrix.shape[0]
    return pl.pallas_call(
        lambda src, out: cut_kernel(order, wide, src, out),
        out_shape=jax.ShapeDtypeStruct((8, rows, len(order) * wide), matrix.dtype),
        in_specs=specs(0, 1),
        out_specs=specs(0, 1)[0],
        compiler_params=pltpu.CompilerParams(vmem_limit_bytes=32 << 20),
        cost_estimate=pl.CostEstimate(flops=0, bytes_accessed=4 * matrix.size, transcendentals=0),
    )(matrix)


def join_kernel(order, wide, src, out):
    for m in range(8):
        for j, o in enumerate(order):
            first = (o * 8 + m) * wide
            part = src[m, :, j * wide : (j + 1) * wide]
            out[:, first : first + wide] = part.astype(jnp.float32)


def join_columns(chunks, order, wide):
    rows = chunks.shape[1]
    return pl.pallas_call(
        lambda src, out: join_kernel(order, wide, src, out),
        out_shape=jax.ShapeDtypeStruct((rows, len(order) * 8 * wide), F32),
        in_specs=specs(0, 1),
        out_specs=specs(0, 1)[0],
        compiler_params=pltpu.CompilerParams(vmem_limit_bytes=32 << 20),
        cost_estimate=pl.CostEstimate(flops=0, bytes_accessed=6 * chunks.size, transcendentals=0),
    )(chunks)


def distance(k, i):
    mask = 0
    for step in range(3):
        if i >> step & 1:
            mask |= 4 >> (k + step) % 3
    return mask


def join_kernel_rows(counts, *refs):
    total = sum(counts)
    sources, outs, sems = refs[:total], refs[total : total + len(counts)], refs[-1]
    copies = []
    for out, count in zip(outs, counts):
        at = 0
        for src in sources[len(copies) : len(copies) + count]:
            rows = src.shape[0]
            copies.append(pltpu.make_async_copy(src, out.at[pl.ds(at, rows)], sems.at[len(copies)]))
            at += rows
    for copy in copies:
        copy.start()
    for copy in copies:
        copy.wait()


def join_rows(*lists):
    counts = [len(pieces) for pieces in lists]
    pieces = [piece for listed in lists for piece in listed]
    shapes = [
        jax.ShapeDtypeStruct((sum(p.shape[0] for p in listed),) + listed[0].shape[1:], listed[0].dtype)
        for listed in lists
    ]
    outs = pl.pallas_call(
        lambda *refs: join_kernel_rows(counts, *refs),
        out_shape=shapes,
        in_specs=[pl.BlockSpec(memory_space=pl.ANY)] * len(pieces),
        out_specs=specs(0, len(lists)),
        scratch_shapes=[pltpu.SemaphoreType.DMA((len(pieces),))],
        compiler_params=pltpu.CompilerParams(vmem_limit_bytes=32 << 20),
        cost_estimate=pl.CostEstimate(
            flops=0, bytes_accessed=4 * sum(p.size for p in pieces), transcendentals=0
        ),
    )(*pieces)
    return list(outs)


def gather_send(parts, step):
    return [swap(parts[k], CUBE[(k + step) % 3]) for k in range(3)]


def gather_join(parts, wires):
    return join_rows(*([a, b] for a, b in zip(parts, wires)))


def gather_step(parts, step):
    return gather_join(parts, gather_send(parts, step))


def reduce_send(parts):
    half = parts[0].shape[0] // 2
    step = half.bit_length() - 1
    return [swap(parts[k][half:], CUBE[(k + step) % 3]) for k in range(3)]


def reduce_add(parts, wires):
    half = parts[0].shape[0] // 2
    return [(a[:half].astype(F32) + b.astype(F32)).astype(LOW) for a, b in zip(parts, wires)]


def reduce_step(parts, step):
    return reduce_add(parts, reduce_send(parts))


def thirds(rows):
    third = rows.shape[0] // 3
    return [rows[k * third : (k + 1) * third][None] for k in range(3)]


def gathered_rows(parts):
    return join_rows([part.reshape(-1, part.shape[-1]) for part in parts])[0]


def to_parts(rows):
    return list(rows.reshape(3, 8, -1, rows.shape[-1]))


def own_rows(parts):
    return jnp.concatenate([part[0] for part in parts], axis=0).astype(F32)


def exchange(chunks):
    return lax.all_to_all(chunks, CUBE, 0, 0)


def move_kernel(gather, rows, table, src, out):
    for n in range(src.shape[0] // rows):
        fixed = pl.ds(n * rows, rows)
        moved = pl.ds(pl.multiple_of(table[n], rows), rows)
        if gather:
            out[fixed, :] = src[moved, :]
        else:
            out[moved, :] = src[fixed, :]


def move_rows(table, src, gather):
    rows = src.shape[0] // table.shape[0]
    return pl.pallas_call(
        lambda *refs: move_kernel(gather, rows, *refs),
        out_shape=jax.ShapeDtypeStruct(src.shape, src.dtype),
        in_specs=specs(1, 1),
        out_specs=specs(0, 1)[0],
        compiler_params=pltpu.CompilerParams(vmem_limit_bytes=32 << 20),
        cost_estimate=pl.CostEstimate(flops=0, bytes_accessed=4 * src.size, transcendentals=0),
    )(table, src)


def tell_all(line):
    count = lax.axis_size(AXES)
    return lax.all_to_all(jnp.broadcast_to(line, (count,) + line.shape), AXES, 0, 0)


def wire_halves(shard):
    if lax.axis_size("b") == 1:
        return swap(shard, "h")
    return lax.all_gather(shard, ("b", "h"), axis=0)


def wire_halves_twice(shard):
    if lax.axis_size("b") == 1:
        return swap(shard[:4], "h"), swap(shard[4:], "h")
    return (wire_halves(shard),)


def turned_kernel(left, right, out):
    def block(i, _):
        cols = pl.ds(pl.multiple_of(i * BLK, BLK), BLK)
        out[cols, :] = dot(left[:, cols].T, right[...]).astype(out.dtype)
        return 0

    lax.fori_loop(0, left.shape[1] // BLK, block, 0)


def turned_matmul(left, right):
    return pl.pallas_call(
        turned_kernel,
        out_shape=jax.ShapeDtypeStruct((left.shape[1], right.shape[1]), LOW),
        in_specs=specs(0, 2),
        out_specs=specs(0, 1)[0],
        compiler_params=pltpu.CompilerParams(vmem_limit_bytes=40 << 20),
        cost_estimate=pl.CostEstimate(flops=0, bytes_accessed=1 << 16, transcendentals=0),
    )(left, right)


def scaled_kernel(left, right, scale, out):
    step = 64
    out[...] = jnp.zeros_like(out)

    def block(i, _):
        rows = pl.ds(pl.multiple_of(i * step, step), step)
        part = left[rows, :].astype(jnp.float32) * scale[rows, :] * right[rows, :].astype(jnp.float32)
        total = part[0:8]
        for j in range(1, step // 8):
            total = total + part[8 * j : 8 * j + 8]
        out[...] += total
        return 0

    lax.fori_loop(0, left.shape[0] // step, block, 0)


def scaled_sum(left, right, scale):
    eight = pl.pallas_call(
        scaled_kernel,
        out_shape=jax.ShapeDtypeStruct((8, left.shape[1]), F32),
        in_specs=specs(0, 3),
        out_specs=specs(0, 1)[0],
        compiler_params=pltpu.CompilerParams(vmem_limit_bytes=40 << 20),
        cost_estimate=pl.CostEstimate(flops=0, bytes_accessed=1 << 16, transcendentals=0),
    )(left, right, scale)
    return jnp.sum(eight, axis=0)


def light_distance(part, i):
    return (i & 1) * 4 | (i >> 1 & 1) * (2, 1)[part] | (i >> 2 & 1) * (1, 2)[part]


def light_send(parts):
    half = parts[0].shape[0] // 2
    axes = {4: ("r", "q"), 2: ("q", "r"), 1: ("p", "p")}[half]
    return [swap(part[half:], axis) for part, axis in zip(parts, axes)]


def by_rows_kernel(src, out):
    count = src.shape[0] // 48
    for part in range(2):
        for i in range(8):
            mask = light_distance(part, i)
            for j in range(3):
                row = 3 * part + j
                k = row // 2
                place = [distance(k, e) for e in range(8)].index(mask)
                first = ((k * 8 + place) * 2 + row % 2) * count
                at = ((part * 8 + i) * 3 + j) * count
                out[at : at + count, :] = src[first : first + count, :]


def by_rows_of_light(rows):
    return pl.pallas_call(
        by_rows_kernel,
        out_shape=jax.ShapeDtypeStruct(rows.shape, rows.dtype),
        in_specs=specs(0, 1),
        out_specs=specs(0, 1)[0],
        compiler_params=pltpu.CompilerParams(vmem_limit_bytes=32 << 20),
        cost_estimate=pl.CostEstimate(flops=0, bytes_accessed=1 << 16, transcendentals=0),
    )(rows)


def by_light_kernel(table, src, out):
    rows, wide = src.shape[0] // 8, src.shape[1] // 2
    for part in range(2):
        for i in range(8):
            at = pl.ds(pl.multiple_of((table[0] ^ light_distance(part, i)) * rows, rows), rows)
            to = (part * 8 + i) * wide
            out[:, to : to + wide] = src[at, part * wide : (part + 1) * wide]


def by_light_distance(chunks, at):
    tall, wide = chunks.shape
    return pl.pallas_call(
        by_light_kernel,
        out_shape=jax.ShapeDtypeStruct((tall // 8, wide * 8), chunks.dtype),
        in_specs=specs(1, 1),
        out_specs=specs(0, 1)[0],
        compiler_params=pltpu.CompilerParams(vmem_limit_bytes=32 << 20),
        cost_estimate=pl.CostEstimate(flops=0, bytes_accessed=1 << 16, transcendentals=0),
    )(at["cube"][None].astype(jnp.int32), chunks)


def gather_halves(shard):
    return lax.all_gather(shard, ("b", "h"), axis=0)


def scatter_halves(parts):
    return lax.psum_scatter(parts, ("b", "h"), scatter_dimension=0, tiled=False)


def weave_halves(halves, core, at):
    if lax.axis_size("b") > 1:
        return both(halves, core, at["c"], 2)
    count = halves.shape[1]
    halves, core = (v.reshape((-1,) + v.shape[2:]) for v in (halves, core))
    return weave([(halves, None, 0), (core, None, 1)], at, count, True)


def join_halves(shard, wire, at):
    return both(shard, wire, at["h"], 0) if lax.axis_size("b") == 1 else wire


def send_halves(parts, at):
    if lax.axis_size("b") == 1:
        return swap(pick(parts, 1 - at["h"]), "h")
    return lax.psum_scatter(parts.astype(F32), ("b", "h"), scatter_dimension=0, tiled=False)


def add_halves(parts, wire, at):
    if lax.axis_size("b") == 1:
        return pick(parts, at["h"]).astype(F32) + wire.astype(F32)
    return wire


def add_cores(grad, wire, at, axis):
    return (pick(grad, at["c"], axis).astype(F32) + wire.astype(F32)).astype(LOW)


def send_cores(grad, at, axis):
    return swap(pick(grad, 1 - at["c"], axis), "c")


def fetch_out_wide(shard):
    whole = lax.all_gather(shard, AXES, axis=0, tiled=True)
    whole = whole.reshape(2, 8, 2, HEAD_DIM, -1).transpose(1, 0, 2, 3, 4)
    return whole.reshape(-1, whole.shape[-1])


def grad_out_wide(grad):
    grad = grad.reshape(8, 2, 2, HEAD_DIM, -1).transpose(1, 0, 2, 3, 4)
    return lax.psum_scatter(grad.reshape(-1, grad.shape[-1]), AXES, scatter_dimension=0, tiled=True)


def gelu_tanh(value):
    return (
        0.5
        * value
        * (1.0 + jnp.tanh(0.7978845608028654 * (value + 0.044715 * value * value * value)))
    )


def normalize(hidden):
    scale = lax.rsqrt(jnp.mean(hidden * hidden, axis=-1, keepdims=True) + EPS)
    return (hidden * scale, scale)


def norm_back(grad_unit, unit, scale):
    return scale * (grad_unit - unit * jnp.mean(grad_unit * unit, axis=-1, keepdims=True))


def piece_tables(rows, at):
    both_rows = 2 * rows
    third = both_rows // 3
    side, k, i, half = np.meshgrid(range(2), range(3), range(8), range(2), indexing="ij")
    mask = np.vectorize(distance)(k, i)
    row = k * third + half * (third // 2)
    other, row = row // rows, row % rows
    side, other, row, mask = (jnp.asarray(v.reshape(-1), jnp.int32) for v in (side, other, row, mask))
    spread_at = (16 * (at["h"] ^ other) + 2 * (at["cube"] ^ mask) + (at["c"] ^ side)) * rows + row
    side, place, other = np.meshgrid(range(2), range(8), range(2), indexing="ij")
    side, place, other = (jnp.asarray(v.reshape(-1), jnp.int32) for v in (side, place, other))
    chunk_at = (16 * (at["h"] ^ other) + 2 * place + (at["c"] ^ side)) * rows
    k, i = np.meshgrid(range(3), range(8), indexing="ij")
    mask = jnp.asarray(np.vectorize(distance)(k, i).reshape(-1), jnp.int32)
    cube_at = (at["cube"] ^ mask) * both_rows + jnp.asarray(k.reshape(-1) * third, jnp.int32)
    return spread_at, chunk_at, cube_at


def weave_kernel(kinds, by_half, turn, *refs):
    place, sources, out, sems = refs[0], refs[1:-2], refs[-2], refs[-1]
    copies = []
    for src, (half_off, core_off) in zip(sources, kinds):
        core = place[1] ^ core_off
        count = out.shape[1]
        for part in range(src.shape[0] // count):
            half = part
            if by_half and half_off is not None:
                half = place[0] ^ part
            rows_part = src.at[part * count : (part + 1) * count]
            for j in range(2 if turn else 1):
                dst, src_part = out.at[half, :, core], rows_part
                if turn:
                    first = pl.multiple_of((j ^ place[1]) * turn, turn)
                    dst = out.at[half, :, core, :, pl.ds(first, turn)]
                    src_part = rows_part.at[:, :, j * turn : (j + 1) * turn]
                copies.append(pltpu.make_async_copy(src_part, dst, sems.at[len(copies)]))
    for copy in copies:
        copy.start()
    for copy in copies:
        copy.wait()


def weave(pieces, at, count, by_half, turn=0):
    rows, wide = pieces[0][0].shape[1:]
    place = jnp.stack([at["h"], at["c"]]).astype(jnp.int32)
    kinds = [piece[1:] for piece in pieces]
    arrays = [piece[0] for piece in pieces]
    return pl.pallas_call(
        lambda *refs: weave_kernel(kinds, by_half, turn, *refs),
        out_shape=jax.ShapeDtypeStruct((2 if by_half else 1, count, 2, rows, wide), arrays[0].dtype),
        in_specs=specs(1, 0) + [pl.BlockSpec(memory_space=pl.ANY)] * len(arrays),
        out_specs=specs(0, 1)[0],
        scratch_shapes=[pltpu.SemaphoreType.DMA((4 * len(arrays),))],
        compiler_params=pltpu.CompilerParams(vmem_limit_bytes=32 << 20),
        cost_estimate=pl.CostEstimate(flops=0, bytes_accessed=1 << 16, transcendentals=0),
    )(place, *arrays)


def small_line(segment_ids, padding_mask, attention_norm_gain, feed_gain, position_bias):
    codes = (segment_ids * 2 + padding_mask).astype(LOW)
    fields = [codes[0], codes[1], attention_norm_gain, feed_gain, position_bias]
    return jnp.concatenate([jnp.pad(field, (0, 128 - field.shape[0])) for field in fields])


def prepare_kernel(rows, place, lines, buckets, gains, query_more, key_more, diag, rng):
    count = lines.shape[0]
    fields = [lines[:, 128 * i : 128 * (i + 1)].astype(jnp.float32) for i in range(5)]
    codes = jnp.where(place[0] == 0, fields[0], fields[1])
    turned = codes.T
    lanes = lax.broadcasted_iota(jnp.int32, (rows, 2 * HEAD_DIM), 1) % HEAD_DIM
    for dev in range(count):
        code = turned[:rows, dev : dev + 1].astype(jnp.int32)
        segment = code >> 1
        key = jnp.where(lanes == segment, 1.0, 0.0)
        key = jnp.where((lanes == PAD_LANE) & ((code & 1) == 0), -FAR, key)
        query = jnp.where((lanes < PAD_LANE) & (lanes != segment), -FAR, 0.0)
        key_more[dev * rows : (dev + 1) * rows, :] = key.astype(key_more.dtype)
        query_more[dev * rows : (dev + 1) * rows, :] = query.astype(query_more.dtype)
        wide = gains.shape[1] // count
        for i in range(2):
            gains[i : i + 1, dev * wide : (dev + 1) * wide] = fields[2 + i][dev : dev + 1, :wide]
    heads = lax.broadcasted_iota(jnp.int32, fields[4].shape, 1)
    line = buckets[...]
    hot = lax.broadcasted_iota(jnp.int32, (BUCKETS, line.shape[1]), 0) == line
    for n in range(2):
        bias = jnp.sum(jnp.where(heads == 2 * place[1] + n, fields[4], 0.0), axis=1, keepdims=True)
        chosen = jnp.sum(jnp.where(hot, bias, 0.0), axis=0, keepdims=True)
        diag[n : n + 1, :] = jnp.where(line < 0, -FAR, chosen)
    real = lax.broadcasted_iota(jnp.int32, codes.shape, 1) < rows
    segments = codes.astype(jnp.int32) >> 1
    total = count * rows
    starts = [jnp.sum(jnp.where(real & (segments < s), 1.0, 0.0)).astype(jnp.int32) for s in range(1, PAD_LANE)]
    for i in range(total // BLK):
        first, last = i * BLK, i * BLK + BLK - 1
        low, high = jnp.int32(max(first - WINDOW + 1, 0)), jnp.int32(min(last + WINDOW, total))
        for start in starts:
            low = jnp.where(start <= first, jnp.maximum(low, start), low)
            high = jnp.where(start > last, jnp.minimum(high, start), high)
        rng[0, i] = low // BLK
        rng[1, i] = (high + BLK - 1) // BLK


def prepare(lines, buckets, near, lane, rows):
    count = lines.shape[0]
    place = jnp.stack([near, lane]).astype(jnp.int32)
    shape = jax.ShapeDtypeStruct
    total = count * rows
    gains, query_more, key_more, diag, rng = pl.pallas_call(
        lambda *refs: prepare_kernel(rows, *refs),
        out_shape=[
            shape((2, count * HEAD_DIM), F32),
            shape((total, 2 * HEAD_DIM), LOW),
            shape((total, 2 * HEAD_DIM), LOW),
            shape((2, LINE), F32),
            shape((2, total // BLK), jnp.int32),
        ],
        in_specs=specs(1, 2),
        out_specs=specs(0, 4) + specs(1, 0),
        compiler_params=pltpu.CompilerParams(vmem_limit_bytes=32 << 20),
        cost_estimate=pl.CostEstimate(flops=0, bytes_accessed=1 << 16, transcendentals=0),
    )(place, lines, buckets[None])
    return gains, (query_more, key_more), diag, rng


def prepare_wide(lines, buckets, near, lane, rows, halo, at):
    count = lines.shape[0]
    shard = 32 * HEAD_DIM // count
    gain_attn = lines[:, 256 : 256 + shard].reshape(-1).astype(F32)
    gain_feed = lines[:, 384 : 384 + shard].reshape(-1).astype(F32)
    bias_full = lines[:, 512 : 512 + BUCKETS * 32 // count].reshape(BUCKETS, -1).astype(F32)
    codes = pick(jnp.stack([lines[:, :rows], lines[:, 128 : 128 + rows]]).astype(jnp.int32), near)
    rim = jnp.full((halo,), -2, jnp.int32)
    codes = jnp.concatenate([rim, codes.reshape(-1), rim])
    length = 32 * rows
    codes = lax.dynamic_slice_in_dim(codes, at["b"] * length, length + 2 * halo)
    bias_here = pick(bias_full.reshape(BUCKETS, -1, 2), lane, 1)
    hot = buckets[None] == jnp.arange(BUCKETS, dtype=jnp.int32)[:, None]
    diag = jnp.sum(jnp.where(hot[:, None], bias_here[:, :, None], 0.0), axis=0)
    diag = jnp.where(buckets < 0, -FAR, diag)
    return gain_attn, gain_feed, barring_lanes(codes, halo), diag, query_ranges(codes >> 1, halo)


def in_order(pieces, table):
    count = table.shape[0]
    cut = pieces.reshape(count, -1, pieces.shape[-1])
    return jnp.take(cut, jnp.argsort(table), axis=0).reshape(pieces.shape)


def as_pieces(rows, table):
    count = table.shape[0]
    cut = rows.reshape(count, -1, rows.shape[-1])
    return jnp.take(cut, table // cut.shape[1], axis=0).reshape(rows.shape)


def with_sides(rows, halo):
    count = lax.axis_size("b")
    before = lax.ppermute(rows[-halo:], "b", [(i, i + 1) for i in range(count - 1)])
    after_it = lax.ppermute(rows[:halo], "b", [(i + 1, i) for i in range(count - 1)])
    return jnp.concatenate([before, rows, after_it], axis=0)


def add_sides(rows, halo):
    count = lax.axis_size("b")
    after_it = lax.ppermute(rows[:halo], "b", [(i + 1, i) for i in range(count - 1)])
    before = lax.ppermute(rows[-halo:], "b", [(i, i + 1) for i in range(count - 1)])
    mine = rows[halo:-halo]
    return mine.at[-halo:].add(after_it).at[:halo].add(before)


def local(
    layer_input,
    output_cotangent,
    segment_ids,
    padding_mask,
    bucket_table,
    attention_norm_gain,
    stacked_query_key_value,
    attention_out,
    position_bias,
    feed_gain,
    feed_in,
    feed_out,
):
    at = {name: lax.axis_index(name) for name in AXES}
    at["cube"] = 4 * at["p"] + 2 * at["q"] + at["r"]
    blocks = lax.axis_size("b")
    halves = 2 * blocks
    one_block = blocks == 1
    _, rows, width = layer_input.shape
    shard_rows = stacked_query_key_value.shape[0]
    hidden_shard = feed_out.shape[0]
    hidden_here = hidden_shard * halves * 2
    halo = 0 if one_block else WINDOW
    length = 32 * rows
    near = at["h"]
    far = 1 - near
    span = 2 * HEAD_DIM
    side = 3 * span
    lane = 8 * at["c"] + at["cube"]
    expand_order = tuple(range(2 * halves))
    project_order = (0, 2, 4, 1, 3, 5)

    lines = tell_all(small_line(segment_ids, padding_mask, attention_norm_gain, feed_gain, position_bias))
    x_near = pick(layer_input, near)
    x_far = swap(pick(layer_input, far), "h")
    cut = cut_columns(stacked_query_key_value, project_order, span)
    cut_in = cut_columns(feed_in, expand_order, 2 * hidden_shard)
    masked = output_cotangent * padding_mask[..., None].astype(LOW)
    x_far, lines, cut, cut_in, masked, attention_out, feed_out = fence(
        x_far, lines, cut, cut_in, masked, attention_out, feed_out
    )

    cut = exchange(cut)
    x_here = jnp.concatenate([x_near, x_far], axis=0)
    x_parts = gather_step(thirds(x_here), 0)
    buckets = bucket_line(bucket_table)
    spread_at, chunk_at, cube_at = piece_tables(rows, at)
    out_wire = swap(attention_out, "h") if one_block else ()
    x_parts, cut, buckets, spread_at, chunk_at, cube_at, masked, out_wire = fence(
        x_parts, cut, buckets, spread_at, chunk_at, cube_at, masked, out_wire
    )
    project_wire = wire_halves(cut)
    x_parts = gather_step(x_parts, 1)
    x_parts, project_wire, masked, feed_out = fence(x_parts, project_wire, masked, feed_out)
    x_parts = gather_step(x_parts, 2)
    res_far = swap(pick(masked, far), "h")
    if one_block:
        gains_both, barring, diag, rng = prepare(lines, buckets, near, lane, rows)
        gain_attn, gain_feed = gains_both[0], gains_both[1]
        project_pair = join_rows([cut, project_wire])[0]
    else:
        gain_attn, gain_feed, barring, diag, rng = prepare_wide(lines, buckets, near, lane, rows, halo, at)
        project_pair = project_wire.reshape(-1, shard_rows, 2 * side)
    if one_block:
        out_halves = both(attention_out, out_wire, at["h"], 0)
        out_halves = jnp.broadcast_to(out_halves, (8,) + out_halves.shape)
    else:
        out_halves = ()
    x_parts, gain_attn, gain_feed, barring, diag, rng, cut_in, project_pair, out_halves, res_far = fence(
        x_parts, gain_attn, gain_feed, barring, diag, rng, cut_in, project_pair, out_halves, res_far
    )

    project_core = swap(project_pair, "c")
    cut_in = exchange(cut_in)
    gathered = gathered_rows(x_parts)
    gathered, project_core = fence(gathered, project_core)
    gathered_unit, gathered_scale = normalize(gathered.astype(F32))
    normed_one = (gathered_unit * gain_attn).astype(LOW)
    if one_block:
        pieces = [(project_pair, 0, 0), (project_core, 0, 1)]
        project = weave(pieces, at, 8, True, side).reshape(width, -1)
    else:
        shape = (-1, 8, shard_rows, 2 * side)
        project = both(project_pair.reshape(shape), project_core.reshape(shape), at["c"], 2).reshape(width, -1)
        project = jnp.where(
            at["c"] == 0, project, jnp.concatenate([project[:, side:], project[:, :side]], axis=1)
        )
    projected = matmul(normed_one, project).astype(LOW)
    projected, cut_in, masked, out_halves = fence(projected, cut_in, masked, out_halves)
    out_chunks = exchange(out_halves) if one_block else ()
    own, other = projected[:, :side], swap(projected[:, side:], "c")
    res = jnp.concatenate([pick(masked, near), res_far], axis=0)
    res_parts = thirds(res)
    res_wires = gather_send(res_parts, 0)
    own, other = fence(own, other)

    expand_halves = gather_halves(cut_in)
    if one_block:
        tables = (spread_at, chunk_at, rng)
        tokens = (own, other)
    else:
        tables = (rng,)
        ordered = in_order(jnp.concatenate([own, other], axis=0), spread_at)
        sides = with_sides(ordered[:, span:], halo)
        tokens = (ordered[:, :span], sides[:, :span], sides[:, span:])
    extras = [(*barring, diag[n : n + 1]) for n in range(2)]
    first = attend_forward(one_block, halo, 0, tables, tokens, extras[0], ())
    *mixed, mixed_t, level = attend_forward(one_block, halo, 1, tables, tokens, extras[1], first[:1])
    saved = (first, (mixed_t, level))
    if not one_block:
        mixed = jnp.split(as_pieces(mixed[0], chunk_at), 2, axis=0)
    mixed, mixed_other, out_chunks, feed_out, expand_halves = fence(*mixed, out_chunks, feed_out, expand_halves)
    down_halves = gather_halves(feed_out)
    mixed_wire = swap(mixed_other, "c")
    mixed, mixed_wire, out_chunks, expand_halves = fence(mixed, mixed_wire, out_chunks, expand_halves)
    out_wire = swap(out_chunks, "c") if one_block else ()
    mixed = both(mixed, mixed_wire, at["c"], 1, joined=True)
    mixed = exchange(mixed.reshape(8, 2 * rows, 2 * span))
    expand_core = swap(expand_halves, "c")
    if one_block:
        pieces = [(out_chunks.reshape(16, HEAD_DIM, width), 0, 0), (out_wire.reshape(16, HEAD_DIM, width), 0, 1)]
        out_full = weave(pieces, at, 16, False).reshape(-1, width)
    else:
        out_full = fetch_out_wide(attention_out)
    mixed, out_full, expand_core, res_wires = fence(mixed, out_full, expand_core, res_wires)
    res_parts = gather_join(res_parts, res_wires)
    mixed_chunks = mixed.reshape(16 * rows, 2 * span)
    res_wires = gather_send(res_parts, 1)
    mixed = mixed.transpose(1, 0, 2).reshape(2 * rows, -1)
    tokens_here = x_here.astype(F32)
    hidden_one = tokens_here + matmul(mixed, out_full)

    unit_two, scale_two = normalize(hidden_one)
    normed_two = (unit_two * gain_feed).astype(LOW)
    normed_two, mixed = fence(normed_two, mixed)
    parts = gather_step(thirds(normed_two), 0)
    expand = weave_halves(expand_halves, expand_core, at).reshape(width, -1)
    parts, expand, down_halves = fence(parts, expand, down_halves)
    down_core = swap(down_halves, "c")
    parts = gather_step(parts, 1)
    parts, res_wires = fence(parts, res_wires)
    parts = gather_step(parts, 2)
    res_parts = gather_join(res_parts, res_wires)
    res_wires = gather_send(res_parts, 2)
    down = weave_halves(down_halves[:, None], down_core[:, None], at).reshape(hidden_here, width)
    parts, down = fence(parts, down)
    fed = gathered_rows(parts)
    gate_up = matmul(fed, expand)
    gate = gate_up[:, :hidden_here]
    upward = gate_up[:, hidden_here:]
    activated, gelu_pull = jax.vjp(gelu_tanh, gate)
    inner = (activated * upward).astype(LOW)

    inner, res_wires = fence(inner, res_wires)
    res_all = gathered_rows(gather_join(res_parts, res_wires))
    grad_res = res.astype(F32)
    grad_inner = matmul(res_all, down, NT)
    grad_gate = gelu_pull(grad_inner * upward)[0]
    grad_gate_up = jnp.concatenate([grad_gate, grad_inner * activated], axis=1).astype(LOW)
    grad_fed = matmul(grad_gate_up, expand, NT).astype(LOW)
    grad_fed, inner, res_all, fed = fence(grad_fed, inner, res_all, fed)
    parts = reduce_step(to_parts(grad_fed), 2)
    grad_down = matmul(inner, res_all, TN).astype(LOW).reshape(halves, 2, hidden_shard, width)
    parts, inner, grad_down = fence(parts, inner, grad_down)
    parts = reduce_step(parts, 1)
    down_wire = send_cores(grad_down, at, 1)
    final = matmul(by_rows_of_light(inner), down).astype(LOW)
    parts, final, down_wire = fence(parts, final, down_wire)
    parts = reduce_step(parts, 0)
    grad_down = add_cores(grad_down, down_wire, at, 1)
    parts, grad_down = fence(parts, grad_down)
    grad_normed_two = own_rows(parts)
    grad_hidden = grad_res + norm_back(grad_normed_two * gain_feed, unit_two, scale_two)

    grad_hidden_low = grad_hidden.astype(LOW)
    grad_mixed = matmul(grad_hidden_low, out_full, NT).astype(LOW)
    grad_mixed = grad_mixed.reshape(2 * rows, 8, 2 * span).transpose(1, 0, 2)
    grad_mixed, fed, grad_down = fence(grad_mixed, fed, grad_down)
    grad_down = scatter_halves(grad_down)
    grad_mixed = exchange(grad_mixed)
    grad_expand = matmul(fed, grad_gate_up, TN).astype(LOW).reshape(halves, 8, 2, shard_rows, -1)
    if one_block:
        mixed = by_light_distance(mixed_chunks, at)
    grad_mixed, final, mixed, grad_expand = fence(grad_mixed, final, mixed, grad_expand)
    final_parts = list(final.reshape(2, 8, rows, width))
    grad_mixed = grad_mixed.reshape(16 * rows, 2 * span)
    g_halves = grad_mixed[:, :span], grad_mixed[:, span:]
    g_own = jnp.where(at["c"] == 0, *g_halves)
    g_other = swap(jnp.where(at["c"] == 0, *g_halves[::-1]), "c")
    expand_wire = send_cores(grad_expand, at, 2)
    grad_out = matmul(mixed, grad_hidden_low, TN)
    if one_block:
        grad_out = grad_out.astype(LOW).reshape(2, 8, 2, HEAD_DIM, width)
        out_wire = send_cores(grad_out, at, 2)
    else:
        out_wire = ()
    g_own, g_other, expand_wire, out_wire = fence(g_own, g_other, expand_wire, out_wire)
    grad_expand = add_cores(grad_expand, expand_wire, at, 2)
    if one_block:
        grads = (g_own, g_other)
    else:
        grads = (in_order(jnp.concatenate([g_own, g_other], axis=0), chunk_at),)
    final_wires = light_send(final_parts)
    grad_expand = scatter_halves(grad_expand)
    *half_grads, d_diag_first = attend_backward(one_block, halo, 0, tables, tokens, extras[0], grads, saved[0], ())
    half_grads, final_wires, out_wire, grad_out = fence(half_grads, final_wires, out_wire, grad_out)
    final_parts = reduce_add(final_parts, final_wires)
    final_wires = light_send(final_parts)
    if one_block:
        out_parts = list(add_cores(grad_out, out_wire, at, 2))
        out_wires = light_send(out_parts)
    else:
        out_parts = out_wires = ()
    *d_all, d_diag = attend_backward(
        one_block, halo, 1, tables, tokens, extras[1], grads, saved[1], tuple(half_grads)
    )
    if one_block:
        d_own, d_other = d_all
    else:
        dq, dk, dv = d_all
        d_all = jnp.concatenate([dq, add_sides(dk, halo), add_sides(dv, halo)], axis=1)
        d_own, d_other = jnp.split(as_pieces(d_all.astype(LOW), spread_at), 2, axis=0)
    d_own, d_other, final_wires, out_wires, grad_expand = fence(d_own, d_other, final_wires, out_wires, grad_expand)
    d_other = swap(d_other, "c")
    final_parts = jnp.stack(reduce_add(final_parts, final_wires))
    final_wires = swap(final_parts[:, 1], "p")
    if one_block:
        out_parts = reduce_add(out_parts, out_wires)
        out_wires = light_send(out_parts)
    (d_other,) = fence(d_other)
    grad_projected = jnp.concatenate([d_own, d_other], axis=1)
    grad_normed_one = matmul(grad_projected, project, NT).astype(LOW)
    grad_normed_one, grad_projected, final_wires, out_wires, final_parts, out_parts, grad_down = fence(
        grad_normed_one, grad_projected, final_wires, out_wires, final_parts, out_parts, grad_down
    )

    def turn(got):
        return jnp.concatenate([got[..., side:], got[..., :side]], axis=-1)

    parts = reduce_step(to_parts(grad_normed_one), 2)
    grad_expand = exchange(grad_expand)
    grad_project = turned_matmul(normed_one, grad_projected).reshape(halves, 8, 2, shard_rows, -1)
    grad_gain_rows = scaled_sum(grad_normed_one, gathered, gathered_scale)
    grad_feed_gain = jnp.sum(grad_normed_two * unit_two, axis=0)
    sums = jnp.concatenate([d_diag_first, d_diag], axis=0)
    hot = buckets == jnp.arange(BUCKETS, dtype=jnp.int32)[:, None]
    sums = jnp.sum(jnp.where(hot[:, None], sums, 0.0), axis=2)
    lanes = (jnp.arange(16, dtype=jnp.int32) == lane).astype(F32)
    grad_position_bias = (sums[:, None, :] * lanes[:, None]).reshape(-1)
    count = lax.axis_size(AXES)
    gains = attention_norm_gain.shape[0]
    small = [grad_feed_gain, grad_gain_rows, grad_position_bias]
    small = jnp.concatenate([line.reshape(count, -1) for line in small], axis=1)
    final_near, final_far = (final_parts[:, 0].astype(F32) + final_wires.astype(F32)).astype(LOW).astype(F32)
    final_near = (hidden_one[:rows] + final_near).astype(LOW)
    final_far = (hidden_one[rows:] + final_far).astype(LOW)
    final_far = swap(final_far, "h")
    if one_block:
        out_parts = jnp.stack(reduce_add(out_parts, out_wires))
    parts, small, final_far, grad_project, out_parts, grad_expand = fence(
        parts, small, final_far, grad_project, out_parts, grad_expand
    )
    project_wire = send_cores(grad_project, at, 2)
    parts = reduce_step(parts, 1)
    grad_project = scatter_halves(add_cores(grad_project, turn(project_wire), at, 2))
    (parts,) = fence(parts)
    if one_block:
        out_wires = swap(out_parts[:, 1], "p")
    parts = reduce_step(parts, 0)
    parts, out_wires, grad_project, small = fence(parts, out_wires, grad_project, small)
    grad_project = exchange(grad_project)
    if one_block:
        out_halves = (out_parts[:, 0].astype(F32) + out_wires.astype(F32)).astype(LOW)
        out_wires = send_halves(out_halves, at)
    grad_part = own_rows(parts)
    unit_one, scale_one = normalize(tokens_here)
    token_grad = grad_hidden + norm_back(grad_part * gain_attn, unit_one, scale_one)
    token_grad = token_grad.astype(LOW)
    token_wire = swap(token_grad[rows:], "h")
    grad_project, small = fence(grad_project, small)
    small = jnp.sum(lax.all_to_all(small, AXES, 0, 0), axis=0)
    input_grad = both(token_grad[:rows], token_wire, near, 0)
    layer_output = both(final_near, final_far, near, 0)
    grad_expand = join_columns(grad_expand, expand_order, 2 * hidden_shard)
    grad_feed_gain = small[:gains]
    grad_attention_gain = small[gains : 2 * gains]
    grad_position_bias = small[2 * gains :]
    grad_out = add_halves(out_halves, out_wires, at) if one_block else grad_out_wide(grad_out)
    grad_down = grad_down.astype(F32)
    grad_project = jnp.where(at["c"] == 0, grad_project, turn(grad_project))
    grad_project = join_columns(grad_project, project_order, span)
    return (
        layer_output,
        input_grad,
        grad_attention_gain,
        grad_project,
        grad_out,
        grad_position_bias,
        grad_feed_gain,
        grad_expand,
        grad_down,
    )


def solution(mesh):
    wide = Mesh(mesh.devices.reshape(-1, 2, 2, 2, 2, 2), AXES)
    lead, tokens, rows = P(AXES), P(None, AXES), P(AXES, None)
    return jax.shard_map(
        local,
        mesh=wide,
        in_specs=(tokens, tokens, tokens, tokens, P(), lead, rows, rows, lead, lead, rows, rows),
        out_specs=(tokens, tokens, lead, rows, rows, lead, lead, rows, rows),
        check_vma=False,
    )
```

```python
import jax
import jax.numpy as jnp
import numpy as np
from jax import lax
from jax.experimental import pallas as pl
from jax.experimental.pallas import tpu as pltpu
from jax.sharding import Mesh, PartitionSpec as P

EPS = 1e-06
AXES = ("b", "h", "p", "q", "r", "c")
CUBE = ("p", "q", "r")
SWAP = [(0, 1), (1, 0)]
LOW = jnp.bfloat16
F32 = jnp.float32
HEAD_DIM = 64
BUCKETS = 32
WINDOW = 1024
BLK = 256
FAR = float(2**30)
NT = (((1,), (1,)), ((), ()))
NN = (((1,), (0,)), ((), ()))
DIAGS = 2 * (WINDOW // BLK) + 1
MID = WINDOW // BLK
PAD_LANE = 16
LINE = (DIAGS + 1) * BLK
FORWARD_COST = 1
BACKWARD_COST = 1


def dot(a, b, dims=NN):
    return lax.dot_general(a, b, dims, preferred_element_type=jnp.float32)


def fill_rows(table, own, other, rows, targets):
    pieces = own.shape[0] // rows
    for side, src in enumerate((own, other)):
        for i in range(pieces):
            at = pl.multiple_of(table[side * pieces + i], rows)
            col = 0
            for dst in targets:
                wide = dst.shape[-1]
                dst[pl.ds(at, rows), :] = src[i * rows : (i + 1) * rows, col : col + wide]
                col += wide


def drain_rows(table, src, own, other, rows, col):
    pieces = own.shape[0] // rows
    wide = src.shape[-1]
    for side, dst in enumerate((own, other)):
        for i in range(pieces):
            at = pl.multiple_of(table[side * pieces + i], rows)
            dst[i * rows : (i + 1) * rows, col : col + wide] = src[pl.ds(at, rows), :]


def make_tiles(line, tiles):
    strip = jnp.broadcast_to(line[...], (8, LINE))
    strip = pltpu.roll(strip, 0, 1, stride=1, stride_axis=0)
    for g in range(BLK // 8):
        moved = strip if g == 0 else pltpu.roll(strip, 8 * g, 1)
        for d in range(DIAGS):
            first = BLK * (DIAGS - d)
            tiles[d, 8 * g : 8 * g + 8, :] = moved[:, first : first + BLK]
    tiles[DIAGS + 1] = jnp.full((BLK, BLK), -FAR, jnp.float32)


def sum_tiles(tiles, line):
    total = jnp.zeros((8, LINE), jnp.float32)
    edge = jnp.zeros((8, BLK), jnp.float32)
    for g in range(BLK // 8):
        parts = [tiles[d, 8 * g : 8 * g + 8, :] for d in reversed(range(DIAGS))]
        strip = jnp.concatenate([edge] + parts, axis=1)
        total = total + (strip if g == 0 else pltpu.roll(strip, LINE - 8 * g, 1))
    out = total[0:1]
    for r in range(1, 8):
        out = out + pltpu.roll(total[r : r + 1], LINE - r, 1)
    line[...] = out


def make_own_tile(key_more, tiles, at):
    rows = lax.broadcasted_iota(jnp.int32, (BLK, BLK), 0)
    cols = lax.broadcasted_iota(jnp.int32, (BLK, BLK), 1)
    gone = key_more[pl.ds(at, BLK), PAD_LANE : PAD_LANE + 1].astype(jnp.float32)
    tiles[DIAGS] = tiles[MID] + jnp.where(rows == cols, 0.0, gone)


def half_of(n):
    lanes = lax.broadcasted_iota(jnp.int32, (BLK, 2 * HEAD_DIM), 1)
    return (lanes < HEAD_DIM) if n == 0 else (lanes >= HEAD_DIM)


def build_pairs(n, q, k, query_more, key_more, qx, kx):
    here = half_of(n)
    lanes = lax.broadcasted_iota(jnp.int32, (BLK, 2 * HEAD_DIM), 1)
    mark = jnp.where(lanes % HEAD_DIM == PAD_LANE, 1.0, 0.0).astype(jnp.bfloat16)

    def fill_q(i, _):
        rows = pl.ds(pl.multiple_of(i * BLK, BLK), BLK)
        more = query_more[rows, :]
        qx[0, rows, :] = jnp.where(here, q[rows, :], more)
        qx[1, rows, :] = jnp.where(here, q[rows, :], more + mark)
        return 0

    def fill_k(i, _):
        rows = pl.ds(pl.multiple_of(i * BLK, BLK), BLK)
        kx[rows, :] = jnp.where(here, k[rows, :], key_more[rows, :])
        return 0

    lax.fori_loop(0, q.shape[0] // BLK, fill_q, 0)
    lax.fori_loop(0, k.shape[0] // BLK, fill_k, 0)


def pair_of(j, first, end, here):
    out = []
    for m in range(2):
        block = first + 2 * j + m
        there = block < end
        block = jnp.minimum(block, end - 1)
        same = (there & (block == here)).astype(jnp.int32)
        away = block - here + MID
        tile = jnp.where(there, jnp.where(block == here, DIAGS, away), DIAGS + 1)
        out.append((pl.ds(pl.multiple_of(block * BLK, BLK), BLK), same, away, tile))
    return out


def forward_kernel(local, halo, n, *refs):
    if local:
        pos, pos_out, rng, own, other, query_more, key_more, diag, *refs = refs
        before, refs = refs[:n], refs[n:]
        outs, refs = (refs[:2], refs[2:]) if n else ((), refs)
        mixed_t, lse, q, k, v, qx, kx, vt, tiles, *joined = refs
        fill_rows(pos, own, other, own.shape[0] // 48, (q, k, v))
    else:
        rng, q, k, v, query_more, key_more, diag, *refs = refs
        before, refs = refs[:n], refs[n:]
        joined, refs = refs[:n], refs[n:]
        mixed_t, lse, qx, kx, vt, tiles = refs
    make_tiles(diag, tiles)
    build_pairs(n, q, k, query_more, key_more, qx, kx)
    cols = slice(n * HEAD_DIM, (n + 1) * HEAD_DIM)

    def turn(i, _):
        rows = pl.ds(pl.multiple_of(i * BLK, BLK), BLK)
        vt[:, rows] = v[rows, :].T[cols]
        return 0

    lax.fori_loop(0, v.shape[0] // BLK, turn, 0)

    def query_block(i, _):
        at = pl.multiple_of(i * BLK, BLK)
        rows = pl.ds(at, BLK)
        here = i + halo // BLK
        first, end = rng[0, i], rng[1, i]
        make_own_tile(key_more, tiles, pl.multiple_of(here * BLK, BLK))

        def key_blocks(j, carry):
            top, total, acc = carry
            both = pair_of(j, first, end, here)
            s = [
                dot(kx[span, :], qx[1 - same, rows, :], NT) + tiles[tile]
                for span, same, _, tile in both
            ]
            high = jnp.max(jnp.maximum(s[0], s[1]), axis=0, keepdims=True)
            high = jnp.maximum(top, high)
            p = [jnp.exp(part - high) for part in s]
            shrink = jnp.exp(top - high)
            total = total * shrink + jnp.sum(p[0] + p[1], axis=0, keepdims=True)
            acc = acc * shrink
            for part, (span, _, _, _) in zip(p, both):
                acc = acc + dot(vt[:, span], part.astype(jnp.bfloat16))
            return high, total, acc

        start = (
            jnp.full((1, BLK), -1e30, jnp.float32),
            jnp.zeros((1, BLK), jnp.float32),
            jnp.zeros((HEAD_DIM, BLK), jnp.float32),
        )
        top, total, acc = lax.fori_loop(0, (end - first + 1) // 2, key_blocks, start)
        mixed_t[:, rows] = acc / total
        lse[:, rows] = top + jnp.log(total)
        if n:
            whole = jnp.concatenate([before[0][:, rows], mixed_t[:, rows]], axis=0)
            joined[0][rows, :] = whole.T.astype(jnp.bfloat16)
        return 0

    lax.fori_loop(0, q.shape[0] // BLK, query_block, 0)
    if local and n:
        drain_rows(pos_out, joined[0], *outs, outs[0].shape[0] // 16, 0)


def backward_kernel(local, halo, n, *refs):
    if local:
        pos, pos_out, rng, own, other, query_more, key_more, diag, g_own, g_other, mixed_t, lse, *refs = refs
        before, refs = refs[: 3 * n], refs[3 * n :]
        outs, refs = refs[: 3 - n], refs[3 - n :]
        d_diag, q, k, v, g, qx, kx, vx, gx, kt, tiles, dk, dv, dtiles, *whole = refs
        fill_rows(pos, own, other, own.shape[0] // 48, (q, k, v))
        fill_rows(pos_out, g_own, g_other, g_own.shape[0] // 16, (g,))
        dq_out, dk_out, dv_out = whole if n else outs
    else:
        rng, q, k, v, query_more, key_more, diag, g, mixed_t, lse, *refs = refs
        before, refs = refs[: 3 * n], refs[3 * n :]
        dq_out, dk_out, dv_out, d_diag, qx, kx, vx, gx, kt, tiles, dk, dv, dtiles = refs
    make_tiles(diag, tiles)
    build_pairs(n, q, k, query_more, key_more, qx, kx)
    blank = jnp.zeros((BLK, 2 * HEAD_DIM), jnp.bfloat16)
    mine = half_of(n)
    cols = slice(n * HEAD_DIM, (n + 1) * HEAD_DIM)

    def store(out, slot, rows, part):
        part = part.astype(out.dtype)
        out[rows, :] = jnp.where(mine, part, before[slot][rows, :]) if n else part

    def turn(i, _):
        rows = pl.ds(pl.multiple_of(i * BLK, BLK), BLK)
        kt[:, rows] = k[rows, :].T[cols]
        vx[rows, :] = jnp.where(mine, v[rows, :], blank)
        dk[rows, :] = jnp.zeros((BLK, 2 * HEAD_DIM), jnp.float32)
        dv[rows, :] = jnp.zeros((BLK, 2 * HEAD_DIM), jnp.float32)
        return 0

    def spread_g(i, _):
        rows = pl.ds(pl.multiple_of(i * BLK, BLK), BLK)
        gx[rows, :] = jnp.where(mine, g[rows, :], blank)
        return 0

    lax.fori_loop(0, k.shape[0] // BLK, turn, 0)
    lax.fori_loop(0, q.shape[0] // BLK, spread_g, 0)
    for slot in range(DIAGS):
        dtiles[slot] = jnp.zeros((BLK, BLK), jnp.float32)

    def query_block(i, _):
        at = pl.multiple_of(i * BLK, BLK)
        rows = pl.ds(at, BLK)
        here = i + halo // BLK
        first, end = rng[0, i], rng[1, i]
        make_own_tile(key_more, tiles, pl.multiple_of(here * BLK, BLK))
        turned = g[rows, :].astype(jnp.float32).T[cols] * mixed_t[:, rows]
        delta = jnp.sum(turned, axis=0, keepdims=True)
        level = lse[:, rows]

        def key_blocks(j, acc):
            both = pair_of(j, first, end, here)
            s = [
                dot(kx[span, :], qx[1 - same, rows, :], NT) + tiles[tile]
                for span, same, _, tile in both
            ]
            dp = [dot(vx[span, :], gx[rows, :], NT) for span, _, _, _ in both]
            for m, (span, same, away, _) in enumerate(both):
                p = jnp.exp(s[m] - level)
                ds = (p * (dp[m] - delta)).astype(jnp.bfloat16)
                dtiles[away] += ds.astype(jnp.float32)
                dv[span, :] += dot(p.astype(jnp.bfloat16), gx[rows, :])
                dk[span, :] += dot(ds, qx[0, rows, :])
                acc = acc + dot(kt[:, span], ds)
            return acc

        zero = jnp.zeros((HEAD_DIM, BLK), jnp.float32)
        acc = lax.fori_loop(0, (end - first + 1) // 2, key_blocks, zero)
        empty = jnp.zeros((HEAD_DIM, BLK), jnp.float32)
        store(dq_out, 0, rows, jnp.concatenate([empty, acc] if n else [acc, empty], axis=0).T)
        return 0

    lax.fori_loop(0, q.shape[0] // BLK, query_block, 0)

    sum_tiles(dtiles, d_diag)

    def finish(i, _):
        rows = pl.ds(pl.multiple_of(i * BLK, BLK), BLK)
        store(dk_out, 1, rows, dk[rows, :])
        store(dv_out, 2, rows, dv[rows, :])
        return 0

    lax.fori_loop(0, k.shape[0] // BLK, finish, 0)
    if local and n:
        rows = own.shape[0] // 48
        for col, src in enumerate(whole):
            drain_rows(pos, src, *outs, rows, col * 2 * HEAD_DIM)


def specs(smem, vmem):
    return [pl.BlockSpec(memory_space=pltpu.SMEM)] * smem + [pl.BlockSpec(memory_space=pltpu.VMEM)] * vmem


def costs(length, times):
    return pl.CostEstimate(flops=length * times, bytes_accessed=1 << 16, transcendentals=0)


def attend_forward(local, halo, n, tables, tokens, extras, before):
    length, reach = extras[0].shape[0], extras[1].shape[0]
    both = 2 * HEAD_DIM
    shape = jax.ShapeDtypeStruct
    low = jnp.bfloat16
    outs, scratch, last = [], [], []
    if n:
        outs = [shape((length // 2, both), low)] * 2 if local else [shape((length, both), low)]
    outs = outs + [shape((HEAD_DIM, length), jnp.float32), shape((1, length), jnp.float32)]
    if local:
        scratch = [pltpu.VMEM((length, both), low)] + [pltpu.VMEM((reach, both), low)] * 2
        last = [pltpu.VMEM((length, both), low)] * n
    scratch = scratch + [
        pltpu.VMEM((2, length, both), low),
        pltpu.VMEM((reach, both), low),
        pltpu.VMEM((HEAD_DIM, reach), low),
        pltpu.VMEM((DIAGS + 2, BLK, BLK), jnp.float32),
    ]
    return pl.pallas_call(
        lambda *refs: forward_kernel(local, halo, n, *refs),
        out_shape=outs,
        in_specs=specs(len(tables), len(tokens) + len(extras) + len(before)),
        out_specs=specs(0, len(outs)),
        scratch_shapes=scratch + last,
        compiler_params=pltpu.CompilerParams(vmem_limit_bytes=56 << 20),
        cost_estimate=costs(length, FORWARD_COST),
    )(*tables, *tokens, *extras, *before)


def attend_backward(local, halo, n, tables, tokens, extras, grads, saved, before):
    length, reach = extras[0].shape[0], extras[1].shape[0]
    both = 2 * HEAD_DIM
    shape = jax.ShapeDtypeStruct
    low = jnp.bfloat16
    kind = low if local else jnp.float32
    d_diag = shape((1, LINE), jnp.float32)
    scratch, last = [], []
    if local and n:
        outs = [shape((length // 2, 3 * both), low)] * 2 + [d_diag]
    else:
        outs = [shape((length, both), kind)] + [shape((reach, both), kind)] * 2 + [d_diag]
    if local:
        scratch = [pltpu.VMEM((size, both), low) for size in (length, reach, reach, length)]
        last = [pltpu.VMEM((size, both), low) for size in (length, reach, reach)] * n
    scratch = scratch + [
        pltpu.VMEM((2, length, both), low),
        pltpu.VMEM((reach, both), low),
        pltpu.VMEM((reach, both), low),
        pltpu.VMEM((length, both), low),
        pltpu.VMEM((HEAD_DIM, reach), low),
        pltpu.VMEM((DIAGS + 2, BLK, BLK), jnp.float32),
        pltpu.VMEM((reach, both), jnp.float32),
        pltpu.VMEM((reach, both), jnp.float32),
        pltpu.VMEM((DIAGS, BLK, BLK), jnp.float32),
    ]
    operands = (*tokens, *extras, *grads, *saved, *before)
    return pl.pallas_call(
        lambda *refs: backward_kernel(local, halo, n, *refs),
        out_shape=outs,
        in_specs=specs(len(tables), len(operands)),
        out_specs=specs(0, len(outs)),
        scratch_shapes=scratch + last,
        compiler_params=pltpu.CompilerParams(vmem_limit_bytes=60 << 20),
        cost_estimate=costs(length, BACKWARD_COST),
    )(*tables, *operands)


def bucket_line(bucket_table):
    edge = jnp.full((2 * BLK,), -1, jnp.int32)
    wide = jnp.concatenate([edge, bucket_table, edge])[::-1]
    return wide[BLK - 1 : BLK - 1 + LINE]


def query_ranges(segments, halo):
    reach = segments.shape[0]
    first = halo + BLK * jnp.arange((reach - 2 * halo) // BLK, dtype=jnp.int32)
    last = first + BLK - 1
    cut = segments.reshape(-1, BLK)[halo // BLK : (reach - halo) // BLK]
    low = jnp.sum(segments[None, :] < cut[:, :1], axis=1)
    high = jnp.sum(segments[None, :] <= cut[:, -1:], axis=1)
    low = jnp.maximum(low, jnp.maximum(first - WINDOW + 1, 0))
    high = jnp.minimum(high, jnp.minimum(last + WINDOW, reach))
    return jnp.stack([low // BLK, (high + BLK - 1) // BLK]).astype(jnp.int32)


def barring_lanes(codes, halo):
    lanes = jnp.arange(2 * HEAD_DIM, dtype=jnp.int32) % HEAD_DIM
    segments = (codes >> 1)[:, None]
    key_more = jnp.where(lanes == segments, 1.0, 0.0)
    key_more = jnp.where((lanes == PAD_LANE) & ((codes & 1) == 0)[:, None], -FAR, key_more)
    mine = segments[halo : codes.shape[0] - halo]
    query_more = jnp.where((lanes < PAD_LANE) & (lanes != mine), -FAR, 0.0)
    return query_more.astype(jnp.bfloat16), key_more.astype(jnp.bfloat16)


def swap(value, axis):
    return lax.ppermute(value, axis, SWAP)


def pick(value, index, axis=0):
    return lax.dynamic_index_in_dim(value, index, axis, keepdims=False)


def both(mine, theirs, bit, axis, joined=False):
    put = jnp.concatenate if joined else jnp.stack
    return jnp.where(bit == 0, put([mine, theirs], axis), put([theirs, mine], axis))


def matmul(left, right, dims=NN):
    return lax.dot_general(left, right, dims, preferred_element_type=F32)


TN = (((0,), (0,)), ((), ()))


def fence(*values):
    return lax.optimization_barrier(values)


def cut_kernel(order, wide, src, out):
    for m in range(8):
        for j, o in enumerate(order):
            first = (o * 8 + m) * wide
            out[m, :, j * wide : (j + 1) * wide] = src[:, first : first + wide]


def cut_columns(matrix, order, wide):
    rows = matrix.shape[0]
    return pl.pallas_call(
        lambda src, out: cut_kernel(order, wide, src, out),
        out_shape=jax.ShapeDtypeStruct((8, rows, len(order) * wide), matrix.dtype),
        in_specs=specs(0, 1),
        out_specs=specs(0, 1)[0],
        compiler_params=pltpu.CompilerParams(vmem_limit_bytes=32 << 20),
        cost_estimate=pl.CostEstimate(flops=0, bytes_accessed=4 * matrix.size, transcendentals=0),
    )(matrix)


def join_kernel(order, wide, src, out):
    for m in range(8):
        for j, o in enumerate(order):
            first = (o * 8 + m) * wide
            part = src[m, :, j * wide : (j + 1) * wide]
            out[:, first : first + wide] = part.astype(jnp.float32)


def join_columns(chunks, order, wide):
    rows = chunks.shape[1]
    return pl.pallas_call(
        lambda src, out: join_kernel(order, wide, src, out),
        out_shape=jax.ShapeDtypeStruct((rows, len(order) * 8 * wide), F32),
        in_specs=specs(0, 1),
        out_specs=specs(0, 1)[0],
        compiler_params=pltpu.CompilerParams(vmem_limit_bytes=32 << 20),
        cost_estimate=pl.CostEstimate(flops=0, bytes_accessed=6 * chunks.size, transcendentals=0),
    )(chunks)


def distance(k, i):
    mask = 0
    for step in range(3):
        if i >> step & 1:
            mask |= 4 >> (k + step) % 3
    return mask


def join_kernel_rows(counts, *refs):
    total = sum(counts)
    sources, outs, sems = refs[:total], refs[total : total + len(counts)], refs[-1]
    copies = []
    for out, count in zip(outs, counts):
        at = 0
        for src in sources[len(copies) : len(copies) + count]:
            rows = src.shape[0]
            copies.append(pltpu.make_async_copy(src, out.at[pl.ds(at, rows)], sems.at[len(copies)]))
            at += rows
    for copy in copies:
        copy.start()
    for copy in copies:
        copy.wait()


def join_rows(*lists):
    counts = [len(pieces) for pieces in lists]
    pieces = [piece for listed in lists for piece in listed]
    shapes = [
        jax.ShapeDtypeStruct((sum(p.shape[0] for p in listed),) + listed[0].shape[1:], listed[0].dtype)
        for listed in lists
    ]
    outs = pl.pallas_call(
        lambda *refs: join_kernel_rows(counts, *refs),
        out_shape=shapes,
        in_specs=[pl.BlockSpec(memory_space=pl.ANY)] * len(pieces),
        out_specs=specs(0, len(lists)),
        scratch_shapes=[pltpu.SemaphoreType.DMA((len(pieces),))],
        compiler_params=pltpu.CompilerParams(vmem_limit_bytes=32 << 20),
        cost_estimate=pl.CostEstimate(
            flops=0, bytes_accessed=4 * sum(p.size for p in pieces), transcendentals=0
        ),
    )(*pieces)
    return list(outs)


def gather_send(parts, step):
    return [swap(parts[k], CUBE[(k + step) % 3]) for k in range(3)]


def gather_join(parts, wires):
    return join_rows(*([a, b] for a, b in zip(parts, wires)))


def gather_step(parts, step):
    return gather_join(parts, gather_send(parts, step))


def reduce_send(parts):
    half = parts[0].shape[0] // 2
    step = half.bit_length() - 1
    return [swap(parts[k][half:], CUBE[(k + step) % 3]) for k in range(3)]


def reduce_add(parts, wires):
    half = parts[0].shape[0] // 2
    return [(a[:half].astype(F32) + b.astype(F32)).astype(LOW) for a, b in zip(parts, wires)]


def reduce_step(parts, step):
    return reduce_add(parts, reduce_send(parts))


def thirds(rows):
    third = rows.shape[0] // 3
    return [rows[k * third : (k + 1) * third][None] for k in range(3)]


def gathered_rows(parts):
    return join_rows([part.reshape(-1, part.shape[-1]) for part in parts])[0]


def to_parts(rows):
    return list(rows.reshape(3, 8, -1, rows.shape[-1]))


def own_rows(parts):
    return jnp.concatenate([part[0] for part in parts], axis=0).astype(F32)


def exchange(chunks):
    return lax.all_to_all(chunks, CUBE, 0, 0)


def move_kernel(gather, rows, table, src, out):
    for n in range(src.shape[0] // rows):
        fixed = pl.ds(n * rows, rows)
        moved = pl.ds(pl.multiple_of(table[n], rows), rows)
        if gather:
            out[fixed, :] = src[moved, :]
        else:
            out[moved, :] = src[fixed, :]


def move_rows(table, src, gather):
    rows = src.shape[0] // table.shape[0]
    return pl.pallas_call(
        lambda *refs: move_kernel(gather, rows, *refs),
        out_shape=jax.ShapeDtypeStruct(src.shape, src.dtype),
        in_specs=specs(1, 1),
        out_specs=specs(0, 1)[0],
        compiler_params=pltpu.CompilerParams(vmem_limit_bytes=32 << 20),
        cost_estimate=pl.CostEstimate(flops=0, bytes_accessed=4 * src.size, transcendentals=0),
    )(table, src)


def tell_all(line):
    count = lax.axis_size(AXES)
    return lax.all_to_all(jnp.broadcast_to(line, (count,) + line.shape), AXES, 0, 0)


def wire_halves(shard):
    if lax.axis_size("b") == 1:
        return swap(shard, "h")
    return lax.all_gather(shard, ("b", "h"), axis=0)


def wire_halves_twice(shard):
    if lax.axis_size("b") == 1:
        return swap(shard[:4], "h"), swap(shard[4:], "h")
    return (wire_halves(shard),)


def turned_kernel(left, right, out):
    def block(i, _):
        cols = pl.ds(pl.multiple_of(i * BLK, BLK), BLK)
        out[cols, :] = dot(left[:, cols].T, right[...]).astype(out.dtype)
        return 0

    lax.fori_loop(0, left.shape[1] // BLK, block, 0)


def turned_matmul(left, right):
    return pl.pallas_call(
        turned_kernel,
        out_shape=jax.ShapeDtypeStruct((left.shape[1], right.shape[1]), LOW),
        in_specs=specs(0, 2),
        out_specs=specs(0, 1)[0],
        compiler_params=pltpu.CompilerParams(vmem_limit_bytes=40 << 20),
        cost_estimate=pl.CostEstimate(flops=0, bytes_accessed=1 << 16, transcendentals=0),
    )(left, right)


def scaled_kernel(left, right, scale, out):
    step = 64
    out[...] = jnp.zeros_like(out)

    def block(i, _):
        rows = pl.ds(pl.multiple_of(i * step, step), step)
        part = left[rows, :].astype(jnp.float32) * scale[rows, :] * right[rows, :].astype(jnp.float32)
        total = part[0:8]
        for j in range(1, step // 8):
            total = total + part[8 * j : 8 * j + 8]
        out[...] += total
        return 0

    lax.fori_loop(0, left.shape[0] // step, block, 0)


def scaled_sum(left, right, scale):
    eight = pl.pallas_call(
        scaled_kernel,
        out_shape=jax.ShapeDtypeStruct((8, left.shape[1]), F32),
        in_specs=specs(0, 3),
        out_specs=specs(0, 1)[0],
        compiler_params=pltpu.CompilerParams(vmem_limit_bytes=40 << 20),
        cost_estimate=pl.CostEstimate(flops=0, bytes_accessed=1 << 16, transcendentals=0),
    )(left, right, scale)
    return jnp.sum(eight, axis=0)


def light_distance(part, i):
    return (i & 1) * 4 | (i >> 1 & 1) * (2, 1)[part] | (i >> 2 & 1) * (1, 2)[part]


def light_send(parts):
    half = parts[0].shape[0] // 2
    axes = {4: ("r", "q"), 2: ("q", "r"), 1: ("p", "p")}[half]
    return [swap(part[half:], axis) for part, axis in zip(parts, axes)]


def by_rows_kernel(src, out):
    count = src.shape[0] // 48
    for part in range(2):
        for i in range(8):
            mask = light_distance(part, i)
            for j in range(3):
                row = 3 * part + j
                k = row // 2
                place = [distance(k, e) for e in range(8)].index(mask)
                first = ((k * 8 + place) * 2 + row % 2) * count
                at = ((part * 8 + i) * 3 + j) * count
                out[at : at + count, :] = src[first : first + count, :]


def by_rows_of_light(rows):
    return pl.pallas_call(
        by_rows_kernel,
        out_shape=jax.ShapeDtypeStruct(rows.shape, rows.dtype),
        in_specs=specs(0, 1),
        out_specs=specs(0, 1)[0],
        compiler_params=pltpu.CompilerParams(vmem_limit_bytes=32 << 20),
        cost_estimate=pl.CostEstimate(flops=0, bytes_accessed=1 << 16, transcendentals=0),
    )(rows)


def by_light_kernel(table, src, out):
    rows, wide = src.shape[0] // 8, src.shape[1] // 2
    for part in range(2):
        for i in range(8):
            at = pl.ds(pl.multiple_of((table[0] ^ light_distance(part, i)) * rows, rows), rows)
            to = (part * 8 + i) * wide
            out[:, to : to + wide] = src[at, part * wide : (part + 1) * wide]


def by_light_distance(chunks, at):
    tall, wide = chunks.shape
    return pl.pallas_call(
        by_light_kernel,
        out_shape=jax.ShapeDtypeStruct((tall // 8, wide * 8), chunks.dtype),
        in_specs=specs(1, 1),
        out_specs=specs(0, 1)[0],
        compiler_params=pltpu.CompilerParams(vmem_limit_bytes=32 << 20),
        cost_estimate=pl.CostEstimate(flops=0, bytes_accessed=1 << 16, transcendentals=0),
    )(at["cube"][None].astype(jnp.int32), chunks)


def gather_halves(shard):
    return lax.all_gather(shard, ("b", "h"), axis=0)


def scatter_halves(parts):
    return lax.psum_scatter(parts, ("b", "h"), scatter_dimension=0, tiled=False)


def weave_halves(halves, core, at):
    if lax.axis_size("b") > 1:
        return both(halves, core, at["c"], 2)
    count = halves.shape[1]
    halves, core = (v.reshape((-1,) + v.shape[2:]) for v in (halves, core))
    return weave([(halves, None, 0), (core, None, 1)], at, count, True)


def join_halves(shard, wire, at):
    return both(shard, wire, at["h"], 0) if lax.axis_size("b") == 1 else wire


def send_halves(parts, at):
    if lax.axis_size("b") == 1:
        return swap(pick(parts, 1 - at["h"]), "h")
    return lax.psum_scatter(parts.astype(F32), ("b", "h"), scatter_dimension=0, tiled=False)


def add_halves(parts, wire, at):
    if lax.axis_size("b") == 1:
        return pick(parts, at["h"]).astype(F32) + wire.astype(F32)
    return wire


def add_cores(grad, wire, at, axis):
    return (pick(grad, at["c"], axis).astype(F32) + wire.astype(F32)).astype(LOW)


def send_cores(grad, at, axis):
    return swap(pick(grad, 1 - at["c"], axis), "c")


def fetch_out_wide(shard):
    whole = lax.all_gather(shard, AXES, axis=0, tiled=True)
    whole = whole.reshape(2, 8, 2, HEAD_DIM, -1).transpose(1, 0, 2, 3, 4)
    return whole.reshape(-1, whole.shape[-1])


def grad_out_wide(grad):
    grad = grad.reshape(8, 2, 2, HEAD_DIM, -1).transpose(1, 0, 2, 3, 4)
    return lax.psum_scatter(grad.reshape(-1, grad.shape[-1]), AXES, scatter_dimension=0, tiled=True)


def gelu_tanh(value):
    return (
        0.5
        * value
        * (1.0 + jnp.tanh(0.7978845608028654 * (value + 0.044715 * value * value * value)))
    )


def normalize(hidden):
    scale = lax.rsqrt(jnp.mean(hidden * hidden, axis=-1, keepdims=True) + EPS)
    return (hidden * scale, scale)


def norm_back(grad_unit, unit, scale):
    return scale * (grad_unit - unit * jnp.mean(grad_unit * unit, axis=-1, keepdims=True))


def piece_tables(rows, at):
    both_rows = 2 * rows
    third = both_rows // 3
    side, k, i, half = np.meshgrid(range(2), range(3), range(8), range(2), indexing="ij")
    mask = np.vectorize(distance)(k, i)
    row = k * third + half * (third // 2)
    other, row = row // rows, row % rows
    side, other, row, mask = (jnp.asarray(v.reshape(-1), jnp.int32) for v in (side, other, row, mask))
    spread_at = (16 * (at["h"] ^ other) + 2 * (at["cube"] ^ mask) + (at["c"] ^ side)) * rows + row
    side, place, other = np.meshgrid(range(2), range(8), range(2), indexing="ij")
    side, place, other = (jnp.asarray(v.reshape(-1), jnp.int32) for v in (side, place, other))
    chunk_at = (16 * (at["h"] ^ other) + 2 * place + (at["c"] ^ side)) * rows
    k, i = np.meshgrid(range(3), range(8), indexing="ij")
    mask = jnp.asarray(np.vectorize(distance)(k, i).reshape(-1), jnp.int32)
    cube_at = (at["cube"] ^ mask) * both_rows + jnp.asarray(k.reshape(-1) * third, jnp.int32)
    return spread_at, chunk_at, cube_at


def weave_kernel(kinds, by_half, turn, *refs):
    place, sources, out, sems = refs[0], refs[1:-2], refs[-2], refs[-1]
    copies = []
    for src, (half_off, core_off) in zip(sources, kinds):
        core = place[1] ^ core_off
        count = out.shape[1]
        for part in range(src.shape[0] // count):
            half = part
            if by_half and half_off is not None:
                half = place[0] ^ part
            rows_part = src.at[part * count : (part + 1) * count]
            for j in range(2 if turn else 1):
                dst, src_part = out.at[half, :, core], rows_part
                if turn:
                    first = pl.multiple_of((j ^ place[1]) * turn, turn)
                    dst = out.at[half, :, core, :, pl.ds(first, turn)]
                    src_part = rows_part.at[:, :, j * turn : (j + 1) * turn]
                copies.append(pltpu.make_async_copy(src_part, dst, sems.at[len(copies)]))
    for copy in copies:
        copy.start()
    for copy in copies:
        copy.wait()


def weave(pieces, at, count, by_half, turn=0):
    rows, wide = pieces[0][0].shape[1:]
    place = jnp.stack([at["h"], at["c"]]).astype(jnp.int32)
    kinds = [piece[1:] for piece in pieces]
    arrays = [piece[0] for piece in pieces]
    return pl.pallas_call(
        lambda *refs: weave_kernel(kinds, by_half, turn, *refs),
        out_shape=jax.ShapeDtypeStruct((2 if by_half else 1, count, 2, rows, wide), arrays[0].dtype),
        in_specs=specs(1, 0) + [pl.BlockSpec(memory_space=pl.ANY)] * len(arrays),
        out_specs=specs(0, 1)[0],
        scratch_shapes=[pltpu.SemaphoreType.DMA((4 * len(arrays),))],
        compiler_params=pltpu.CompilerParams(vmem_limit_bytes=32 << 20),
        cost_estimate=pl.CostEstimate(flops=0, bytes_accessed=1 << 16, transcendentals=0),
    )(place, *arrays)


def small_line(segment_ids, padding_mask, attention_norm_gain, feed_gain, position_bias):
    codes = (segment_ids * 2 + padding_mask).astype(LOW)
    fields = [codes[0], codes[1], attention_norm_gain, feed_gain, position_bias]
    return jnp.concatenate([jnp.pad(field, (0, 128 - field.shape[0])) for field in fields])


def prepare_kernel(rows, place, lines, buckets, gains, query_more, key_more, diag, rng):
    count = lines.shape[0]
    fields = [lines[:, 128 * i : 128 * (i + 1)].astype(jnp.float32) for i in range(5)]
    codes = jnp.where(place[0] == 0, fields[0], fields[1])
    turned = codes.T
    lanes = lax.broadcasted_iota(jnp.int32, (rows, 2 * HEAD_DIM), 1) % HEAD_DIM
    for dev in range(count):
        code = turned[:rows, dev : dev + 1].astype(jnp.int32)
        segment = code >> 1
        key = jnp.where(lanes == segment, 1.0, 0.0)
        key = jnp.where((lanes == PAD_LANE) & ((code & 1) == 0), -FAR, key)
        query = jnp.where((lanes < PAD_LANE) & (lanes != segment), -FAR, 0.0)
        key_more[dev * rows : (dev + 1) * rows, :] = key.astype(key_more.dtype)
        query_more[dev * rows : (dev + 1) * rows, :] = query.astype(query_more.dtype)
        wide = gains.shape[1] // count
        for i in range(2):
            gains[i : i + 1, dev * wide : (dev + 1) * wide] = fields[2 + i][dev : dev + 1, :wide]
    heads = lax.broadcasted_iota(jnp.int32, fields[4].shape, 1)
    line = buckets[...]
    hot = lax.broadcasted_iota(jnp.int32, (BUCKETS, line.shape[1]), 0) == line
    for n in range(2):
        bias = jnp.sum(jnp.where(heads == 2 * place[1] + n, fields[4], 0.0), axis=1, keepdims=True)
        chosen = jnp.sum(jnp.where(hot, bias, 0.0), axis=0, keepdims=True)
        diag[n : n + 1, :] = jnp.where(line < 0, -FAR, chosen)
    real = lax.broadcasted_iota(jnp.int32, codes.shape, 1) < rows
    segments = codes.astype(jnp.int32) >> 1
    total = count * rows
    starts = [jnp.sum(jnp.where(real & (segments < s), 1.0, 0.0)).astype(jnp.int32) for s in range(1, PAD_LANE)]
    for i in range(total // BLK):
        first, last = i * BLK, i * BLK + BLK - 1
        low, high = jnp.int32(max(first - WINDOW + 1, 0)), jnp.int32(min(last + WINDOW, total))
        for start in starts:
            low = jnp.where(start <= first, jnp.maximum(low, start), low)
            high = jnp.where(start > last, jnp.minimum(high, start), high)
        rng[0, i] = low // BLK
        rng[1, i] = (high + BLK - 1) // BLK


def prepare(lines, buckets, near, lane, rows):
    count = lines.shape[0]
    place = jnp.stack([near, lane]).astype(jnp.int32)
    shape = jax.ShapeDtypeStruct
    total = count * rows
    gains, query_more, key_more, diag, rng = pl.pallas_call(
        lambda *refs: prepare_kernel(rows, *refs),
        out_shape=[
            shape((2, count * HEAD_DIM), F32),
            shape((total, 2 * HEAD_DIM), LOW),
            shape((total, 2 * HEAD_DIM), LOW),
            shape((2, LINE), F32),
            shape((2, total // BLK), jnp.int32),
        ],
        in_specs=specs(1, 2),
        out_specs=specs(0, 4) + specs(1, 0),
        compiler_params=pltpu.CompilerParams(vmem_limit_bytes=32 << 20),
        cost_estimate=pl.CostEstimate(flops=0, bytes_accessed=1 << 16, transcendentals=0),
    )(place, lines, buckets[None])
    return gains, (query_more, key_more), diag, rng


def prepare_wide(lines, buckets, near, lane, rows, halo, at):
    count = lines.shape[0]
    shard = 32 * HEAD_DIM // count
    gain_attn = lines[:, 256 : 256 + shard].reshape(-1).astype(F32)
    gain_feed = lines[:, 384 : 384 + shard].reshape(-1).astype(F32)
    bias_full = lines[:, 512 : 512 + BUCKETS * 32 // count].reshape(BUCKETS, -1).astype(F32)
    codes = pick(jnp.stack([lines[:, :rows], lines[:, 128 : 128 + rows]]).astype(jnp.int32), near)
    rim = jnp.full((halo,), -2, jnp.int32)
    codes = jnp.concatenate([rim, codes.reshape(-1), rim])
    length = 32 * rows
    codes = lax.dynamic_slice_in_dim(codes, at["b"] * length, length + 2 * halo)
    bias_here = pick(bias_full.reshape(BUCKETS, -1, 2), lane, 1)
    hot = buckets[None] == jnp.arange(BUCKETS, dtype=jnp.int32)[:, None]
    diag = jnp.sum(jnp.where(hot[:, None], bias_here[:, :, None], 0.0), axis=0)
    diag = jnp.where(buckets < 0, -FAR, diag)
    return gain_attn, gain_feed, barring_lanes(codes, halo), diag, query_ranges(codes >> 1, halo)


def in_order(pieces, table):
    count = table.shape[0]
    cut = pieces.reshape(count, -1, pieces.shape[-1])
    return jnp.take(cut, jnp.argsort(table), axis=0).reshape(pieces.shape)


def as_pieces(rows, table):
    count = table.shape[0]
    cut = rows.reshape(count, -1, rows.shape[-1])
    return jnp.take(cut, table // cut.shape[1], axis=0).reshape(rows.shape)


def with_sides(rows, halo):
    count = lax.axis_size("b")
    before = lax.ppermute(rows[-halo:], "b", [(i, i + 1) for i in range(count - 1)])
    after_it = lax.ppermute(rows[:halo], "b", [(i + 1, i) for i in range(count - 1)])
    return jnp.concatenate([before, rows, after_it], axis=0)


def add_sides(rows, halo):
    count = lax.axis_size("b")
    after_it = lax.ppermute(rows[:halo], "b", [(i + 1, i) for i in range(count - 1)])
    before = lax.ppermute(rows[-halo:], "b", [(i, i + 1) for i in range(count - 1)])
    mine = rows[halo:-halo]
    return mine.at[-halo:].add(after_it).at[:halo].add(before)


def local(
    layer_input,
    output_cotangent,
    segment_ids,
    padding_mask,
    bucket_table,
    attention_norm_gain,
    stacked_query_key_value,
    attention_out,
    position_bias,
    feed_gain,
    feed_in,
    feed_out,
):
    at = {name: lax.axis_index(name) for name in AXES}
    at["cube"] = 4 * at["p"] + 2 * at["q"] + at["r"]
    blocks = lax.axis_size("b")
    halves = 2 * blocks
    one_block = blocks == 1
    _, rows, width = layer_input.shape
    shard_rows = stacked_query_key_value.shape[0]
    hidden_shard = feed_out.shape[0]
    hidden_here = hidden_shard * halves * 2
    halo = 0 if one_block else WINDOW
    length = 32 * rows
    near = at["h"]
    far = 1 - near
    span = 2 * HEAD_DIM
    side = 3 * span
    lane = 8 * at["c"] + at["cube"]
    expand_order = tuple(range(2 * halves))
    project_order = (0, 2, 4, 1, 3, 5)

    lines = tell_all(small_line(segment_ids, padding_mask, attention_norm_gain, feed_gain, position_bias))
    x_near = pick(layer_input, near)
    x_far = swap(pick(layer_input, far), "h")
    cut = cut_columns(stacked_query_key_value, project_order, span)
    cut_in = cut_columns(feed_in, expand_order, 2 * hidden_shard)
    masked = output_cotangent * padding_mask[..., None].astype(LOW)
    x_far, lines, cut, cut_in, masked, attention_out, feed_out = fence(
        x_far, lines, cut, cut_in, masked, attention_out, feed_out
    )

    cut = exchange(cut)
    x_here = jnp.concatenate([x_near, x_far], axis=0)
    x_parts = gather_step(thirds(x_here), 0)
    buckets = bucket_line(bucket_table)
    spread_at, chunk_at, cube_at = piece_tables(rows, at)
    out_wire = swap(attention_out, "h") if one_block else ()
    x_parts, cut, buckets, spread_at, chunk_at, cube_at, masked, out_wire = fence(
        x_parts, cut, buckets, spread_at, chunk_at, cube_at, masked, out_wire
    )
    project_wire = wire_halves(cut)
    x_parts = gather_step(x_parts, 1)
    x_parts, project_wire, masked, feed_out = fence(x_parts, project_wire, masked, feed_out)
    x_parts = gather_step(x_parts, 2)
    res_far = swap(pick(masked, far), "h")
    if one_block:
        gains_both, barring, diag, rng = prepare(lines, buckets, near, lane, rows)
        gain_attn, gain_feed = gains_both[0], gains_both[1]
        project_pair = join_rows([cut, project_wire])[0]
    else:
        gain_attn, gain_feed, barring, diag, rng = prepare_wide(lines, buckets, near, lane, rows, halo, at)
        project_pair = project_wire.reshape(-1, shard_rows, 2 * side)
    if one_block:
        out_halves = both(attention_out, out_wire, at["h"], 0)
        out_halves = jnp.broadcast_to(out_halves, (8,) + out_halves.shape)
    else:
        out_halves = ()
    x_parts, gain_attn, gain_feed, barring, diag, rng, cut_in, project_pair, out_halves, res_far = fence(
        x_parts, gain_attn, gain_feed, barring, diag, rng, cut_in, project_pair, out_halves, res_far
    )

    project_core = swap(project_pair, "c")
    cut_in = exchange(cut_in)
    gathered = gathered_rows(x_parts)
    gathered, project_core = fence(gathered, project_core)
    gathered_unit, gathered_scale = normalize(gathered.astype(F32))
    normed_one = (gathered_unit * gain_attn).astype(LOW)
    if one_block:
        pieces = [(project_pair, 0, 0), (project_core, 0, 1)]
        project = weave(pieces, at, 8, True, side).reshape(width, -1)
    else:
        shape = (-1, 8, shard_rows, 2 * side)
        project = both(project_pair.reshape(shape), project_core.reshape(shape), at["c"], 2).reshape(width, -1)
        project = jnp.where(
            at["c"] == 0, project, jnp.concatenate([project[:, side:], project[:, :side]], axis=1)
        )
    projected = matmul(normed_one, project).astype(LOW)
    projected, cut_in, masked, out_halves = fence(projected, cut_in, masked, out_halves)
    out_chunks = exchange(out_halves) if one_block else ()
    own, other = projected[:, :side], swap(projected[:, side:], "c")
    res = jnp.concatenate([pick(masked, near), res_far], axis=0)
    res_parts = thirds(res)
    res_wires = gather_send(res_parts, 0)
    own, other = fence(own, other)

    expand_halves = gather_halves(cut_in)
    if one_block:
        tables = (spread_at, chunk_at, rng)
        tokens = (own, other)
    else:
        tables = (rng,)
        ordered = in_order(jnp.concatenate([own, other], axis=0), spread_at)
        sides = with_sides(ordered[:, span:], halo)
        tokens = (ordered[:, :span], sides[:, :span], sides[:, span:])
    extras = [(*barring, diag[n : n + 1]) for n in range(2)]
    first = attend_forward(one_block, halo, 0, tables, tokens, extras[0], ())
    *mixed, mixed_t, level = attend_forward(one_block, halo, 1, tables, tokens, extras[1], first[:1])
    saved = (first, (mixed_t, level))
    if not one_block:
        mixed = jnp.split(as_pieces(mixed[0], chunk_at), 2, axis=0)
    mixed, mixed_other, out_chunks, feed_out, expand_halves = fence(*mixed, out_chunks, feed_out, expand_halves)
    down_halves = gather_halves(feed_out)
    mixed_wire = swap(mixed_other, "c")
    mixed, mixed_wire, out_chunks, expand_halves = fence(mixed, mixed_wire, out_chunks, expand_halves)
    out_wire = swap(out_chunks, "c") if one_block else ()
    mixed = both(mixed, mixed_wire, at["c"], 1, joined=True)
    mixed = exchange(mixed.reshape(8, 2 * rows, 2 * span))
    expand_core = swap(expand_halves, "c")
    if one_block:
        pieces = [(out_chunks.reshape(16, HEAD_DIM, width), 0, 0), (out_wire.reshape(16, HEAD_DIM, width), 0, 1)]
        out_full = weave(pieces, at, 16, False).reshape(-1, width)
    else:
        out_full = fetch_out_wide(attention_out)
    mixed, out_full, expand_core, res_wires = fence(mixed, out_full, expand_core, res_wires)
    res_parts = gather_join(res_parts, res_wires)
    mixed_chunks = mixed.reshape(16 * rows, 2 * span)
    res_wires = gather_send(res_parts, 1)
    mixed = mixed.transpose(1, 0, 2).reshape(2 * rows, -1)
    tokens_here = x_here.astype(F32)
    hidden_one = tokens_here + matmul(mixed, out_full)

    unit_two, scale_two = normalize(hidden_one)
    normed_two = (unit_two * gain_feed).astype(LOW)
    normed_two, mixed = fence(normed_two, mixed)
    parts = gather_step(thirds(normed_two), 0)
    expand = weave_halves(expand_halves, expand_core, at).reshape(width, -1)
    parts, expand, down_halves = fence(parts, expand, down_halves)
    down_core = swap(down_halves, "c")
    parts = gather_step(parts, 1)
    parts, res_wires = fence(parts, res_wires)
    parts = gather_step(parts, 2)
    res_parts = gather_join(res_parts, res_wires)
    res_wires = gather_send(res_parts, 2)
    down = weave_halves(down_halves[:, None], down_core[:, None], at).reshape(hidden_here, width)
    parts, down = fence(parts, down)
    fed = gathered_rows(parts)
    gate_up = matmul(fed, expand)
    gate = gate_up[:, :hidden_here]
    upward = gate_up[:, hidden_here:]
    activated, gelu_pull = jax.vjp(gelu_tanh, gate)
    inner = (activated * upward).astype(LOW)

    inner, res_wires = fence(inner, res_wires)
    res_all = gathered_rows(gather_join(res_parts, res_wires))
    grad_res = res.astype(F32)
    grad_inner = matmul(res_all, down, NT)
    grad_gate = gelu_pull(grad_inner * upward)[0]
    grad_gate_up = jnp.concatenate([grad_gate, grad_inner * activated], axis=1).astype(LOW)
    grad_fed = matmul(grad_gate_up, expand, NT).astype(LOW)
    grad_fed, inner, res_all, fed = fence(grad_fed, inner, res_all, fed)
    parts = reduce_step(to_parts(grad_fed), 2)
    grad_down = matmul(inner, res_all, TN).astype(LOW).reshape(halves, 2, hidden_shard, width)
    parts, inner, grad_down = fence(parts, inner, grad_down)
    parts = reduce_step(parts, 1)
    down_wire = send_cores(grad_down, at, 1)
    final = matmul(by_rows_of_light(inner), down).astype(LOW)
    parts, final, down_wire = fence(parts, final, down_wire)
    parts = reduce_step(parts, 0)
    grad_down = add_cores(grad_down, down_wire, at, 1)
    parts, grad_down = fence(parts, grad_down)
    grad_normed_two = own_rows(parts)
    grad_hidden = grad_res + norm_back(grad_normed_two * gain_feed, unit_two, scale_two)

    grad_hidden_low = grad_hidden.astype(LOW)
    grad_mixed = matmul(grad_hidden_low, out_full, NT).astype(LOW)
    grad_mixed = grad_mixed.reshape(2 * rows, 8, 2 * span).transpose(1, 0, 2)
    grad_mixed, fed, grad_down = fence(grad_mixed, fed, grad_down)
    grad_down = scatter_halves(grad_down)
    grad_mixed = exchange(grad_mixed)
    grad_expand = turned_matmul(fed, grad_gate_up).reshape(halves, 8, 2, shard_rows, -1)
    if one_block:
        mixed = by_light_distance(mixed_chunks, at)
    grad_mixed, final, mixed, grad_expand = fence(grad_mixed, final, mixed, grad_expand)
    final_parts = list(final.reshape(2, 8, rows, width))
    grad_mixed = grad_mixed.reshape(16 * rows, 2 * span)
    g_halves = grad_mixed[:, :span], grad_mixed[:, span:]
    g_own = jnp.where(at["c"] == 0, *g_halves)
    g_other = swap(jnp.where(at["c"] == 0, *g_halves[::-1]), "c")
    expand_wire = send_cores(grad_expand, at, 2)
    grad_out = matmul(mixed, grad_hidden_low, TN)
    if one_block:
        grad_out = grad_out.astype(LOW).reshape(2, 8, 2, HEAD_DIM, width)
        out_wire = send_cores(grad_out, at, 2)
    else:
        out_wire = ()
    g_own, g_other, expand_wire, out_wire = fence(g_own, g_other, expand_wire, out_wire)
    grad_expand = add_cores(grad_expand, expand_wire, at, 2)
    if one_block:
        grads = (g_own, g_other)
    else:
        grads = (in_order(jnp.concatenate([g_own, g_other], axis=0), chunk_at),)
    final_wires = light_send(final_parts)
    grad_expand = scatter_halves(grad_expand)
    *half_grads, d_diag_first = attend_backward(one_block, halo, 0, tables, tokens, extras[0], grads, saved[0], ())
    half_grads, final_wires, out_wire, grad_out = fence(half_grads, final_wires, out_wire, grad_out)
    final_parts = reduce_add(final_parts, final_wires)
    final_wires = light_send(final_parts)
    if one_block:
        out_parts = list(add_cores(grad_out, out_wire, at, 2))
        out_wires = light_send(out_parts)
    else:
        out_parts = out_wires = ()
    *d_all, d_diag = attend_backward(
        one_block, halo, 1, tables, tokens, extras[1], grads, saved[1], tuple(half_grads)
    )
    if one_block:
        d_own, d_other = d_all
    else:
        dq, dk, dv = d_all
        d_all = jnp.concatenate([dq, add_sides(dk, halo), add_sides(dv, halo)], axis=1)
        d_own, d_other = jnp.split(as_pieces(d_all.astype(LOW), spread_at), 2, axis=0)
    d_own, d_other, final_wires, out_wires, grad_expand = fence(d_own, d_other, final_wires, out_wires, grad_expand)
    d_other = swap(d_other, "c")
    final_parts = jnp.stack(reduce_add(final_parts, final_wires))
    final_wires = swap(final_parts[:, 1], "p")
    if one_block:
        out_parts = reduce_add(out_parts, out_wires)
        out_wires = light_send(out_parts)
    (d_other,) = fence(d_other)
    grad_projected = jnp.concatenate([d_own, d_other], axis=1)
    grad_normed_one = matmul(grad_projected, project, NT).astype(LOW)
    grad_normed_one, grad_projected, final_wires, out_wires, final_parts, out_parts, grad_down = fence(
        grad_normed_one, grad_projected, final_wires, out_wires, final_parts, out_parts, grad_down
    )

    def turn(got):
        return jnp.concatenate([got[..., side:], got[..., :side]], axis=-1)

    parts = reduce_step(to_parts(grad_normed_one), 2)
    grad_expand = exchange(grad_expand)
    grad_project = turned_matmul(normed_one, grad_projected).reshape(halves, 8, 2, shard_rows, -1)
    grad_gain_rows = scaled_sum(grad_normed_one, gathered, gathered_scale)
    grad_feed_gain = jnp.sum(grad_normed_two * unit_two, axis=0)
    sums = jnp.concatenate([d_diag_first, d_diag], axis=0)
    hot = buckets == jnp.arange(BUCKETS, dtype=jnp.int32)[:, None]
    sums = jnp.sum(jnp.where(hot[:, None], sums, 0.0), axis=2)
    lanes = (jnp.arange(16, dtype=jnp.int32) == lane).astype(F32)
    grad_position_bias = (sums[:, None, :] * lanes[:, None]).reshape(-1)
    count = lax.axis_size(AXES)
    gains = attention_norm_gain.shape[0]
    small = [grad_feed_gain, grad_gain_rows, grad_position_bias]
    small = jnp.concatenate([line.reshape(count, -1) for line in small], axis=1)
    final_near, final_far = (final_parts[:, 0].astype(F32) + final_wires.astype(F32)).astype(LOW).astype(F32)
    final_near = (hidden_one[:rows] + final_near).astype(LOW)
    final_far = (hidden_one[rows:] + final_far).astype(LOW)
    final_far = swap(final_far, "h")
    if one_block:
        out_parts = jnp.stack(reduce_add(out_parts, out_wires))
    parts, small, final_far, grad_project, out_parts, grad_expand = fence(
        parts, small, final_far, grad_project, out_parts, grad_expand
    )
    project_wire = send_cores(grad_project, at, 2)
    parts = reduce_step(parts, 1)
    grad_project = scatter_halves(add_cores(grad_project, turn(project_wire), at, 2))
    (parts,) = fence(parts)
    if one_block:
        out_wires = swap(out_parts[:, 1], "p")
    parts = reduce_step(parts, 0)
    parts, out_wires, grad_project, small = fence(parts, out_wires, grad_project, small)
    grad_project = exchange(grad_project)
    if one_block:
        out_halves = (out_parts[:, 0].astype(F32) + out_wires.astype(F32)).astype(LOW)
        out_wires = send_halves(out_halves, at)
    grad_part = own_rows(parts)
    unit_one, scale_one = normalize(tokens_here)
    token_grad = grad_hidden + norm_back(grad_part * gain_attn, unit_one, scale_one)
    token_grad = token_grad.astype(LOW)
    token_wire = swap(token_grad[rows:], "h")
    grad_project, small = fence(grad_project, small)
    small = jnp.sum(lax.all_to_all(small, AXES, 0, 0), axis=0)
    input_grad = both(token_grad[:rows], token_wire, near, 0)
    layer_output = both(final_near, final_far, near, 0)
    grad_expand = join_columns(grad_expand, expand_order, 2 * hidden_shard)
    grad_feed_gain = small[:gains]
    grad_attention_gain = small[gains : 2 * gains]
    grad_position_bias = small[2 * gains :]
    grad_out = add_halves(out_halves, out_wires, at) if one_block else grad_out_wide(grad_out)
    grad_down = grad_down.astype(F32)
    grad_project = jnp.where(at["c"] == 0, grad_project, turn(grad_project))
    grad_project = join_columns(grad_project, project_order, span)
    return (
        layer_output,
        input_grad,
        grad_attention_gain,
        grad_project,
        grad_out,
        grad_position_bias,
        grad_feed_gain,
        grad_expand,
        grad_down,
    )


def solution(mesh):
    wide = Mesh(mesh.devices.reshape(-1, 2, 2, 2, 2, 2), AXES)
    lead, tokens, rows = P(AXES), P(None, AXES), P(AXES, None)
    return jax.shard_map(
        local,
        mesh=wide,
        in_specs=(tokens, tokens, tokens, tokens, P(), lead, rows, rows, lead, lead, rows, rows),
        out_specs=(tokens, tokens, lead, rows, rows, lead, lead, rows, rows),
        check_vma=False,
    )
```
